32 devices in a mesh: dp: 8 (over y, x, core), mp: 4 (over z).
Axes of the slice: x: 2, y: 2, z: 4, core: 2. Of those that a mesh axis runs over, the one named last changes fastest.
Arguments:
- replica_grads: bfloat16 [8, 512, 12288], P('dp', None, 'mp'), may hold values from -320 to 320
- owners: int32 [4, 6], P('mp'), may hold values from 0 to 7, as said below
- left_stats: float32 [8, 512, 2048], P('dp', None, 'mp'), may hold values from -1 to 5, as said below
- right_stats: float32 [8, 512, 2048], P('dp', None, 'mp'), may hold values from -1 to 5, as said below
Outputs:
- update: float32 [512, 12288], P(None, 'mp')
The draws below stay inside these ranges and needn't reach their ends.
Inputs may be any that keep to these rules, and one draw needn't show every extreme that they name: `owners`: within one row no replica owns more than 1 block, and some replica owns exactly 1. `left_stats`: each slot's 512 x 512 block is symmetric and diagonally dominant with a positive diagonal; slots that no block names are unused. `right_stats`: each slot's 512 x 512 block is symmetric and diagonally dominant with a positive diagonal; slots that no block names are unused.
All inputs are finite; a program needn't handle non-finite values.
Results may differ from the reference program's by a relative error of at most 0.0003.
Values sent between devices are 32-bit elements; how exact they have to be, the bound alone decides.
No kernel may reach another device: no remote copies, remote signals or barrier semaphores. Data moves between devices by JAX's collectives and lax.ppermute only.
A program may use at most 64 MiB of HBM per device.

```python
import math
import jax
import jax.numpy as jnp
from jax import lax

BLK = 512
NBLK = 6
SLOTS = 1
NEWTON = 2
REPLICAS = 8
SHARDS = 4
OWNER_SLOTS = 8
COLS = 12288
N_MP = 4


def stat_blocks(key, high):
    slot_total = OWNER_SLOTS
    diag_key, off_key = jax.random.split(key)
    diagonal = jnp.exp(jax.random.uniform(diag_key, (slot_total, SHARDS, BLK), jnp.float32, math.log(0.3), math.log(high)))
    uniform_off = jax.random.uniform(off_key, (slot_total, SHARDS, BLK, BLK), jnp.float32, -1.0, 1.0)
    symmetric = 0.5 * (uniform_off + jnp.swapaxes(uniform_off, -1, -2))
    coupling = 0.9 / (BLK * math.sqrt(high / 0.3))
    root_diag = jnp.sqrt(diagonal)
    matrix = coupling * root_diag[..., :, None] * root_diag[..., None, :] * symmetric
    matrix = matrix + jnp.eye(BLK, dtype=jnp.float32) * diagonal[..., :, None]
    return jnp.transpose(matrix, (0, 2, 1, 3)).reshape(slot_total, BLK, SHARDS * BLK)


def draw_left_stats(key, part):
    key = jax.random.fold_in(key, 11)
    return stat_blocks(key, 3.0)


def draw_right_stats(key, part):
    key = jax.random.fold_in(key, 12)
    return stat_blocks(key, 3.0)


def grad_scales(key, row_high):
    row_key, col_key = jax.random.split(key)
    row_scale = jnp.exp(jax.random.uniform(row_key, (BLK,), jnp.float32, 0.0, math.log(row_high)))
    position = jnp.arange(COLS, dtype=jnp.float32) / COLS
    col_scale = jnp.exp(position * math.log(3.0)) * jnp.exp(jax.random.uniform(col_key, (COLS,), jnp.float32, 0.0, math.log(4.0)))
    return 0.5 * row_scale[None, :, None] * col_scale[None, None, :]


def draw_replica_grads(key, part):
    key = jax.random.fold_in(key, 21)
    scale_key, noise_key = jax.random.split(key, 2)
    entries = jnp.clip(jax.random.normal(noise_key, (REPLICAS, BLK, COLS), jnp.float32), -4.0, 4.0)
    entries = entries * grad_scales(scale_key, 10.0)
    return entries.astype(jnp.bfloat16)


def draw_owners(key, part):
    key = jax.random.fold_in(key, 31)

    def one_row(row_key):
        pick_key, place_key = jax.random.split(row_key)
        chosen = jax.random.permutation(pick_key, REPLICAS)
        positions = jnp.maximum(jnp.arange(NBLK) - (SLOTS - 1), 0)
        owner_list = chosen[positions]
        placing = jax.random.permutation(place_key, NBLK)
        return owner_list[placing].astype(jnp.int32)
    return jax.vmap(one_row)(jax.random.split(key, SHARDS))


def setup_inputs(seed: int = 0) -> dict:
    seeds = jax.random.split(jax.random.key(seed), 5)
    replica_grads = draw_replica_grads(jax.random.fold_in(seeds[4], 71), 0)
    owners = draw_owners(jax.random.fold_in(seeds[4], 71), 0)
    left_stats = draw_left_stats(jax.random.fold_in(seeds[4], 71), 0)
    right_stats = draw_right_stats(jax.random.fold_in(seeds[4], 71), 0)
    return {"replica_grads": replica_grads, "owners": owners, "left_stats": left_stats, "right_stats": right_stats}


clip_level = 1.0
graft_eps = 1e-06

def mat_product(left_side, right_side):
    return jnp.matmul(left_side, right_side, precision=lax.Precision.HIGHEST)

def inverse_root(statistic):
    order_size = statistic.shape[-1]
    identity = jnp.eye(order_size, dtype=jnp.float32)
    frobenius = jnp.sqrt(lax.optimization_barrier(jnp.sum(statistic * statistic, axis=(-2, -1), keepdims=True)))
    scaled = statistic / frobenius
    factor = (5.0 * identity - scaled) * 0.25
    root = factor * frobenius ** (-0.25)
    for iteration in range(NEWTON - 1):
        square = mat_product(factor, factor)
        fourth = mat_product(square, square)
        scaled = mat_product(fourth, scaled)
        factor = (5.0 * identity - scaled) * 0.25
        root = mat_product(root, factor)
    return root

def block_update(block, left_prev, right_prev):
    order_size = block.shape[-1]
    transposed = jnp.swapaxes(block, -1, -2)
    left = 0.5 * left_prev + mat_product(block, transposed) / order_size
    right = 0.5 * right_prev + mat_product(transposed, block) / order_size
    pre = mat_product(mat_product(inverse_root(left), block), inverse_root(right))
    block_norm = lax.optimization_barrier(jnp.sum(block * block, axis=(-2, -1), keepdims=True))
    pre_norm = lax.optimization_barrier(jnp.sum(pre * pre, axis=(-2, -1), keepdims=True))
    return pre * jnp.sqrt(block_norm / (pre_norm + graft_eps))

def slot_ranks(owner_row):
    positions = jnp.arange(owner_row.shape[0], dtype=jnp.int32)
    matching = owner_row[:, None] == owner_row[None, :]
    earlier = positions[:, None] > positions[None, :]
    return lax.optimization_barrier(jnp.sum((matching & earlier).astype(jnp.int32), axis=1)).astype(jnp.int32)

def reference(replica_grads, owners, left_stats, right_stats):
    grad_sum = lax.optimization_barrier(jnp.sum(replica_grads.astype(jnp.float32), axis=0))
    mean_square = jnp.sum(grad_sum * grad_sum) / grad_sum.size
    clip_factor = jnp.minimum(1.0, clip_level / jnp.sqrt(mean_square))
    clipped = grad_sum * clip_factor
    pieces = []
    for shard in range(N_MP):
        owner_row = owners[shard]
        ranks = slot_ranks(owner_row)
        for index in range(NBLK):
            column = (shard * NBLK + index) * BLK
            block = clipped[:, column:column + BLK]
            slot = (owner_row[index] * SLOTS + ranks[index]).astype(jnp.int32)
            left_prev = lax.dynamic_index_in_dim(left_stats, slot, 0, keepdims=False)[:, shard * BLK:(shard + 1) * BLK]
            right_prev = lax.dynamic_index_in_dim(right_stats, slot, 0, keepdims=False)[:, shard * BLK:(shard + 1) * BLK]
            pieces.append(block_update(block, left_prev, right_prev))
    return jnp.concatenate(pieces, axis=1)
```

```python
import jax
import jax.numpy as jnp
from jax import lax
from jax.sharding import PartitionSpec as P

clip_level = 1.0
graft_eps = 1e-06


def mat_product(left_side, right_side):
    return jnp.matmul(left_side, right_side, precision=lax.Precision.HIGH)


def inverse_root(statistic):
    order_size = statistic.shape[-1]
    identity = jnp.eye(order_size, dtype=jnp.float32)
    frobenius = jnp.sqrt(jnp.sum(statistic * statistic))
    scaled = statistic / frobenius
    square = mat_product(scaled, scaled)
    factor_square = (25.0 * identity - 10.0 * scaled + square) * 0.0625
    factor_scaled = (5.0 * scaled - square) * 0.25
    fourth = mat_product(factor_square, factor_square)
    tail = mat_product(fourth, factor_scaled)
    return (6.25 * identity - 1.25 * scaled - tail) * (0.25 * frobenius ** (-0.25))


def general_body(replica_grads, owners, left_stats, right_stats):
    width = left_stats.shape[1]
    owner_row = owners[0]
    block_count = owner_row.shape[0]
    replica = lax.axis_index("dp")
    replica_count = lax.axis_size("dp")
    entry_count = width * block_count * width * lax.axis_size("mp")
    share_rows = width // replica_count
    share = lax.psum_scatter(
        replica_grads[0].astype(jnp.float32), "dp", scatter_dimension=0, tiled=True
    )
    squares = lax.psum(jnp.sum(share * share), ("dp", "mp"))
    clip_factor = jnp.minimum(1.0, clip_level / jnp.sqrt(squares / entry_count))
    share_blocks = jnp.transpose(share.reshape(share_rows, block_count, width), (1, 0, 2))
    targets = jnp.arange(replica_count, dtype=jnp.int32)
    routing = (owner_row[None, :] == targets[:, None]).astype(jnp.float32)
    outgoing = jnp.einsum("db,brc->drc", routing, share_blocks, precision=lax.Precision.HIGHEST)
    arrived = lax.all_to_all(outgoing, "dp", split_axis=0, concat_axis=0, tiled=True)
    block = arrived.reshape(width, width) * clip_factor
    update = block_update(block, jnp.sum(block * block), 1.0, left_stats[0], right_stats[0])
    chosen = (owner_row == replica).astype(jnp.float32)
    whole = lax.psum(chosen[:, None, None] * update[None], "dp")
    return jnp.transpose(whole, (1, 0, 2)).reshape(width, block_count * width)


def block_update(block, block_norm, clip_factor, left_prev, right_prev):
    order_size = block.shape[-1]
    stat_scale = clip_factor * clip_factor / order_size
    transposed = block.T
    left = 0.5 * left_prev + mat_product(block, transposed) * stat_scale
    right = 0.5 * right_prev + mat_product(transposed, block) * stat_scale
    pre = mat_product(mat_product(inverse_root(left), block), inverse_root(right)) * clip_factor
    pre_norm = jnp.sum(pre * pre)
    return pre * (clip_factor * jnp.sqrt(block_norm / (pre_norm + graft_eps)))


def paired_body(replica_grads, owners, left_stats, right_stats):
    width = left_stats.shape[1]
    owner_row = owners[0]
    block_count = owner_row.shape[0]
    me = lax.axis_index("dp")
    core = me & 1
    entry_count = width * block_count * width * lax.axis_size("mp")
    grads = replica_grads[0]
    matches = (owner_row[None, :] == jnp.arange(8, dtype=jnp.int32)[:, None]).astype(jnp.int32)
    owned = jnp.sum(matches, axis=1)
    block_of = jnp.sum(matches * jnp.arange(block_count, dtype=jnp.int32)[None, :], axis=1)

    first_pairs = [(i, i ^ (2 if i % 2 == 0 else 4)) for i in range(8)]
    second_pairs = [(i, i ^ (4 if i % 2 == 0 else 2)) for i in range(8)]
    core_pairs = [(i, i ^ 1) for i in range(8)]

    def over(pairs, value):
        return lax.ppermute(value, "dp", pairs)

    def target(slot, device):
        device_core = device & 1
        first = jnp.where(device_core == 0, 2, 4)
        second = 6 - first
        return device ^ ((slot >> 1) * first) ^ ((slot & 1) * second)

    def own_piece(device_target):
        column = block_of[device_target] * width
        return lax.dynamic_slice(grads, (0, column), (width, width)).astype(jnp.float32)

    sums = {}
    for slot in (3, 2, 1, 0):
        arrived = over(core_pairs, own_piece(target(slot, me ^ 1)))
        sums[slot] = arrived + own_piece(target(slot, me))
    sum_one = sums[1] + over(first_pairs, sums[3])
    sum_zero = sums[0] + over(first_pairs, sums[2])
    block = sum_zero + over(second_pairs, sum_one)

    block_norm = jnp.sum(block * block)
    mine = owned[me] > 0
    squares = lax.psum(jnp.where(mine, block_norm, 0.0), ("dp", "mp"))
    clip_factor = jnp.minimum(1.0, clip_level / jnp.sqrt(squares / entry_count))
    update = block_update(block, block_norm, clip_factor, left_stats[0], right_stats[0])

    mine_near = over(second_pairs, update)
    mine_far = over(first_pairs, update)
    near_far = over(first_pairs, mine_near)
    held = [update, mine_near, mine_far, near_far]
    slots = held + [over(core_pairs, value) for value in held]
    places = jnp.stack(
        [target(slot, me) for slot in range(4)] + [target(slot, me ^ 1) for slot in range(4)]
    )
    stacked = jnp.stack(slots)
    pieces = []
    for index in range(block_count):
        place = jnp.argmax(places == owner_row[index])
        pieces.append(lax.dynamic_index_in_dim(stacked, place, 0, keepdims=False))
    return jnp.concatenate(pieces, axis=1)


def solution(mesh):
    return jax.shard_map(
        paired_body if mesh.shape["dp"] == 8 else general_body,
        mesh=mesh,
        in_specs=(P("dp", None, "mp"), P("mp", None), P("dp", None, "mp"), P("dp", None, "mp")),
        out_specs=P(None, "mp"),
        check_vma=False,
    )
```

```python
import jax
import jax.numpy as jnp
from jax import lax
from jax.experimental import pallas as pl
from jax.experimental.pallas import tpu as pltpu
from jax.sharding import PartitionSpec as P

clip_level = 1.0
graft_eps = 1e-06


def mat_product(left_side, right_side):
    return jnp.matmul(left_side, right_side, precision=lax.Precision.HIGH)


def inverse_root(statistic):
    order_size = statistic.shape[-1]
    identity = jnp.eye(order_size, dtype=jnp.float32)
    frobenius = jnp.sqrt(jnp.sum(statistic * statistic))
    scaled = statistic / frobenius
    square = mat_product(scaled, scaled)
    factor_square = (25.0 * identity - 10.0 * scaled + square) * 0.0625
    factor_scaled = (5.0 * scaled - square) * 0.25
    fourth = mat_product(factor_square, factor_square)
    tail = mat_product(fourth, factor_scaled)
    return (6.25 * identity - 1.25 * scaled - tail) * (0.25 * frobenius ** (-0.25))


def general_body(replica_grads, owners, left_stats, right_stats):
    width = left_stats.shape[1]
    owner_row = owners[0]
    block_count = owner_row.shape[0]
    replica = lax.axis_index("dp")
    replica_count = lax.axis_size("dp")
    entry_count = width * block_count * width * lax.axis_size("mp")
    share_rows = width // replica_count
    share = lax.psum_scatter(
        replica_grads[0].astype(jnp.float32), "dp", scatter_dimension=0, tiled=True
    )
    squares = lax.psum(jnp.sum(share * share), ("dp", "mp"))
    clip_factor = jnp.minimum(1.0, clip_level / jnp.sqrt(squares / entry_count))
    share_blocks = jnp.transpose(share.reshape(share_rows, block_count, width), (1, 0, 2))
    targets = jnp.arange(replica_count, dtype=jnp.int32)
    routing = (owner_row[None, :] == targets[:, None]).astype(jnp.float32)
    outgoing = jnp.einsum("db,brc->drc", routing, share_blocks, precision=lax.Precision.HIGHEST)
    arrived = lax.all_to_all(outgoing, "dp", split_axis=0, concat_axis=0, tiled=True)
    block = arrived.reshape(width, width) * clip_factor
    update = block_update(block, jnp.sum(block * block), 1.0, left_stats[0], right_stats[0])
    chosen = (owner_row == replica).astype(jnp.float32)
    whole = lax.psum(chosen[:, None, None] * update[None], "dp")
    return jnp.transpose(whole, (1, 0, 2)).reshape(width, block_count * width)


def block_update(block, block_norm, clip_factor, left_prev, right_prev):
    order_size = block.shape[-1]
    stat_scale = clip_factor * clip_factor / order_size
    transposed = block.T
    left = 0.5 * left_prev + mat_product(block, transposed) * stat_scale
    right = 0.5 * right_prev + mat_product(transposed, block) * stat_scale
    pre = mat_product(mat_product(inverse_root(left), block), inverse_root(right)) * clip_factor
    pre_norm = jnp.sum(pre * pre)
    return pre * (clip_factor * jnp.sqrt(block_norm / (pre_norm + graft_eps)))


MIB = 1 << 20
F32 = jnp.float32


def split(value):
    high = value.astype(jnp.bfloat16)
    return high, (value - high.astype(F32)).astype(jnp.bfloat16)


def narrow_dot(left_side, right_side, dims):
    return lax.dot_general(left_side, right_side, (dims, ((), ())), preferred_element_type=F32)


def split_product(left_side, right_side, dims=((1,), (0,))):
    small = narrow_dot(left_side[0], right_side[1], dims) + narrow_dot(left_side[1], right_side[0], dims)
    return narrow_dot(left_side[0], right_side[0], dims) + small


def pair_target(slot, device):
    first = 2 + 2 * (device & 1)
    return device ^ ((slot >> 1) * first) ^ ((slot & 1) * (6 - first))


def column_of(owners_ref, block_count, target):
    column = 0
    for index in range(1, block_count):
        column = column + jnp.where(owners_ref[index] == target, index, 0)
    return column


def piece_call(grads, owners, me, slot, flip, arrivals, with_norm=False):
    width = grads.shape[0]
    block_count = grads.shape[1] // width
    rows = width // 4

    def kernel(owners_ref, me_ref, grad_ref, *refs):
        total = grad_ref[...].astype(F32)
        for ref in refs[: len(arrivals)]:
            total = total + ref[...]
        refs[len(arrivals)][...] = total
        if with_norm:
            norm_ref = refs[len(arrivals) + 1]
            owned = 0
            for index in range(block_count):
                owned = owned + jnp.where(owners_ref[index] == me_ref[0], 1, 0)
            part = jnp.sum(total * total, keepdims=True).reshape(1, 1) * owned.astype(F32)

            @pl.when(pl.program_id(0) == 0)
            def _():
                norm_ref[...] = jnp.zeros_like(norm_ref)

            norm_ref[...] += jnp.broadcast_to(part, norm_ref.shape)

    def grad_index(step, owners_ref, me_ref):
        return step, column_of(owners_ref, block_count, pair_target(slot, me_ref[0] ^ flip))

    plain = pl.BlockSpec((rows, width), lambda step, owners_ref, me_ref: (step, 0))
    out_specs = [plain]
    out_shape = [jax.ShapeDtypeStruct((width, width), F32)]
    if with_norm:
        out_specs.append(pl.BlockSpec((8, 128), lambda step, owners_ref, me_ref: (0, 0)))
        out_shape.append(jax.ShapeDtypeStruct((8, 128), F32))
    result = pl.pallas_call(
        kernel,
        grid_spec=pltpu.PrefetchScalarGridSpec(
            num_scalar_prefetch=2,
            grid=(width // rows,),
            in_specs=[pl.BlockSpec((rows, width), grad_index)] + [plain] * len(arrivals),
            out_specs=out_specs,
        ),
        out_shape=out_shape,
        cost_estimate=pl.CostEstimate(
            flops=width * width * (len(arrivals) + 1),
            bytes_accessed=width * width * (6 + 4 * len(arrivals)),
            transcendentals=0,
        ),
        name="piece",
    )(owners, me, grads, *arrivals)
    return result if with_norm else result[0]


def gram_kernel(block_ref, left_ref, right_ref):
    block = split(block_ref[...])
    left_ref[...] = split_product(block, block, ((1,), (1,)))
    right_ref[...] = split_product(block, block, ((0,), (0,)))


def gram_call(block):
    width = block.shape[0]
    shape = jax.ShapeDtypeStruct(block.shape, F32)
    return pl.pallas_call(
        gram_kernel,
        in_specs=[pl.BlockSpec(memory_space=pltpu.VMEM)],
        out_specs=[pl.BlockSpec(memory_space=pltpu.VMEM)] * 2,
        out_shape=[shape, shape],
        compiler_params=pltpu.CompilerParams(vmem_limit_bytes=24 * MIB),
        cost_estimate=pl.CostEstimate(
            flops=12 * width**3, bytes_accessed=12 * width * width, transcendentals=0
        ),
        name="gram",
    )(block)


def root_of(previous, gram, gram_scale):
    order_size = previous.shape[0]
    rows = lax.broadcasted_iota(jnp.int32, previous.shape, 0)
    columns = lax.broadcasted_iota(jnp.int32, previous.shape, 1)
    identity = jnp.where(rows == columns, 1.0, 0.0)
    statistic = 0.5 * previous + gram * gram_scale
    squares = jnp.sum(statistic * statistic, keepdims=True).reshape(1, 1)
    frobenius = jnp.sqrt(squares)
    scaled = statistic * (1.0 / frobenius)
    parts = split(scaled)
    square = split_product(parts, parts)
    factor_square = split((25.0 * identity - 10.0 * scaled + square) * 0.0625)
    factor_scaled = split((5.0 * scaled - square) * 0.25)
    fourth = split(split_product(factor_square, factor_square))
    tail = split_product(fourth, factor_scaled)
    return (6.25 * identity - 1.25 * scaled - tail) * (0.25 * lax.rsqrt(jnp.sqrt(frobenius)))


def update_call(block, left_gram, right_gram, left_prev, right_prev, norms, entry_count):
    width = block.shape[0]

    def kernel(block_ref, left_gram_ref, right_gram_ref, left_ref, right_ref, *refs):
        out_ref = refs[-1]
        squares = refs[0][...]
        for ref in refs[1:-1]:
            squares = squares + ref[...]
        clip_factor = jnp.minimum(1.0, clip_level / jnp.sqrt(squares[:1, :1] / entry_count))
        gram_scale = clip_factor * clip_factor / width
        left_root = root_of(left_ref[...], left_gram_ref[...], gram_scale)
        right_root = root_of(right_ref[...], right_gram_ref[...], gram_scale)
        block = block_ref[...]
        halfway = split_product(split(left_root), split(block))
        pre = split_product(split(halfway), split(right_root)) * clip_factor
        block_norm = jnp.sum(block * block, keepdims=True).reshape(1, 1) * (clip_factor * clip_factor)
        pre_norm = jnp.sum(pre * pre, keepdims=True).reshape(1, 1)
        out_ref[...] = pre * jnp.sqrt(block_norm / (pre_norm + graft_eps))

    return pl.pallas_call(
        kernel,
        in_specs=[pl.BlockSpec(memory_space=pltpu.VMEM)] * (5 + len(norms)),
        out_specs=pl.BlockSpec(memory_space=pltpu.VMEM),
        out_shape=jax.ShapeDtypeStruct(block.shape, F32),
        compiler_params=pltpu.CompilerParams(vmem_limit_bytes=40 * MIB),
        cost_estimate=pl.CostEstimate(
            flops=48 * width**3, bytes_accessed=24 * width * width, transcendentals=0
        ),
        name="update",
    )(block, left_gram, right_gram, left_prev, right_prev, *norms)


def assemble_call(owners, me, slots, block_count):
    width = slots[0].shape[0]

    def kernel(owners_ref, me_ref, *refs):
        out_ref, sem = refs[-2:]
        for index in range(block_count):
            spot = out_ref.at[:, pl.ds(index * width, width)]
            for place in range(len(slots)):
                target = pair_target(place & 3, me_ref[0] ^ (place >> 2))

                @pl.when(owners_ref[index] == target)
                def _():
                    pltpu.make_async_copy(refs[place], spot, sem.at[index]).start()

        for index in range(block_count):
            spot = out_ref.at[:, pl.ds(index * width, width)]
            pltpu.make_async_copy(refs[0], spot, sem.at[index]).wait()

    return pl.pallas_call(
        kernel,
        in_specs=[pl.BlockSpec(memory_space=pltpu.SMEM)] * 2
        + [pl.BlockSpec(memory_space=pl.ANY)] * len(slots),
        out_specs=pl.BlockSpec(memory_space=pl.ANY),
        out_shape=jax.ShapeDtypeStruct((width, block_count * width), F32),
        scratch_shapes=[pltpu.SemaphoreType.DMA((block_count,))],
        cost_estimate=pl.CostEstimate(
            flops=0, bytes_accessed=8 * width * width * block_count, transcendentals=0
        ),
        name="assemble",
    )(owners, me, *slots)


def paired_body(replica_grads, owners, left_stats, right_stats):
    width = left_stats.shape[1]
    owner_row = owners[0]
    block_count = owner_row.shape[0]
    me = lax.axis_index("dp").astype(jnp.int32).reshape(1)
    group_count = lax.axis_size("mp")
    entry_count = width * block_count * width * group_count
    grads = replica_grads[0]

    first_pairs = [(i, i ^ (2 + 2 * (i % 2))) for i in range(8)]
    second_pairs = [(i, i ^ (4 - 2 * (i % 2))) for i in range(8)]
    core_pairs = [(i, i ^ 1) for i in range(8)]

    def over(pairs, value):
        return lax.ppermute(value, "dp", pairs)

    def piece(slot, flip, *arrivals):
        return piece_call(grads, owner_row, me, slot, flip, arrivals)

    from_core = {slot: over(core_pairs, piece(slot, 1)) for slot in (3, 2, 1, 0)}
    from_first_three = over(first_pairs, piece(3, 0, from_core[3]))
    from_first_two = over(first_pairs, piece(2, 0, from_core[2]))
    from_second = over(second_pairs, piece(1, 0, from_core[1], from_first_three))
    arrivals = (from_core[0], from_first_two, from_second)
    block, norm = piece_call(grads, owner_row, me, 0, 0, arrivals, with_norm=True)

    group_norm = norm
    for flip in range(1, 8):
        group_norm = group_norm + over([(i, i ^ flip) for i in range(8)], norm)
    norms = [group_norm]
    for shift in range(1, group_count):
        pairs = [(i, (i + shift) % group_count) for i in range(group_count)]
        norms.append(lax.ppermute(group_norm, "mp", pairs))
    left_gram, right_gram = gram_call(block)
    update = update_call(
        block, left_gram, right_gram, left_stats[0], right_stats[0], norms, entry_count
    )

    mine_near = over(second_pairs, update)
    mine_far = over(first_pairs, update)
    near_far = over(first_pairs, mine_near)
    held = [update, mine_near, mine_far, near_far]
    slots = held + [over(core_pairs, value) for value in held]
    return assemble_call(owner_row, me, slots, block_count)


def solution(mesh):
    return jax.shard_map(
        paired_body if mesh.shape["dp"] == 8 else general_body,
        mesh=mesh,
        in_specs=(P("dp", None, "mp"), P("mp", None), P("dp", None, "mp"), P("dp", None, "mp")),
        out_specs=P(None, "mp"),
        check_vma=False,
    )
```

```python
import jax
import jax.numpy as jnp
from jax import lax
from jax.experimental import pallas as pl
from jax.experimental.pallas import tpu as pltpu
from jax.sharding import PartitionSpec as P

clip_level = 1.0
graft_eps = 1e-06


def mat_product(left_side, right_side):
    return jnp.matmul(left_side, right_side, precision=lax.Precision.HIGH)


def inverse_root(statistic):
    order_size = statistic.shape[-1]
    identity = jnp.eye(order_size, dtype=jnp.float32)
    frobenius = jnp.sqrt(jnp.sum(statistic * statistic))
    scaled = statistic / frobenius
    square = mat_product(scaled, scaled)
    factor_square = (25.0 * identity - 10.0 * scaled + square) * 0.0625
    factor_scaled = (5.0 * scaled - square) * 0.25
    fourth = mat_product(factor_square, factor_square)
    tail = mat_product(fourth, factor_scaled)
    return (6.25 * identity - 1.25 * scaled - tail) * (0.25 * frobenius ** (-0.25))


def general_body(replica_grads, owners, left_stats, right_stats):
    width = left_stats.shape[1]
    owner_row = owners[0]
    block_count = owner_row.shape[0]
    replica = lax.axis_index("dp")
    replica_count = lax.axis_size("dp")
    entry_count = width * block_count * width * lax.axis_size("mp")
    share_rows = width // replica_count
    share = lax.psum_scatter(
        replica_grads[0].astype(jnp.float32), "dp", scatter_dimension=0, tiled=True
    )
    squares = lax.psum(jnp.sum(share * share), ("dp", "mp"))
    clip_factor = jnp.minimum(1.0, clip_level / jnp.sqrt(squares / entry_count))
    share_blocks = jnp.transpose(share.reshape(share_rows, block_count, width), (1, 0, 2))
    targets = jnp.arange(replica_count, dtype=jnp.int32)
    routing = (owner_row[None, :] == targets[:, None]).astype(jnp.float32)
    outgoing = jnp.einsum("db,brc->drc", routing, share_blocks, precision=lax.Precision.HIGHEST)
    arrived = lax.all_to_all(outgoing, "dp", split_axis=0, concat_axis=0, tiled=True)
    block = arrived.reshape(width, width) * clip_factor
    update = block_update(block, jnp.sum(block * block), 1.0, left_stats[0], right_stats[0])
    chosen = (owner_row == replica).astype(jnp.float32)
    whole = lax.psum(chosen[:, None, None] * update[None], "dp")
    return jnp.transpose(whole, (1, 0, 2)).reshape(width, block_count * width)


def block_update(block, block_norm, clip_factor, left_prev, right_prev):
    order_size = block.shape[-1]
    stat_scale = clip_factor * clip_factor / order_size
    transposed = block.T
    left = 0.5 * left_prev + mat_product(block, transposed) * stat_scale
    right = 0.5 * right_prev + mat_product(transposed, block) * stat_scale
    pre = mat_product(mat_product(inverse_root(left), block), inverse_root(right)) * clip_factor
    pre_norm = jnp.sum(pre * pre)
    return pre * (clip_factor * jnp.sqrt(block_norm / (pre_norm + graft_eps)))


MIB = 1 << 20
F32 = jnp.float32
HALVES = (0, 1)


def split(value):
    high = value.astype(jnp.bfloat16)
    return high, (value - high.astype(F32)).astype(jnp.bfloat16)


def narrow_dot(left_side, right_side, dims):
    return lax.dot_general(left_side, right_side, (dims, ((), ())), preferred_element_type=F32)


def split_product(left_side, right_side, dims=((1,), (0,))):
    small = narrow_dot(left_side[0], right_side[1], dims) + narrow_dot(left_side[1], right_side[0], dims)
    return narrow_dot(left_side[0], right_side[0], dims) + small


def pair_target(slot, device):
    first = 2 + 2 * (device & 1)
    return device ^ ((slot >> 1) * first) ^ ((slot & 1) * (6 - first))


def local_call(kernel, name, out_shape, operands, scalars=(), flops=0, vmem=None, **options):
    whole = pl.BlockSpec(memory_space=pltpu.VMEM)
    arrays = list(operands) + (list(out_shape) if isinstance(out_shape, (list, tuple)) else [out_shape])
    moved = sum(array.size * array.dtype.itemsize for array in arrays)
    return pl.pallas_call(
        kernel,
        in_specs=[pl.BlockSpec(memory_space=pltpu.SMEM)] * len(scalars) + [whole] * len(operands),
        out_specs=jax.tree.map(lambda _: whole, out_shape),
        out_shape=out_shape,
        compiler_params=pltpu.CompilerParams(vmem_limit_bytes=vmem),
        cost_estimate=pl.CostEstimate(flops=flops, bytes_accessed=moved, transcendentals=0),
        name=name,
        **options,
    )(*scalars, *operands)


def owner_block(owners_ref, grad_ref, rows, width, target):
    column = 0
    for index in range(1, grad_ref.shape[1] // width):
        column = column + jnp.where(owners_ref[index] == target, index * width, 0)
    columns = pl.ds(pl.multiple_of(column, width), width)
    return grad_ref[rows, columns].astype(F32)


def half_rows(half, width):
    return pl.ds(half * (width // 2), width // 2)


def half_shape(width):
    return jax.ShapeDtypeStruct((width // 2, width), F32)


def pack_call(owners, me, grads, slots, width):
    def kernel(owners_ref, me_ref, grad_ref, *out_refs):
        place = 0
        for slot in slots:
            target = pair_target(slot, me_ref[0] ^ 1)
            for half in HALVES:
                out_refs[place][...] = owner_block(owners_ref, grad_ref, half_rows(half, width), width, target)
                place += 1

    shapes = [half_shape(width)] * (2 * len(slots))
    return local_call(kernel, "pack", shapes, (grads,), (owners, me), vmem=8 * MIB)


def add_call(owners, me, grads, slot, half, arrivals, width):
    def kernel(owners_ref, me_ref, grad_ref, *refs):
        target = pair_target(slot, me_ref[0])
        total = owner_block(owners_ref, grad_ref, half_rows(half, width), width, target)
        for ref in refs[:-1]:
            total = total + ref[...]
        refs[-1][...] = total

    return local_call(kernel, "add", half_shape(width), (grads, *arrivals), (owners, me), vmem=8 * MIB)


def join_call(owners, me, grads, arrivals, width, device_count):
    block_count = grads.shape[1] // width

    def kernel(owners_ref, me_ref, grad_ref, *refs):
        block_ref, norm_ref = refs[-2:]
        squares = jnp.zeros((1, 1), F32)
        for half in HALVES:
            rows = half_rows(half, width)
            total = owner_block(owners_ref, grad_ref, rows, width, me_ref[0])
            for ref in refs[half:-2:2]:
                total = total + ref[...]
            block_ref[rows, :] = total
            squares = squares + jnp.sum(total * total, keepdims=True).reshape(1, 1)
        owned = 0
        for index in range(block_count):
            owned = owned + jnp.where(owners_ref[index] == me_ref[0], 1, 0)
        norm_ref[...] = jnp.broadcast_to(squares * owned.astype(F32), norm_ref.shape)

    shapes = [jax.ShapeDtypeStruct((width, width), F32), jax.ShapeDtypeStruct((device_count, 128), F32)]
    return local_call(kernel, "join", shapes, (grads, *arrivals), (owners, me), vmem=8 * MIB)


def gram_kernel(block_ref, left_ref, right_ref):
    block = split(block_ref[...])
    left_ref[...] = split_product(block, block, ((1,), (1,)))
    right_ref[...] = split_product(block, block, ((0,), (0,)))


def gram_call(block):
    shape = jax.ShapeDtypeStruct(block.shape, F32)
    flops = 12 * block.shape[0] ** 3
    return local_call(gram_kernel, "gram", [shape, shape], (block,), flops=flops, vmem=16 * MIB)


def root_of(previous, gram, gram_scale):
    rows = lax.broadcasted_iota(jnp.int32, previous.shape, 0)
    columns = lax.broadcasted_iota(jnp.int32, previous.shape, 1)
    identity = jnp.where(rows == columns, 1.0, 0.0)
    statistic = 0.5 * previous + gram * gram_scale
    squares = jnp.sum(statistic * statistic, keepdims=True).reshape(1, 1)
    frobenius = jnp.sqrt(squares)
    scaled = statistic * (1.0 / frobenius)
    parts = split(scaled)
    square = split_product(parts, parts)
    factor_square = split((25.0 * identity - 10.0 * scaled + square) * 0.0625)
    factor_scaled = split((5.0 * scaled - square) * 0.25)
    fourth = split(split_product(factor_square, factor_square))
    tail = split_product(fourth, factor_scaled)
    return (6.25 * identity - 1.25 * scaled - tail) * (0.25 * lax.rsqrt(jnp.sqrt(frobenius)))


def update_call(block, left_gram, right_gram, left_prev, right_prev, norms, entry_count):
    width = block.shape[0]

    def kernel(block_ref, left_gram_ref, right_gram_ref, left_ref, right_ref, norm_ref, *out_refs):
        squares = jnp.sum(norm_ref[:, :1], axis=0, keepdims=True)
        clip_factor = jnp.minimum(1.0, clip_level / jnp.sqrt(squares / entry_count))
        gram_scale = clip_factor * clip_factor / width
        left_root = root_of(left_ref[...], left_gram_ref[...], gram_scale)
        right_root = root_of(right_ref[...], right_gram_ref[...], gram_scale)
        block = block_ref[...]
        halfway = split_product(split(left_root), split(block))
        pre = split_product(split(halfway), split(right_root)) * clip_factor
        block_norm = jnp.sum(block * block, keepdims=True).reshape(1, 1) * (clip_factor * clip_factor)
        pre_norm = jnp.sum(pre * pre, keepdims=True).reshape(1, 1)
        update = pre * jnp.sqrt(block_norm / (pre_norm + graft_eps))
        for half in HALVES:
            out_refs[half][...] = update[half * (width // 2) : (half + 1) * (width // 2)]

    operands = (block, left_gram, right_gram, left_prev, right_prev, norms)
    shapes = [half_shape(width)] * 2
    return local_call(kernel, "update", shapes, operands, flops=48 * width**3, vmem=24 * MIB)


def assemble_call(owners, me, slots, block_count):
    width = slots[0].shape[1]

    def kernel(owners_ref, me_ref, *refs):
        out_ref, sem = refs[-2:]

        def spot(index, half):
            return out_ref.at[half_rows(half, width), pl.ds(index * width, width)]

        for index in range(block_count):
            for place in range(8):
                target = pair_target(place & 3, me_ref[0] ^ (place >> 2))

                @pl.when(owners_ref[index] == target)
                def _():
                    for half in HALVES:
                        source = refs[2 * place + half]
                        pltpu.make_async_copy(source, spot(index, half), sem.at[index, half]).start()

        for index in range(block_count):
            for half in HALVES:
                pltpu.make_async_copy(refs[half], spot(index, half), sem.at[index, half]).wait()

    return pl.pallas_call(
        kernel,
        in_specs=[pl.BlockSpec(memory_space=pltpu.SMEM)] * 2
        + [pl.BlockSpec(memory_space=pltpu.VMEM)] * len(slots),
        out_specs=pl.BlockSpec(memory_space=pl.ANY),
        out_shape=jax.ShapeDtypeStruct((width, block_count * width), F32),
        scratch_shapes=[pltpu.SemaphoreType.DMA((block_count, 2))],
        cost_estimate=pl.CostEstimate(
            flops=0, bytes_accessed=8 * width * width * block_count, transcendentals=0
        ),
        name="assemble",
    )(owners, me, *slots)


def paired_body(replica_grads, owners, left_stats, right_stats):
    width = left_stats.shape[1]
    owner_row = owners[0]
    block_count = owner_row.shape[0]
    me = lax.axis_index("dp").astype(jnp.int32).reshape(1)
    device_count = 8 * lax.axis_size("mp")
    entry_count = width * block_count * width * lax.axis_size("mp")
    grads = replica_grads[0]

    first_pairs = [(i, i ^ (2 + 2 * (i % 2))) for i in range(8)]
    second_pairs = [(i, i ^ (4 - 2 * (i % 2))) for i in range(8)]
    core_pairs = [(i, i ^ 1) for i in range(8)]

    def over(pairs, value):
        return lax.ppermute(value, "dp", pairs)

    def own_plus(slot, half, *arrivals):
        return add_call(owner_row, me, grads, slot, half, arrivals, width)

    packed = {}
    for slots in ((3, 2), (1, 0)):
        pieces = pack_call(owner_row, me, grads, slots, width)
        packed.update(zip([(slot, half) for slot in slots for half in HALVES], pieces))
    from_core = {key: over(core_pairs, value) for key, value in packed.items()}
    from_first = {}
    for slot in (3, 2):
        for half in HALVES:
            from_first[slot, half] = over(first_pairs, own_plus(slot, half, from_core[slot, half]))
    from_second = [
        over(second_pairs, own_plus(1, half, from_core[1, half], from_first[3, half])) for half in HALVES
    ]
    arrivals = [from_core[0, half] for half in HALVES] + [from_first[2, half] for half in HALVES]
    block, norm = join_call(owner_row, me, grads, arrivals + from_second, width, device_count)
    norms = lax.all_to_all(norm, ("dp", "mp"), split_axis=0, concat_axis=0, tiled=True)
    left_gram, right_gram = gram_call(block)
    update = update_call(block, left_gram, right_gram, left_stats[0], right_stats[0], norms, entry_count)

    near = [over(second_pairs, value) for value in update]
    far = [over(first_pairs, value) for value in update]
    relayed = [over(first_pairs, value) for value in near]
    held = list(update) + near + far + relayed
    slots = held + [over(core_pairs, value) for value in held]
    return assemble_call(owner_row, me, slots, block_count)


def solution(mesh):
    return jax.shard_map(
        paired_body if mesh.shape["dp"] == 8 else general_body,
        mesh=mesh,
        in_specs=(P("dp", None, "mp"), P("mp", None), P("dp", None, "mp"), P("dp", None, "mp")),
        out_specs=P(None, "mp"),
        check_vma=False,
    )
```

```python
import functools

import jax
import jax.numpy as jnp
from jax import lax
from jax.experimental import pallas as pl
from jax.experimental.pallas import tpu as pltpu
from jax.sharding import PartitionSpec as P

clip_level = 1.0
graft_eps = 1e-06


def mat_product(left_side, right_side):
    return jnp.matmul(left_side, right_side, precision=lax.Precision.HIGH)


def inverse_root(statistic):
    order_size = statistic.shape[-1]
    identity = jnp.eye(order_size, dtype=jnp.float32)
    frobenius = jnp.sqrt(jnp.sum(statistic * statistic))
    scaled = statistic / frobenius
    square = mat_product(scaled, scaled)
    factor_square = (25.0 * identity - 10.0 * scaled + square) * 0.0625
    factor_scaled = (5.0 * scaled - square) * 0.25
    fourth = mat_product(factor_square, factor_square)
    tail = mat_product(fourth, factor_scaled)
    return (6.25 * identity - 1.25 * scaled - tail) * (0.25 * frobenius ** (-0.25))


def general_body(replica_grads, owners, left_stats, right_stats):
    width = left_stats.shape[1]
    owner_row = owners[0]
    block_count = owner_row.shape[0]
    replica = lax.axis_index("dp")
    replica_count = lax.axis_size("dp")
    entry_count = width * block_count * width * lax.axis_size("mp")
    share_rows = width // replica_count
    share = lax.psum_scatter(
        replica_grads[0].astype(jnp.float32), "dp", scatter_dimension=0, tiled=True
    )
    squares = lax.psum(jnp.sum(share * share), ("dp", "mp"))
    clip_factor = jnp.minimum(1.0, clip_level / jnp.sqrt(squares / entry_count))
    share_blocks = jnp.transpose(share.reshape(share_rows, block_count, width), (1, 0, 2))
    targets = jnp.arange(replica_count, dtype=jnp.int32)
    routing = (owner_row[None, :] == targets[:, None]).astype(jnp.float32)
    outgoing = jnp.einsum("db,brc->drc", routing, share_blocks, precision=lax.Precision.HIGHEST)
    arrived = lax.all_to_all(outgoing, "dp", split_axis=0, concat_axis=0, tiled=True)
    block = arrived.reshape(width, width) * clip_factor
    update = block_update(block, jnp.sum(block * block), 1.0, left_stats[0], right_stats[0])
    chosen = (owner_row == replica).astype(jnp.float32)
    whole = lax.psum(chosen[:, None, None] * update[None], "dp")
    return jnp.transpose(whole, (1, 0, 2)).reshape(width, block_count * width)


def block_update(block, block_norm, clip_factor, left_prev, right_prev):
    order_size = block.shape[-1]
    stat_scale = clip_factor * clip_factor / order_size
    transposed = block.T
    left = 0.5 * left_prev + mat_product(block, transposed) * stat_scale
    right = 0.5 * right_prev + mat_product(transposed, block) * stat_scale
    pre = mat_product(mat_product(inverse_root(left), block), inverse_root(right)) * clip_factor
    pre_norm = jnp.sum(pre * pre)
    return pre * (clip_factor * jnp.sqrt(block_norm / (pre_norm + graft_eps)))


SMALL = 2 << 20
LARGE = 14 << 20
F32 = jnp.float32
HALVES = (0, 1)


def split(value):
    high = value.astype(jnp.bfloat16)
    return high, (value - high.astype(F32)).astype(jnp.bfloat16)


def narrow_dot(left_side, right_side, dims):
    return lax.dot_general(left_side, right_side, (dims, ((), ())), preferred_element_type=F32)


def split_product(left_side, right_side, dims=((1,), (0,))):
    small = narrow_dot(left_side[0], right_side[1], dims) + narrow_dot(left_side[1], right_side[0], dims)
    return narrow_dot(left_side[0], right_side[0], dims) + small


def pair_target(slot, device):
    first = 2 + 2 * (device & 1)
    return device ^ ((slot >> 1) * first) ^ ((slot & 1) * (6 - first))


def local_call(kernel, name, out_shape, operands, scalars=(), flops=0, vmem=None, **options):
    whole = pl.BlockSpec(memory_space=pltpu.VMEM)
    arrays = list(operands) + (list(out_shape) if isinstance(out_shape, (list, tuple)) else [out_shape])
    moved = sum(array.size * array.dtype.itemsize for array in arrays)
    return pl.pallas_call(
        kernel,
        in_specs=[pl.BlockSpec(memory_space=pltpu.SMEM)] * len(scalars) + [whole] * len(operands),
        out_specs=jax.tree.map(lambda _: whole, out_shape),
        out_shape=out_shape,
        compiler_params=pltpu.CompilerParams(vmem_limit_bytes=vmem or SMALL),
        cost_estimate=pl.CostEstimate(flops=flops, bytes_accessed=moved, transcendentals=0),
        name=name,
        **options,
    )(*scalars, *operands)


def owner_block(owners_ref, grad_ref, rows, width, target):
    column = 0
    for index in range(1, grad_ref.shape[1] // width):
        column = column + jnp.where(owners_ref[index] == target, index * width, 0)
    columns = pl.ds(pl.multiple_of(column, width), width)
    return grad_ref[rows, columns].astype(F32)


def half_rows(half, width):
    return pl.ds(half * (width // 2), width // 2)


def half_shape(width):
    return jax.ShapeDtypeStruct((width // 2, width), F32)


def pack_kernel(slots, width, owners_ref, me_ref, grad_ref, *out_refs):
    place = 0
    for slot in slots:
        target = pair_target(slot, me_ref[0] ^ 1)
        for half in HALVES:
            out_refs[place][...] = owner_block(owners_ref, grad_ref, half_rows(half, width), width, target)
            place += 1


def pack_call(owners, me, grads, slots, width):
    shapes = [half_shape(width)] * (2 * len(slots))
    kernel = functools.partial(pack_kernel, slots, width)
    return local_call(kernel, "pack", shapes, (grads,), (owners, me))


def add_call(owners, me, grads, slot, half, arrivals, width):
    def kernel(owners_ref, me_ref, grad_ref, *refs):
        target = pair_target(slot, me_ref[0])
        total = owner_block(owners_ref, grad_ref, half_rows(half, width), width, target)
        for ref in refs[:-1]:
            total = total + ref[...]
        refs[-1][...] = total

    return local_call(kernel, "add", half_shape(width), (grads, *arrivals), (owners, me))


def join_call(owners, me, total, arrival, norm, block_count, device_count):
    def kernel(owners_ref, me_ref, total_ref, arrival_ref, *refs):
        block_ref, norm_ref = refs[-2:]
        block = total_ref[...] + arrival_ref[...]
        block_ref[...] = block
        owned = 0
        for index in range(block_count):
            owned = owned + jnp.where(owners_ref[index] == me_ref[0], 1, 0)
        squares = jnp.sum(block * block, keepdims=True).reshape(1, 1) * owned.astype(F32)
        if norm is not None:
            squares = squares + refs[0][:1, :1]
        norm_ref[...] = jnp.broadcast_to(squares, norm_ref.shape)

    shapes = [half_shape(total.shape[1]), jax.ShapeDtypeStruct((device_count, 128), F32)]
    operands = (total, arrival) if norm is None else (total, arrival, norm)
    return local_call(kernel, "join", shapes, operands, (owners, me))


def whole_block(block_refs):
    return jnp.concatenate([ref[...] for ref in block_refs], axis=0)


def gram_kernel(upper_ref, lower_ref, left_ref, right_ref):
    block = split(whole_block((upper_ref, lower_ref)))
    left_ref[...] = split_product(block, block, ((1,), (1,)))
    right_ref[...] = split_product(block, block, ((0,), (0,)))


def gram_call(block):
    width = block[0].shape[1]
    shape = jax.ShapeDtypeStruct((width, width), F32)
    return local_call(gram_kernel, "gram", [shape, shape], block, flops=12 * width**3, vmem=LARGE)


def root_of(previous, gram, gram_scale):
    rows = lax.broadcasted_iota(jnp.int32, previous.shape, 0)
    columns = lax.broadcasted_iota(jnp.int32, previous.shape, 1)
    identity = jnp.where(rows == columns, 1.0, 0.0)
    statistic = 0.5 * previous + gram * gram_scale
    squares = jnp.sum(statistic * statistic, keepdims=True).reshape(1, 1)
    frobenius = jnp.sqrt(squares)
    scaled = statistic * (1.0 / frobenius)
    parts = split(scaled)
    square = split_product(parts, parts)
    factor_square = split((25.0 * identity - 10.0 * scaled + square) * 0.0625)
    factor_scaled = split((5.0 * scaled - square) * 0.25)
    fourth = split(split_product(factor_square, factor_square))
    tail = split_product(fourth, factor_scaled)
    return (6.25 * identity - 1.25 * scaled - tail) * (0.25 * lax.rsqrt(jnp.sqrt(frobenius)))


def update_call(block, left_gram, right_gram, left_prev, right_prev, norms, entry_count):
    width = block[0].shape[1]

    def kernel(upper_ref, lower_ref, left_gram_ref, right_gram_ref, left_ref, right_ref, norm_ref, *out_refs):
        squares = jnp.sum(norm_ref[:, :1], axis=0, keepdims=True)
        clip_factor = jnp.minimum(1.0, clip_level / jnp.sqrt(squares / entry_count))
        gram_scale = clip_factor * clip_factor / width
        left_root = root_of(left_ref[...], left_gram_ref[...], gram_scale)
        right_root = root_of(right_ref[...], right_gram_ref[...], gram_scale)
        block = whole_block((upper_ref, lower_ref))
        halfway = split_product(split(left_root), split(block))
        pre = split_product(split(halfway), split(right_root)) * clip_factor
        block_norm = jnp.sum(block * block, keepdims=True).reshape(1, 1) * (clip_factor * clip_factor)
        pre_norm = jnp.sum(pre * pre, keepdims=True).reshape(1, 1)
        update = pre * jnp.sqrt(block_norm / (pre_norm + graft_eps))
        for half in HALVES:
            out_refs[half][...] = update[half * (width // 2) : (half + 1) * (width // 2)]

    operands = (*block, left_gram, right_gram, left_prev, right_prev, norms)
    shapes = [half_shape(width)] * 2
    return local_call(kernel, "update", shapes, operands, flops=48 * width**3, vmem=LARGE)


def assemble_call(owners, me, places, slots, block_count, started):
    width = slots[0].shape[1]

    def kernel(owners_ref, me_ref, *refs):
        out_ref, sem = refs[-2:]
        copies = []
        for number, (place, half) in enumerate(places):
            target = pair_target(place & 3, me_ref[0] ^ (place >> 2))
            owned, column = 0, 0
            for index in range(block_count):
                matches = owners_ref[index] == target
                owned = owned + jnp.where(matches, 1, 0)
                column = column + jnp.where(matches, index * width, 0)
            columns = pl.ds(pl.multiple_of(column, width), width)
            spot = out_ref.at[half_rows(half, width), columns]
            copies.append((owned, pltpu.make_async_copy(refs[number], spot, sem.at[number])))
        for owned, copy in copies:
            pl.when(owned == 1)(copy.start)
        for owned, copy in copies:
            pl.when(owned == 1)(copy.wait)

    in_specs = [pl.BlockSpec(memory_space=pltpu.SMEM)] * 2
    in_specs += [pl.BlockSpec(memory_space=pltpu.VMEM)] * len(slots)
    operands = [owners, me, *slots]
    aliases = {}
    if started is not None:
        aliases = {len(operands): 0}
        in_specs.append(pl.BlockSpec(memory_space=pltpu.HBM))
        operands.append(started)
    return pl.pallas_call(
        kernel,
        in_specs=in_specs,
        out_specs=pl.BlockSpec(memory_space=pltpu.HBM),
        out_shape=jax.ShapeDtypeStruct((width, block_count * width), F32),
        scratch_shapes=[pltpu.SemaphoreType.DMA((len(slots),))],
        input_output_aliases=aliases,
        compiler_params=pltpu.CompilerParams(vmem_limit_bytes=SMALL),
        cost_estimate=pl.CostEstimate(
            flops=0, bytes_accessed=8 * slots[0].size * len(slots), transcendentals=0
        ),
        name="assemble",
    )(*operands)


def paired_body(replica_grads, owners, left_stats, right_stats):
    width = left_stats.shape[1]
    owner_row = owners[0]
    block_count = owner_row.shape[0]
    me = lax.axis_index("dp").astype(jnp.int32).reshape(1)
    device_count = 8 * lax.axis_size("mp")
    entry_count = width * block_count * width * lax.axis_size("mp")

    first_pairs = [(i, i ^ (2 + 2 * (i % 2))) for i in range(8)]
    second_pairs = [(i, i ^ (4 - 2 * (i % 2))) for i in range(8)]
    core_pairs = [(i, i ^ 1) for i in range(8)]

    def over(pairs, value):
        return lax.ppermute(value, "dp", pairs)

    def own_plus(slot, half, *arrivals):
        return add_call(owner_row, me, grads, slot, half, arrivals, width)

    grads = replica_grads[0]
    pieces = pack_call(owner_row, me, grads, (3, 2), width)
    pieces += pack_call(owner_row, me, grads, (1, 0), width)
    keys = [(slot, half) for slot in (3, 2, 1, 0) for half in HALVES]
    from_core = {key: over(core_pairs, value) for key, value in zip(keys, pieces)}
    from_first = {}
    for slot in (3, 2):
        for half in HALVES:
            from_first[slot, half] = over(first_pairs, own_plus(slot, half, from_core[slot, half]))
    from_second = [
        over(second_pairs, own_plus(1, half, from_core[1, half], from_first[3, half])) for half in HALVES
    ]
    norm, block = None, []
    for half in HALVES:
        total = own_plus(0, half, from_core[0, half], from_first[2, half])
        joined, norm = join_call(owner_row, me, total, from_second[half], norm, block_count, device_count)
        block.append(joined)
    norms = lax.all_to_all(norm, ("dp", "mp"), split_axis=0, concat_axis=0, tiled=True)
    left_gram, right_gram = gram_call(block)
    update = update_call(block, left_gram, right_gram, left_stats[0], right_stats[0], norms, entry_count)

    near = [over(second_pairs, value) for value in update]
    far = [over(first_pairs, value) for value in update]
    relayed = [over(first_pairs, value) for value in near]
    held = dict(zip([(place, half) for place in range(4) for half in HALVES], [*update, *near, *far, *relayed]))
    held.update({(place + 4, half): over(core_pairs, value) for (place, half), value in held.items()})
    result = None
    for places in (
        [key for key in held if key[0] & 3 != 3],
        [(3, 0), (7, 0)],
        [(3, 1), (7, 1)],
    ):
        result = assemble_call(owner_row, me, places, [held[key] for key in places], block_count, result)
    return result


def solution(mesh):
    return jax.shard_map(
        paired_body if mesh.shape["dp"] == 8 else general_body,
        mesh=mesh,
        in_specs=(P("dp", None, "mp"), P("mp", None), P("dp", None, "mp"), P("dp", None, "mp")),
        out_specs=P(None, "mp"),
        check_vma=False,
    )
```

```python
import functools

import jax
import jax.numpy as jnp
from jax import lax
from jax.experimental import pallas as pl
from jax.experimental.pallas import tpu as pltpu
from jax.sharding import PartitionSpec as P

clip_level = 1.0
graft_eps = 1e-06


def mat_product(left_side, right_side):
    return jnp.matmul(left_side, right_side, precision=lax.Precision.HIGH)


def inverse_root(statistic):
    order_size = statistic.shape[-1]
    identity = jnp.eye(order_size, dtype=jnp.float32)
    frobenius = jnp.sqrt(jnp.sum(statistic * statistic))
    scaled = statistic / frobenius
    square = mat_product(scaled, scaled)
    factor_square = (25.0 * identity - 10.0 * scaled + square) * 0.0625
    factor_scaled = (5.0 * scaled - square) * 0.25
    fourth = mat_product(factor_square, factor_square)
    tail = mat_product(fourth, factor_scaled)
    return (6.25 * identity - 1.25 * scaled - tail) * (0.25 * frobenius ** (-0.25))


def general_body(replica_grads, owners, left_stats, right_stats):
    width = left_stats.shape[1]
    owner_row = owners[0]
    block_count = owner_row.shape[0]
    replica = lax.axis_index("dp")
    replica_count = lax.axis_size("dp")
    entry_count = width * block_count * width * lax.axis_size("mp")
    share_rows = width // replica_count
    share = lax.psum_scatter(
        replica_grads[0].astype(jnp.float32), "dp", scatter_dimension=0, tiled=True
    )
    squares = lax.psum(jnp.sum(share * share), ("dp", "mp"))
    clip_factor = jnp.minimum(1.0, clip_level / jnp.sqrt(squares / entry_count))
    share_blocks = jnp.transpose(share.reshape(share_rows, block_count, width), (1, 0, 2))
    targets = jnp.arange(replica_count, dtype=jnp.int32)
    routing = (owner_row[None, :] == targets[:, None]).astype(jnp.float32)
    outgoing = jnp.einsum("db,brc->drc", routing, share_blocks, precision=lax.Precision.HIGHEST)
    arrived = lax.all_to_all(outgoing, "dp", split_axis=0, concat_axis=0, tiled=True)
    block = arrived.reshape(width, width) * clip_factor
    update = block_update(block, jnp.sum(block * block), 1.0, left_stats[0], right_stats[0])
    chosen = (owner_row == replica).astype(jnp.float32)
    whole = lax.psum(chosen[:, None, None] * update[None], "dp")
    return jnp.transpose(whole, (1, 0, 2)).reshape(width, block_count * width)


def block_update(block, block_norm, clip_factor, left_prev, right_prev):
    order_size = block.shape[-1]
    stat_scale = clip_factor * clip_factor / order_size
    transposed = block.T
    left = 0.5 * left_prev + mat_product(block, transposed) * stat_scale
    right = 0.5 * right_prev + mat_product(transposed, block) * stat_scale
    pre = mat_product(mat_product(inverse_root(left), block), inverse_root(right)) * clip_factor
    pre_norm = jnp.sum(pre * pre)
    return pre * (clip_factor * jnp.sqrt(block_norm / (pre_norm + graft_eps)))


SMALL = 2 << 20
LARGE = 14 << 20
F32 = jnp.float32
HALVES = (0, 1)


def split(value):
    high = value.astype(jnp.bfloat16)
    return high, (value - high.astype(F32)).astype(jnp.bfloat16)


def narrow_dot(left_side, right_side, dims):
    return lax.dot_general(left_side, right_side, (dims, ((), ())), preferred_element_type=F32)


def split_product(left_side, right_side, dims=((1,), (0,))):
    small = narrow_dot(left_side[0], right_side[1], dims) + narrow_dot(left_side[1], right_side[0], dims)
    return narrow_dot(left_side[0], right_side[0], dims) + small


def pair_target(slot, device):
    first = 2 + 2 * (device & 1)
    return device ^ ((slot >> 1) * first) ^ ((slot & 1) * (6 - first))


def local_call(kernel, name, out_shape, operands, scalars=(), flops=0, vmem=None, **options):
    whole = pl.BlockSpec(memory_space=pltpu.VMEM)
    arrays = list(operands) + (list(out_shape) if isinstance(out_shape, (list, tuple)) else [out_shape])
    moved = sum(array.size * array.dtype.itemsize for array in arrays)
    return pl.pallas_call(
        kernel,
        in_specs=[pl.BlockSpec(memory_space=pltpu.SMEM)] * len(scalars) + [whole] * len(operands),
        out_specs=jax.tree.map(lambda _: whole, out_shape),
        out_shape=out_shape,
        compiler_params=pltpu.CompilerParams(vmem_limit_bytes=vmem or SMALL),
        cost_estimate=pl.CostEstimate(flops=flops, bytes_accessed=moved, transcendentals=0),
        name=name,
        **options,
    )(*scalars, *operands)


def owner_block(owners_ref, grad_ref, rows, width, target):
    column = 0
    for index in range(1, grad_ref.shape[1] // width):
        column = column + jnp.where(owners_ref[index] == target, index * width, 0)
    columns = pl.ds(pl.multiple_of(column, width), width)
    return grad_ref[rows, columns].astype(F32)


def rows_of(half, width):
    return pl.ds(0, width) if half is None else pl.ds(half * (width // 2), width // 2)


def piece_shape(half, width):
    return jax.ShapeDtypeStruct((width if half is None else width // 2, width), F32)


def piece_of(ref, half, width):
    return ref[rows_of(half, width), :] if ref.shape[0] == width else ref[...]


def pack_call(owners, me, grads, pieces, width):
    def kernel(owners_ref, me_ref, grad_ref, *out_refs):
        for (slot, half), out_ref in zip(pieces, out_refs):
            target = pair_target(slot, me_ref[0] ^ 1)
            out_ref[...] = owner_block(owners_ref, grad_ref, rows_of(half, width), width, target)

    shapes = [piece_shape(half, width) for _, half in pieces]
    return local_call(kernel, "pack", shapes, (grads,), (owners, me))


def add_call(owners, me, grads, slot, half, arrivals, width):
    def kernel(owners_ref, me_ref, grad_ref, *refs):
        target = pair_target(slot, me_ref[0])
        total = owner_block(owners_ref, grad_ref, rows_of(half, width), width, target)
        for ref in refs[:-1]:
            total = total + piece_of(ref, half, width)
        refs[-1][...] = total

    return local_call(kernel, "add", piece_shape(half, width), (grads, *arrivals), (owners, me))


def join_call(owners, me, total, half, arrival, norm, block_count):
    width = total.shape[1]

    def kernel(owners_ref, me_ref, total_ref, arrival_ref, *refs):
        block_ref, norm_ref = refs[-2:]
        block = piece_of(total_ref, half, width) + arrival_ref[...]
        block_ref[...] = block
        owned = 0
        for index in range(block_count):
            owned = owned + jnp.where(owners_ref[index] == me_ref[0], 1, 0)
        squares = jnp.sum(block * block, keepdims=True).reshape(1, 1) * owned.astype(F32)
        if norm is not None:
            squares = squares + refs[0][:1, :1]
        rows = lax.broadcasted_iota(jnp.int32, norm_ref.shape, 0)
        norm_ref[...] = jnp.where(rows == 0, squares, 0.0)

    shapes = [piece_shape(half, width), jax.ShapeDtypeStruct((8, 128), F32)]
    operands = (total, arrival) if norm is None else (total, arrival, norm)
    return local_call(kernel, "join", shapes, operands, (owners, me))


def whole_block(block_refs):
    return jnp.concatenate([ref[...] for ref in block_refs], axis=0)


def gram_kernel(upper_ref, lower_ref, left_ref, right_ref):
    block = split(whole_block((upper_ref, lower_ref)))
    left_ref[...] = split_product(block, block, ((1,), (1,)))
    right_ref[...] = split_product(block, block, ((0,), (0,)))


def gram_call(block):
    width = block[0].shape[1]
    shape = jax.ShapeDtypeStruct((width, width), F32)
    return local_call(gram_kernel, "gram", [shape, shape], block, flops=12 * width**3, vmem=LARGE)


def root_of(previous, gram, gram_scale):
    rows = lax.broadcasted_iota(jnp.int32, previous.shape, 0)
    columns = lax.broadcasted_iota(jnp.int32, previous.shape, 1)
    identity = jnp.where(rows == columns, 1.0, 0.0)
    statistic = 0.5 * previous + gram * gram_scale
    squares = jnp.sum(statistic * statistic, keepdims=True).reshape(1, 1)
    frobenius = jnp.sqrt(squares)
    scaled = statistic * (1.0 / frobenius)
    parts = split(scaled)
    square = split_product(parts, parts)
    factor_square = split((25.0 * identity - 10.0 * scaled + square) * 0.0625)
    factor_scaled = split((5.0 * scaled - square) * 0.25)
    fourth = split(split_product(factor_square, factor_square))
    tail = split_product(fourth, factor_scaled)
    return (6.25 * identity - 1.25 * scaled - tail) * (0.25 * lax.rsqrt(jnp.sqrt(frobenius)))


def update_call(block, left_gram, right_gram, left_prev, right_prev, norms, entry_count):
    width = block[0].shape[1]

    def kernel(upper_ref, lower_ref, left_gram_ref, right_gram_ref, left_ref, right_ref, norm_ref, *out_refs):
        squares = jnp.sum(norm_ref[:, :1], axis=0, keepdims=True)
        clip_factor = jnp.minimum(1.0, clip_level / jnp.sqrt(squares / entry_count))
        gram_scale = clip_factor * clip_factor / width
        left_root = root_of(left_ref[...], left_gram_ref[...], gram_scale)
        right_root = root_of(right_ref[...], right_gram_ref[...], gram_scale)
        block = whole_block((upper_ref, lower_ref))
        halfway = split_product(split(left_root), split(block))
        pre = split_product(split(halfway), split(right_root)) * clip_factor
        block_norm = jnp.sum(block * block, keepdims=True).reshape(1, 1) * (clip_factor * clip_factor)
        pre_norm = jnp.sum(pre * pre, keepdims=True).reshape(1, 1)
        update = pre * jnp.sqrt(block_norm / (pre_norm + graft_eps))
        out_refs[0][...] = update
        for half in HALVES:
            out_refs[1 + half][...] = update[half * (width // 2) : (half + 1) * (width // 2)]

    operands = (*block, left_gram, right_gram, left_prev, right_prev, norms)
    shapes = [piece_shape(half, width) for half in (None, *HALVES)]
    return local_call(kernel, "update", shapes, operands, flops=48 * width**3, vmem=LARGE)


def assemble_call(owners, me, places, slots, block_count, started):
    width = slots[0].shape[1]

    def kernel(owners_ref, me_ref, *refs):
        out_ref, sem = refs[-2:]
        copies = []
        for number, (place, half) in enumerate(places):
            target = pair_target(place & 3, me_ref[0] ^ (place >> 2))
            owned, column = 0, 0
            for index in range(block_count):
                matches = owners_ref[index] == target
                owned = owned + jnp.where(matches, 1, 0)
                column = column + jnp.where(matches, index * width, 0)
            columns = pl.ds(pl.multiple_of(column, width), width)
            spot = out_ref.at[rows_of(half, width), columns]
            copies.append((owned, pltpu.make_async_copy(refs[number], spot, sem.at[number])))
        for owned, copy in copies:
            pl.when(owned == 1)(copy.start)
        for owned, copy in copies:
            pl.when(owned == 1)(copy.wait)

    in_specs = [pl.BlockSpec(memory_space=pltpu.SMEM)] * 2
    in_specs += [pl.BlockSpec(memory_space=pltpu.VMEM)] * len(slots)
    operands = [owners, me, *slots]
    aliases = {}
    if started is not None:
        aliases = {len(operands): 0}
        in_specs.append(pl.BlockSpec(memory_space=pltpu.HBM))
        operands.append(started)
    return pl.pallas_call(
        kernel,
        in_specs=in_specs,
        out_specs=pl.BlockSpec(memory_space=pltpu.HBM),
        out_shape=jax.ShapeDtypeStruct((width, block_count * width), F32),
        scratch_shapes=[pltpu.SemaphoreType.DMA((len(slots),))],
        input_output_aliases=aliases,
        compiler_params=pltpu.CompilerParams(vmem_limit_bytes=SMALL),
        cost_estimate=pl.CostEstimate(
            flops=0, bytes_accessed=8 * slots[0].size * len(slots), transcendentals=0
        ),
        name="assemble",
    )(*operands)


def paired_body(replica_grads, owners, left_stats, right_stats):
    width = left_stats.shape[1]
    owner_row = owners[0]
    block_count = owner_row.shape[0]
    me = lax.axis_index("dp").astype(jnp.int32).reshape(1)
    entry_count = width * block_count * width * lax.axis_size("mp")

    first_pairs = [(i, i ^ (2 + 2 * (i % 2))) for i in range(8)]
    second_pairs = [(i, i ^ (4 - 2 * (i % 2))) for i in range(8)]
    core_pairs = [(i, i ^ 1) for i in range(8)]

    def over(pairs, value, label="move"):
        with jax.named_scope(label):
            return lax.ppermute(value, "dp", pairs)

    def own_plus(slot, half, *arrivals):
        return add_call(owner_row, me, grads, slot, half, arrivals, width)

    def after(value, *others):
        return lax.optimization_barrier((value, *others))[0]

    grads = replica_grads[0]
    early = pack_call(owner_row, me, grads, [(3, 0), (3, 1)], width)
    core_three = [over(core_pairs, early[h], "core3%d"%h) for h in HALVES]
    sums_three = [own_plus(3, h, core_three[h]) for h in HALVES]
    first_three = [over(first_pairs, sums_three[h], "first3%d"%h) for h in HALVES]
    late = pack_call(owner_row, after(me, *sums_three), grads, [(2, None)], width)
    core_two = over(core_pairs, late[0], "core2")
    late += pack_call(owner_row, after(me, core_two), grads, [(1, None), (0, None)], width)
    core_one = over(core_pairs, late[1], "core1")
    first_two = over(first_pairs, own_plus(2, None, core_two), "first2")
    core_zero = over(core_pairs, after(late[2], first_three[1]), "core0")
    second = [over(second_pairs, own_plus(1, h, core_one, first_three[h]), "second%d"%h) for h in HALVES]
    total = own_plus(0, None, core_zero, first_two)
    norm, block = None, []
    for half in HALVES:
        joined, norm = join_call(owner_row, me, total, half, second[half], norm, block_count)
        block.append(joined)
    norms = lax.all_gather(norm, ("dp", "mp"), axis=0, tiled=True)
    left_gram, right_gram = gram_call(block)
    whole, *own = update_call(block, left_gram, right_gram, left_stats[0], right_stats[0], norms, entry_count)

    near = [over(second_pairs, own[h], "near%d"%h) for h in HALVES]
    far = over(first_pairs, after(whole, near[1]), "far")
    relayed = [over(first_pairs, near[h], "relay%d"%h) for h in HALVES]
    w = after(whole, near[0])
    n = [after(near[h], far) for h in HALVES]
    core_own = over(core_pairs, w, "core_own")
    core_near = [over(core_pairs, n[h], "core_near%d"%h) for h in HALVES]
    core_far = over(core_pairs, far, "core_far")
    core_relay = [over(core_pairs, relayed[h], "core_relay%d"%h) for h in HALVES]
    groups = [{(0,None):w, (4,None):core_own, (1,0):n[0],(1,1):n[1],(5,0):core_near[0],(5,1):core_near[1],(2,None):far,(6,None):core_far}, {(3,0):relayed[0],(7,0):core_relay[0],(3,1):relayed[1],(7,1):core_relay[1]}]

    result = None
    for group in groups:
        keys, here = zip(*group.items())
        result = assemble_call(owner_row, me, keys, here, block_count, result)
    return result


def solution(mesh):
    return jax.shard_map(
        paired_body if mesh.shape["dp"] == 8 else general_body,
        mesh=mesh,
        in_specs=(P("dp", None, "mp"), P("mp", None), P("dp", None, "mp"), P("dp", None, "mp")),
        out_specs=P(None, "mp"),
        check_vma=False,
    )
```

```python
import functools

import jax
import jax.numpy as jnp
from jax import lax
from jax.experimental import pallas as pl
from jax.experimental.pallas import tpu as pltpu
from jax.sharding import PartitionSpec as P

clip_level = 1.0
graft_eps = 1e-06


def mat_product(left_side, right_side):
    return jnp.matmul(left_side, right_side, precision=lax.Precision.HIGH)


def inverse_root(statistic):
    order_size = statistic.shape[-1]
    identity = jnp.eye(order_size, dtype=jnp.float32)
    frobenius = jnp.sqrt(jnp.sum(statistic * statistic))
    scaled = statistic / frobenius
    square = mat_product(scaled, scaled)
    factor_square = (25.0 * identity - 10.0 * scaled + square) * 0.0625
    factor_scaled = (5.0 * scaled - square) * 0.25
    fourth = mat_product(factor_square, factor_square)
    tail = mat_product(fourth, factor_scaled)
    return (6.25 * identity - 1.25 * scaled - tail) * (0.25 * frobenius ** (-0.25))


def general_body(replica_grads, owners, left_stats, right_stats):
    width = left_stats.shape[1]
    owner_row = owners[0]
    block_count = owner_row.shape[0]
    replica = lax.axis_index("dp")
    replica_count = lax.axis_size("dp")
    entry_count = width * block_count * width * lax.axis_size("mp")
    share_rows = width // replica_count
    share = lax.psum_scatter(
        replica_grads[0].astype(jnp.float32), "dp", scatter_dimension=0, tiled=True
    )
    squares = lax.psum(jnp.sum(share * share), ("dp", "mp"))
    clip_factor = jnp.minimum(1.0, clip_level / jnp.sqrt(squares / entry_count))
    share_blocks = jnp.transpose(share.reshape(share_rows, block_count, width), (1, 0, 2))
    targets = jnp.arange(replica_count, dtype=jnp.int32)
    routing = (owner_row[None, :] == targets[:, None]).astype(jnp.float32)
    outgoing = jnp.einsum("db,brc->drc", routing, share_blocks, precision=lax.Precision.HIGHEST)
    arrived = lax.all_to_all(outgoing, "dp", split_axis=0, concat_axis=0, tiled=True)
    block = arrived.reshape(width, width) * clip_factor
    update = block_update(block, jnp.sum(block * block), 1.0, left_stats[0], right_stats[0])
    chosen = (owner_row == replica).astype(jnp.float32)
    whole = lax.psum(chosen[:, None, None] * update[None], "dp")
    return jnp.transpose(whole, (1, 0, 2)).reshape(width, block_count * width)


def block_update(block, block_norm, clip_factor, left_prev, right_prev):
    order_size = block.shape[-1]
    stat_scale = clip_factor * clip_factor / order_size
    transposed = block.T
    left = 0.5 * left_prev + mat_product(block, transposed) * stat_scale
    right = 0.5 * right_prev + mat_product(transposed, block) * stat_scale
    pre = mat_product(mat_product(inverse_root(left), block), inverse_root(right)) * clip_factor
    pre_norm = jnp.sum(pre * pre)
    return pre * (clip_factor * jnp.sqrt(block_norm / (pre_norm + graft_eps)))


SMALL = 2 << 20
LARGE = 14 << 20
F32 = jnp.float32
HALVES = (0, 1)


def split(value):
    high = value.astype(jnp.bfloat16)
    return high, (value - high.astype(F32)).astype(jnp.bfloat16)


def narrow_dot(left_side, right_side, dims):
    return lax.dot_general(left_side, right_side, (dims, ((), ())), preferred_element_type=F32)


def split_product(left_side, right_side, dims=((1,), (0,))):
    small = narrow_dot(left_side[0], right_side[1], dims) + narrow_dot(left_side[1], right_side[0], dims)
    return narrow_dot(left_side[0], right_side[0], dims) + small


def piece_target(kind, device):
    along = 2 + 2 * (device & 1)
    return {"self": device, "straight": device ^ along, "cross": device ^ along ^ 1, "diagonal": device ^ 7}[kind]


def local_call(kernel, name, out_shape, operands, scalars=(), flops=0, vmem=None, **options):
    whole = pl.BlockSpec(memory_space=pltpu.VMEM)
    arrays = list(operands) + (list(out_shape) if isinstance(out_shape, (list, tuple)) else [out_shape])
    moved = sum(array.size * array.dtype.itemsize for array in arrays)
    return pl.pallas_call(
        kernel,
        in_specs=[pl.BlockSpec(memory_space=pltpu.SMEM)] * len(scalars) + [whole] * len(operands),
        out_specs=jax.tree.map(lambda _: whole, out_shape),
        out_shape=out_shape,
        compiler_params=pltpu.CompilerParams(vmem_limit_bytes=vmem or SMALL),
        cost_estimate=pl.CostEstimate(flops=flops, bytes_accessed=moved, transcendentals=0),
        name=name,
        **options,
    )(*scalars, *operands)


def owner_block(owners_ref, grad_ref, rows, width, target):
    column = 0
    for index in range(1, grad_ref.shape[1] // width):
        column = column + jnp.where(owners_ref[index] == target, index * width, 0)
    columns = pl.ds(pl.multiple_of(column, width), width)
    return grad_ref[rows, columns].astype(F32)


def rows_of(half, width):
    return pl.ds(0, width) if half is None else pl.ds(half * (width // 2), width // 2)


def piece_shape(half, width):
    return jax.ShapeDtypeStruct((width if half is None else width // 2, width), F32)


def piece_of(ref, half, width):
    return ref[rows_of(half, width), :] if ref.shape[0] == width else ref[...]


def pack_call(owners, me, grads, pieces, width):
    def kernel(owners_ref, me_ref, grad_ref, *out_refs):
        for (kind, half), out_ref in zip(pieces, out_refs):
            target = piece_target(kind, me_ref[0] ^ 1)
            out_ref[...] = owner_block(owners_ref, grad_ref, rows_of(half, width), width, target)

    shapes = [piece_shape(half, width) for _, half in pieces]
    return local_call(kernel, "pack", shapes, (grads,), (owners, me))


def add_call(owners, me, grads, kind, half, arrivals, width):
    def kernel(owners_ref, me_ref, grad_ref, *refs):
        target = piece_target(kind, me_ref[0])
        total = owner_block(owners_ref, grad_ref, rows_of(half, width), width, target)
        for ref in refs[:-1]:
            total = total + piece_of(ref, half, width)
        refs[-1][...] = total

    return local_call(kernel, "add", piece_shape(half, width), (grads, *arrivals), (owners, me))


def join_call(owners, me, total, half, arrival, norm, block_count):
    width = total.shape[1]

    def kernel(owners_ref, me_ref, total_ref, arrival_ref, *refs):
        block_ref, norm_ref = refs[-2:]
        block = piece_of(total_ref, half, width) + arrival_ref[...]
        block_ref[...] = block
        owned = 0
        for index in range(block_count):
            owned = owned + jnp.where(owners_ref[index] == me_ref[0], 1, 0)
        squares = jnp.sum(block * block, keepdims=True).reshape(1, 1) * owned.astype(F32)
        total_squares = jnp.broadcast_to(squares, norm_ref.shape)
        norm_ref[...] = total_squares if norm is None else total_squares + refs[0][...]

    shapes = [piece_shape(half, width), jax.ShapeDtypeStruct((8, 128), F32)]
    operands = (total, arrival) if norm is None else (total, arrival, norm)
    return local_call(kernel, "join", shapes, operands, (owners, me))


def sum_kernel(*refs):
    total = refs[0][...]
    for ref in refs[1:-1]:
        total = total + ref[...]
    refs[-1][...] = total


def sum_call(*tiles):
    return local_call(sum_kernel, "sum", jax.ShapeDtypeStruct(tiles[0].shape, F32), tiles)


def whole_block(block_refs):
    return jnp.concatenate([ref[...] for ref in block_refs], axis=0)


def gram_kernel(upper_ref, lower_ref, left_ref, right_ref):
    block = split(whole_block((upper_ref, lower_ref)))
    left_ref[...] = split_product(block, block, ((1,), (1,)))
    right_ref[...] = split_product(block, block, ((0,), (0,)))


def gram_call(block):
    width = block[0].shape[1]
    shape = jax.ShapeDtypeStruct((width, width), F32)
    return local_call(gram_kernel, "gram", [shape, shape], block, flops=12 * width**3, vmem=LARGE)


def root_of(previous, gram, gram_scale):
    rows = lax.broadcasted_iota(jnp.int32, previous.shape, 0)
    columns = lax.broadcasted_iota(jnp.int32, previous.shape, 1)
    identity = jnp.where(rows == columns, 1.0, 0.0)
    statistic = 0.5 * previous + gram * gram_scale
    squares = jnp.sum(statistic * statistic, keepdims=True).reshape(1, 1)
    frobenius = jnp.sqrt(squares)
    scaled = statistic * (1.0 / frobenius)
    parts = split(scaled)
    square = split_product(parts, parts)
    factor_square = split((25.0 * identity - 10.0 * scaled + square) * 0.0625)
    factor_scaled = split((5.0 * scaled - square) * 0.25)
    fourth = split(split_product(factor_square, factor_square))
    tail = split_product(fourth, factor_scaled)
    return (6.25 * identity - 1.25 * scaled - tail) * (0.25 * lax.rsqrt(jnp.sqrt(frobenius)))


def update_call(block, left_gram, right_gram, left_prev, right_prev, norms, entry_count):
    width = block[0].shape[1]

    def kernel(upper_ref, lower_ref, left_gram_ref, right_gram_ref, left_ref, right_ref, *refs):
        norm_refs, out_refs = refs[:-3], refs[-3:]
        squares = sum(ref[:1, :1] for ref in norm_refs)
        clip_factor = jnp.minimum(1.0, clip_level / jnp.sqrt(squares / entry_count))
        gram_scale = clip_factor * clip_factor / width
        left_root = root_of(left_ref[...], left_gram_ref[...], gram_scale)
        right_root = root_of(right_ref[...], right_gram_ref[...], gram_scale)
        block = whole_block((upper_ref, lower_ref))
        halfway = split_product(split(left_root), split(block))
        pre = split_product(split(halfway), split(right_root)) * clip_factor
        block_norm = jnp.sum(block * block, keepdims=True).reshape(1, 1) * (clip_factor * clip_factor)
        pre_norm = jnp.sum(pre * pre, keepdims=True).reshape(1, 1)
        update = pre * jnp.sqrt(block_norm / (pre_norm + graft_eps))
        out_refs[0][...] = update
        for half in HALVES:
            out_refs[1 + half][...] = update[half * (width // 2) : (half + 1) * (width // 2)]

    operands = (*block, left_gram, right_gram, left_prev, right_prev, *norms)
    shapes = [piece_shape(half, width) for half in (None, *HALVES)]
    return local_call(kernel, "update", shapes, operands, flops=48 * width**3, vmem=LARGE)


def assemble_call(owners, me, places, slots, block_count, started):
    width = slots[0].shape[1]

    def kernel(owners_ref, me_ref, *refs):
        out_ref, sem = refs[-2:]
        copies = []
        for number, (kind, flip, half) in enumerate(places):
            target = piece_target(kind, me_ref[0] ^ flip)
            owned, column = 0, 0
            for index in range(block_count):
                matches = owners_ref[index] == target
                owned = owned + jnp.where(matches, 1, 0)
                column = column + jnp.where(matches, index * width, 0)
            columns = pl.ds(pl.multiple_of(column, width), width)
            spot = out_ref.at[rows_of(half, width), columns]
            copies.append((owned, pltpu.make_async_copy(refs[number], spot, sem.at[number])))
        for owned, copy in copies:
            pl.when(owned == 1)(copy.start)
        for owned, copy in copies:
            pl.when(owned == 1)(copy.wait)

    in_specs = [pl.BlockSpec(memory_space=pltpu.SMEM)] * 2
    in_specs += [pl.BlockSpec(memory_space=pltpu.VMEM)] * len(slots)
    operands = [owners, me, *slots]
    aliases = {}
    if started is not None:
        aliases = {len(operands): 0}
        in_specs.append(pl.BlockSpec(memory_space=pltpu.HBM))
        operands.append(started)
    return pl.pallas_call(
        kernel,
        in_specs=in_specs,
        out_specs=pl.BlockSpec(memory_space=pltpu.HBM),
        out_shape=jax.ShapeDtypeStruct((width, block_count * width), F32),
        scratch_shapes=[pltpu.SemaphoreType.DMA((len(slots),))],
        input_output_aliases=aliases,
        compiler_params=pltpu.CompilerParams(vmem_limit_bytes=SMALL),
        cost_estimate=pl.CostEstimate(
            flops=0, bytes_accessed=8 * slots[0].size * len(slots), transcendentals=0
        ),
        name="assemble",
    )(*operands)


def paired_body(replica_grads, owners, left_stats, right_stats):
    width = left_stats.shape[1]
    owner_row = owners[0]
    block_count = owner_row.shape[0]
    me = lax.axis_index("dp").astype(jnp.int32).reshape(1)
    group_count = lax.axis_size("mp")
    entry_count = width * block_count * width * group_count
    grads = replica_grads[0]

    def flipped(mask):
        return [(i, i ^ mask) for i in range(8)]

    def over(pairs, value, label):
        with jax.named_scope(label):
            return lax.ppermute(value, "dp", pairs)

    def to_core(value, label):
        return over(flipped(1), value, "core_" + label)

    def to_link(value, label):
        return over([(i, i ^ (2 + 2 * (i % 2))) for i in range(8)], value, "link_" + label)

    def own_plus(kind, half, *arrivals):
        return add_call(owner_row, me, grads, kind, half, arrivals, width)

    def after(value, *others):
        return lax.optimization_barrier((value, *others))[0]

    early = pack_call(owner_row, me, grads, [("diagonal", half) for half in HALVES], width)
    core_diagonal = [to_core(value, "diagonal") for value in early]
    sums = [own_plus("diagonal", half, core_diagonal[half]) for half in HALVES]
    diagonal = [to_link(value, "diagonal") for value in sums]
    later = pack_call(owner_row, after(me, *sums), grads, [("cross", None)], width)
    core_cross = to_core(later[0], "cross")
    cross = to_link(own_plus("cross", None, after(core_cross, diagonal[0])), "cross")
    later = pack_call(owner_row, after(me, core_cross), grads, [("straight", None), ("self", None)], width)
    core_straight = to_core(later[0], "straight")
    core_self = to_core(later[1], "self")
    handed = [to_core(value, "handed") for value in diagonal]
    straight = [
        to_link(own_plus("straight", half, core_straight, handed[half]), "straight") for half in HALVES
    ]
    total = own_plus("self", None, core_self, to_core(cross, "handed_cross"))
    norm, block = None, []
    for half in HALVES:
        joined, norm = join_call(owner_row, me, total, half, straight[half], norm, block_count)
        block.append(joined)
    norm = sum_call(norm, to_core(norm, "norm"))
    norm = sum_call(norm, *[over(flipped(mask), norm, "chip_norm") for mask in (2, 4, 6)])
    norms = [norm]
    for shift in range(1, group_count):
        pairs = [(i, (i + shift) % group_count) for i in range(group_count)]
        with jax.named_scope("group_norm"):
            norms.append(lax.ppermute(norm, "mp", pairs))
    left_gram, right_gram = gram_call(block)
    whole, *own = update_call(block, left_gram, right_gram, left_stats[0], right_stats[0], norms, entry_count)

    core_own = to_core(whole, "own")
    first = [to_link(value, "own") for value in own]
    core_first = [to_core(after(value, core_own), "first") for value in first]
    second = to_link(after(core_own, first[0]), "sibling")
    core_second = to_core(second, "second")
    relayed = [to_link(value, "relayed") for value in core_first]
    core_relayed = [to_core(value, "relayed") for value in relayed]
    groups = [
        [(("self", 0, None), whole), (("self", 1, None), core_own)]
        + [(("straight", 0, half), first[half]) for half in HALVES]
        + [(("straight", 1, half), core_first[half]) for half in HALVES]
        + [(("cross", 0, None), second), (("cross", 1, None), core_second)],
        [(("diagonal", 0, half), relayed[half]) for half in HALVES]
        + [(("diagonal", 1, half), core_relayed[half]) for half in HALVES],
    ]
    result = None
    for group in groups:
        result = assemble_call(owner_row, me, *zip(*group), block_count, result)
    return result


def solution(mesh):
    return jax.shard_map(
        paired_body if mesh.shape["dp"] == 8 else general_body,
        mesh=mesh,
        in_specs=(P("dp", None, "mp"), P("mp", None), P("dp", None, "mp"), P("dp", None, "mp")),
        out_specs=P(None, "mp"),
        check_vma=False,
    )
```

```python
import functools

import jax
import jax.numpy as jnp
from jax import lax
from jax.experimental import pallas as pl
from jax.experimental.pallas import tpu as pltpu
from jax.sharding import PartitionSpec as P

clip_level = 1.0
graft_eps = 1e-06


def mat_product(left_side, right_side):
    return jnp.matmul(left_side, right_side, precision=lax.Precision.HIGH)


def inverse_root(statistic):
    order_size = statistic.shape[-1]
    identity = jnp.eye(order_size, dtype=jnp.float32)
    frobenius = jnp.sqrt(jnp.sum(statistic * statistic))
    scaled = statistic / frobenius
    square = mat_product(scaled, scaled)
    factor_square = (25.0 * identity - 10.0 * scaled + square) * 0.0625
    factor_scaled = (5.0 * scaled - square) * 0.25
    fourth = mat_product(factor_square, factor_square)
    tail = mat_product(fourth, factor_scaled)
    return (6.25 * identity - 1.25 * scaled - tail) * (0.25 * frobenius ** (-0.25))


def general_body(replica_grads, owners, left_stats, right_stats):
    width = left_stats.shape[1]
    owner_row = owners[0]
    block_count = owner_row.shape[0]
    replica = lax.axis_index("dp")
    replica_count = lax.axis_size("dp")
    entry_count = width * block_count * width * lax.axis_size("mp")
    share_rows = width // replica_count
    share = lax.psum_scatter(
        replica_grads[0].astype(jnp.float32), "dp", scatter_dimension=0, tiled=True
    )
    squares = lax.psum(jnp.sum(share * share), ("dp", "mp"))
    clip_factor = jnp.minimum(1.0, clip_level / jnp.sqrt(squares / entry_count))
    share_blocks = jnp.transpose(share.reshape(share_rows, block_count, width), (1, 0, 2))
    targets = jnp.arange(replica_count, dtype=jnp.int32)
    routing = (owner_row[None, :] == targets[:, None]).astype(jnp.float32)
    outgoing = jnp.einsum("db,brc->drc", routing, share_blocks, precision=lax.Precision.HIGHEST)
    arrived = lax.all_to_all(outgoing, "dp", split_axis=0, concat_axis=0, tiled=True)
    block = arrived.reshape(width, width) * clip_factor
    update = block_update(block, jnp.sum(block * block), 1.0, left_stats[0], right_stats[0])
    chosen = (owner_row == replica).astype(jnp.float32)
    whole = lax.psum(chosen[:, None, None] * update[None], "dp")
    return jnp.transpose(whole, (1, 0, 2)).reshape(width, block_count * width)


def block_update(block, block_norm, clip_factor, left_prev, right_prev):
    order_size = block.shape[-1]
    stat_scale = clip_factor * clip_factor / order_size
    transposed = block.T
    left = 0.5 * left_prev + mat_product(block, transposed) * stat_scale
    right = 0.5 * right_prev + mat_product(transposed, block) * stat_scale
    pre = mat_product(mat_product(inverse_root(left), block), inverse_root(right)) * clip_factor
    pre_norm = jnp.sum(pre * pre)
    return pre * (clip_factor * jnp.sqrt(block_norm / (pre_norm + graft_eps)))


SMALL = 2 << 20
LARGE = 14 << 20
F32 = jnp.float32
HALVES = (0, 1)


def split(value):
    high = value.astype(jnp.bfloat16)
    return high, (value - high.astype(F32)).astype(jnp.bfloat16)


def narrow_dot(left_side, right_side, dims):
    return lax.dot_general(left_side, right_side, (dims, ((), ())), preferred_element_type=F32)


def split_product(left_side, right_side, dims=((1,), (0,))):
    small = narrow_dot(left_side[0], right_side[1], dims) + narrow_dot(left_side[1], right_side[0], dims)
    return narrow_dot(left_side[0], right_side[0], dims) + small


def piece_target(kind, device):
    along = 2 + 2 * (device & 1)
    flips = {"self": 0, "straight": along, "side": 6 - along, "corner": 6, "cross": along ^ 1, "diagonal": 7}
    return device ^ flips[kind]


def local_call(kernel, name, out_shape, operands, scalars=(), flops=0, vmem=None, **options):
    whole = pl.BlockSpec(memory_space=pltpu.VMEM)
    arrays = list(operands) + (list(out_shape) if isinstance(out_shape, (list, tuple)) else [out_shape])
    moved = sum(array.size * array.dtype.itemsize for array in arrays)
    return pl.pallas_call(
        kernel,
        in_specs=[pl.BlockSpec(memory_space=pltpu.SMEM)] * len(scalars) + [whole] * len(operands),
        out_specs=jax.tree.map(lambda _: whole, out_shape),
        out_shape=out_shape,
        compiler_params=pltpu.CompilerParams(vmem_limit_bytes=vmem or SMALL),
        cost_estimate=pl.CostEstimate(flops=flops, bytes_accessed=moved, transcendentals=0),
        name=name,
        **options,
    )(*scalars, *operands)


def owner_block(owners_ref, grad_ref, rows, width, target):
    column = 0
    for index in range(1, grad_ref.shape[1] // width):
        column = column + jnp.where(owners_ref[index] == target, index * width, 0)
    columns = pl.ds(pl.multiple_of(column, width), width)
    return grad_ref[rows, columns].astype(F32)


def rows_of(half, width):
    return pl.ds(0, width) if half is None else pl.ds(half * (width // 2), width // 2)


def piece_shape(half, width):
    return jax.ShapeDtypeStruct((width if half is None else width // 2, width), F32)


def piece_of(ref, half, width):
    return ref[rows_of(half, width), :] if ref.shape[0] == width else ref[...]


def pack_call(owners, me, grads, pieces, width):
    def kernel(owners_ref, me_ref, grad_ref, *out_refs):
        for (kind, half), out_ref in zip(pieces, out_refs):
            target = piece_target(kind, me_ref[0] ^ 1)
            out_ref[...] = owner_block(owners_ref, grad_ref, rows_of(half, width), width, target)

    shapes = [piece_shape(half, width) for _, half in pieces]
    return local_call(kernel, "pack", shapes, (grads,), (owners, me))


def add_call(owners, me, grads, kind, half, arrivals, width):
    flat = [value for arrival in arrivals for value in (arrival if isinstance(arrival, list) else [arrival])]

    def kernel(owners_ref, me_ref, grad_ref, *refs):
        target = piece_target(kind, me_ref[0])
        for part in HALVES if half is None else (half,):
            total = owner_block(owners_ref, grad_ref, rows_of(part, width), width, target)
            place = 0
            for arrival in arrivals:
                if isinstance(arrival, list):
                    total = total + refs[place + part][...]
                    place += 2
                else:
                    total = total + piece_of(refs[place], part, width)
                    place += 1
            if half is None:
                refs[-1][rows_of(part, width), :] = total
            else:
                refs[-1][...] = total

    return local_call(kernel, "add", piece_shape(half, width), (grads, *flat), (owners, me))


def join_call(owners, me, total, half, arrival, norm, block_count):
    width = total.shape[1]

    def kernel(owners_ref, me_ref, total_ref, arrival_ref, *refs):
        block_ref, norm_ref = refs[-2:]
        block = piece_of(total_ref, half, width) + arrival_ref[...]
        block_ref[...] = block
        owned = 0
        for index in range(block_count):
            owned = owned + jnp.where(owners_ref[index] == me_ref[0], 1, 0)
        squares = jnp.sum(block * block, keepdims=True).reshape(1, 1) * owned.astype(F32)
        total_squares = jnp.broadcast_to(squares, norm_ref.shape)
        norm_ref[...] = total_squares if norm is None else total_squares + refs[0][...]

    shapes = [piece_shape(half, width), jax.ShapeDtypeStruct((8, 128), F32)]
    operands = (total, arrival) if norm is None else (total, arrival, norm)
    return local_call(kernel, "join", shapes, operands, (owners, me))


def sum_kernel(*refs):
    total = refs[0][...]
    for ref in refs[1:-1]:
        total = total + ref[...]
    refs[-1][...] = total


def sum_call(*tiles):
    return local_call(sum_kernel, "sum", jax.ShapeDtypeStruct(tiles[0].shape, F32), tiles)


def whole_block(block_refs):
    return jnp.concatenate([ref[...] for ref in block_refs], axis=0)


def gram_kernel(upper_ref, lower_ref, left_ref, right_ref):
    block = split(whole_block((upper_ref, lower_ref)))
    left_ref[...] = split_product(block, block, ((1,), (1,)))
    right_ref[...] = split_product(block, block, ((0,), (0,)))


def gram_call(block):
    width = block[0].shape[1]
    shape = jax.ShapeDtypeStruct((width, width), F32)
    return local_call(gram_kernel, "gram", [shape, shape], block, flops=12 * width**3, vmem=LARGE)


def root_of(previous, gram, gram_scale):
    rows = lax.broadcasted_iota(jnp.int32, previous.shape, 0)
    columns = lax.broadcasted_iota(jnp.int32, previous.shape, 1)
    identity = jnp.where(rows == columns, 1.0, 0.0)
    statistic = 0.5 * previous + gram * gram_scale
    squares = jnp.sum(statistic * statistic, keepdims=True).reshape(1, 1)
    frobenius = jnp.sqrt(squares)
    scaled = statistic * (1.0 / frobenius)
    parts = split(scaled)
    square = split_product(parts, parts)
    factor_square = split((25.0 * identity - 10.0 * scaled + square) * 0.0625)
    factor_scaled = split((5.0 * scaled - square) * 0.25)
    fourth = split(split_product(factor_square, factor_square))
    tail = split_product(fourth, factor_scaled)
    return (6.25 * identity - 1.25 * scaled - tail) * (0.25 * lax.rsqrt(jnp.sqrt(frobenius)))


def update_call(block, left_gram, right_gram, left_prev, right_prev, norms, entry_count):
    width = block[0].shape[1]

    def kernel(upper_ref, lower_ref, left_gram_ref, right_gram_ref, left_ref, right_ref, *refs):
        norm_refs, out_refs = refs[:-3], refs[-3:]
        squares = sum(ref[:1, :1] for ref in norm_refs)
        clip_factor = jnp.minimum(1.0, clip_level / jnp.sqrt(squares / entry_count))
        gram_scale = clip_factor * clip_factor / width
        left_root = root_of(left_ref[...], left_gram_ref[...], gram_scale)
        right_root = root_of(right_ref[...], right_gram_ref[...], gram_scale)
        block = whole_block((upper_ref, lower_ref))
        halfway = split_product(split(left_root), split(block))
        pre = split_product(split(halfway), split(right_root)) * clip_factor
        block_norm = jnp.sum(block * block, keepdims=True).reshape(1, 1) * (clip_factor * clip_factor)
        pre_norm = jnp.sum(pre * pre, keepdims=True).reshape(1, 1)
        update = pre * jnp.sqrt(block_norm / (pre_norm + graft_eps))
        out_refs[0][...] = update
        for half in HALVES:
            out_refs[1 + half][...] = update[half * (width // 2) : (half + 1) * (width // 2)]

    operands = (*block, left_gram, right_gram, left_prev, right_prev, *norms)
    shapes = [piece_shape(half, width) for half in (None, *HALVES)]
    return local_call(kernel, "update", shapes, operands, flops=48 * width**3, vmem=LARGE)


def assemble_call(owners, me, places, slots, block_count, started):
    width = slots[0].shape[1]

    def kernel(owners_ref, me_ref, *refs):
        out_ref, sem = refs[-2:]
        copies = []
        for number, (kind, flip, half) in enumerate(places):
            target = piece_target(kind, me_ref[0] ^ flip)
            owned, column = 0, 0
            for index in range(block_count):
                matches = owners_ref[index] == target
                owned = owned + jnp.where(matches, 1, 0)
                column = column + jnp.where(matches, index * width, 0)
            columns = pl.ds(pl.multiple_of(column, width), width)
            spot = out_ref.at[rows_of(half, width), columns]
            copies.append((owned, pltpu.make_async_copy(refs[number], spot, sem.at[number])))
        for owned, copy in copies:
            pl.when(owned == 1)(copy.start)
        for owned, copy in copies:
            pl.when(owned == 1)(copy.wait)

    in_specs = [pl.BlockSpec(memory_space=pltpu.SMEM)] * 2
    in_specs += [pl.BlockSpec(memory_space=pltpu.VMEM)] * len(slots)
    operands = [owners, me, *slots]
    aliases = {}
    if started is not None:
        aliases = {len(operands): 0}
        in_specs.append(pl.BlockSpec(memory_space=pltpu.HBM))
        operands.append(started)
    return pl.pallas_call(
        kernel,
        in_specs=in_specs,
        out_specs=pl.BlockSpec(memory_space=pltpu.HBM),
        out_shape=jax.ShapeDtypeStruct((width, block_count * width), F32),
        scratch_shapes=[pltpu.SemaphoreType.DMA((len(slots),))],
        input_output_aliases=aliases,
        compiler_params=pltpu.CompilerParams(vmem_limit_bytes=SMALL),
        cost_estimate=pl.CostEstimate(
            flops=0, bytes_accessed=8 * slots[0].size * len(slots), transcendentals=0
        ),
        name="assemble",
    )(*operands)


def paired_body(replica_grads, owners, left_stats, right_stats):
    width = left_stats.shape[1]
    owner_row = owners[0]
    block_count = owner_row.shape[0]
    me = lax.axis_index("dp").astype(jnp.int32).reshape(1)
    group_count = lax.axis_size("mp")
    entry_count = width * block_count * width * group_count
    grads = replica_grads[0]

    def flipped(mask):
        return [(i, i ^ mask) for i in range(8)]

    def over(pairs, value, label):
        with jax.named_scope(label):
            return lax.ppermute(value, "dp", pairs)

    def to_core(value, label):
        return over(flipped(1), value, "core_" + label)

    def to_link(value, label):
        return over([(i, i ^ (2 + 2 * (i % 2))) for i in range(8)], value, "link_" + label)

    def to_side(value, label):
        return over([(i, i ^ (4 - 2 * (i % 2))) for i in range(8)], value, "side_" + label)

    def own_plus(kind, half, *arrivals):
        return add_call(owner_row, me, grads, kind, half, arrivals, width)

    def assemble(result, *pieces):
        return assemble_call(owner_row, me, *zip(*pieces), block_count, result)

    def after(value, *others):
        return lax.optimization_barrier((value, *others))[0]

    kinds = ("corner", "straight", "side", "self")
    pieces = []
    for pair in (kinds[:2], kinds[2:]):
        pieces += pack_call(owner_row, me, grads, [(kind, half) for kind in pair for half in HALVES], width)
    keys = [(kind, half) for kind in kinds for half in HALVES]
    from_core = {key: to_core(value, key[0]) for key, value in zip(keys, pieces)}
    from_link = {
        key: to_link(own_plus(*key, from_core[key]), key[0]) for key in keys if key[0] in kinds[:2]
    }
    arrived = [
        to_side(own_plus("side", half, from_core["side", half], from_link["corner", half]), "side")
        for half in HALVES
    ]
    totals = [
        own_plus("self", half, from_core["self", half], from_link["straight", half]) for half in HALVES
    ]
    norm, block = None, []
    for half in HALVES:
        joined, norm = join_call(owner_row, me, totals[half], half, arrived[half], norm, block_count)
        block.append(joined)
    norm = sum_call(norm, to_core(norm, "norm"))
    norm = sum_call(norm, *[over(flipped(mask), norm, "chip_norm") for mask in (2, 4, 6)])
    norms = [norm]
    for shift in range(1, group_count):
        pairs = [(i, (i + shift) % group_count) for i in range(group_count)]
        with jax.named_scope("group_norm"):
            norms.append(lax.ppermute(norm, "mp", pairs))
    left_gram, right_gram = gram_call(block)
    whole, *own = update_call(block, left_gram, right_gram, left_stats[0], right_stats[0], norms, entry_count)

    core_own = to_core(whole, "own")
    first = [to_link(value, "own") for value in own]
    core_first = [to_core(after(value, core_own), "first") for value in first]
    second = to_link(after(core_own, first[0]), "sibling")
    core_second = to_core(second, "second")
    relayed = [to_link(value, "relayed") for value in core_first]
    held = [(("self", 0, None), whole), (("self", 1, None), core_own)]
    held += [(("straight", 0, half), first[half]) for half in HALVES]
    held += [(("straight", 1, half), core_first[half]) for half in HALVES]
    crossed = [(("cross", 0, None), second), (("cross", 1, None), core_second)]
    result = assemble(None, *held)
    core_relayed = [to_core(after(relayed[0], result), "relayed"), to_core(relayed[1], "relayed")]
    result = assemble(result, *crossed, *[(("diagonal", 0, half), relayed[half]) for half in HALVES])
    return assemble(result, *[(("diagonal", 1, half), core_relayed[half]) for half in HALVES])


def solution(mesh):
    return jax.shard_map(
        paired_body if mesh.shape["dp"] == 8 else general_body,
        mesh=mesh,
        in_specs=(P("dp", None, "mp"), P("mp", None), P("dp", None, "mp"), P("dp", None, "mp")),
        out_specs=P(None, "mp"),
        check_vma=False,
    )
```

```python
import functools

import jax
import jax.numpy as jnp
from jax import lax
from jax.experimental import pallas as pl
from jax.experimental.pallas import tpu as pltpu
from jax.sharding import PartitionSpec as P

clip_level = 1.0
graft_eps = 1e-06


def mat_product(left_side, right_side):
    return jnp.matmul(left_side, right_side, precision=lax.Precision.HIGH)


def inverse_root(statistic):
    order_size = statistic.shape[-1]
    identity = jnp.eye(order_size, dtype=jnp.float32)
    frobenius = jnp.sqrt(jnp.sum(statistic * statistic))
    scaled = statistic / frobenius
    square = mat_product(scaled, scaled)
    factor_square = (25.0 * identity - 10.0 * scaled + square) * 0.0625
    factor_scaled = (5.0 * scaled - square) * 0.25
    fourth = mat_product(factor_square, factor_square)
    tail = mat_product(fourth, factor_scaled)
    return (6.25 * identity - 1.25 * scaled - tail) * (0.25 * frobenius ** (-0.25))


def general_body(replica_grads, owners, left_stats, right_stats):
    width = left_stats.shape[1]
    owner_row = owners[0]
    block_count = owner_row.shape[0]
    replica = lax.axis_index("dp")
    replica_count = lax.axis_size("dp")
    entry_count = width * block_count * width * lax.axis_size("mp")
    share_rows = width // replica_count
    share = lax.psum_scatter(
        replica_grads[0].astype(jnp.float32), "dp", scatter_dimension=0, tiled=True
    )
    squares = lax.psum(jnp.sum(share * share), ("dp", "mp"))
    clip_factor = jnp.minimum(1.0, clip_level / jnp.sqrt(squares / entry_count))
    share_blocks = jnp.transpose(share.reshape(share_rows, block_count, width), (1, 0, 2))
    targets = jnp.arange(replica_count, dtype=jnp.int32)
    routing = (owner_row[None, :] == targets[:, None]).astype(jnp.float32)
    outgoing = jnp.einsum("db,brc->drc", routing, share_blocks, precision=lax.Precision.HIGHEST)
    arrived = lax.all_to_all(outgoing, "dp", split_axis=0, concat_axis=0, tiled=True)
    block = arrived.reshape(width, width) * clip_factor
    update = block_update(block, jnp.sum(block * block), 1.0, left_stats[0], right_stats[0])
    chosen = (owner_row == replica).astype(jnp.float32)
    whole = lax.psum(chosen[:, None, None] * update[None], "dp")
    return jnp.transpose(whole, (1, 0, 2)).reshape(width, block_count * width)


def block_update(block, block_norm, clip_factor, left_prev, right_prev):
    order_size = block.shape[-1]
    stat_scale = clip_factor * clip_factor / order_size
    transposed = block.T
    left = 0.5 * left_prev + mat_product(block, transposed) * stat_scale
    right = 0.5 * right_prev + mat_product(transposed, block) * stat_scale
    pre = mat_product(mat_product(inverse_root(left), block), inverse_root(right)) * clip_factor
    pre_norm = jnp.sum(pre * pre)
    return pre * (clip_factor * jnp.sqrt(block_norm / (pre_norm + graft_eps)))


SMALL = 2 << 20
LARGE = 20 << 20
F32 = jnp.float32
HALVES = (0, 1)


def split(value):
    high = value.astype(jnp.bfloat16)
    return high, (value - high.astype(F32)).astype(jnp.bfloat16)


def left_operand(value):
    high, low = split(value)
    return jnp.concatenate([high, high, low], axis=1)


def right_operand(value):
    high, low = split(value)
    return jnp.concatenate([high, low, high], axis=0)


def triple_dot(left_side, right_side):
    return jnp.dot(left_side, right_side, preferred_element_type=F32)


def add_identity(value, amount):
    tile = 128
    rows = lax.broadcasted_iota(jnp.int32, (tile, tile), 0)
    columns = lax.broadcasted_iota(jnp.int32, (tile, tile), 1)
    diagonal = jnp.where(rows == columns, amount, 0.0)
    lines = []
    for i in range(value.shape[0] // tile):
        line = value[i * tile : (i + 1) * tile]
        parts = [line[:, j * tile : (j + 1) * tile] for j in range(value.shape[1] // tile)]
        parts[i] = parts[i] + diagonal
        lines.append(jnp.concatenate(parts, axis=1))
    return jnp.concatenate(lines, axis=0)


def piece_target(kind, device):
    along = 2 + 2 * (device & 1)
    flips = {"self": 0, "straight": along, "side": 6 - along, "corner": 6, "cross": along ^ 1, "diagonal": 7}
    return device ^ flips[kind]


def local_call(kernel, name, out_shape, operands, scalars=(), flops=0, vmem=None, **options):
    whole = pl.BlockSpec(memory_space=pltpu.VMEM)
    arrays = list(operands) + (list(out_shape) if isinstance(out_shape, (list, tuple)) else [out_shape])
    moved = sum(array.size * array.dtype.itemsize for array in arrays)
    return pl.pallas_call(
        kernel,
        in_specs=[pl.BlockSpec(memory_space=pltpu.SMEM)] * len(scalars) + [whole] * len(operands),
        out_specs=jax.tree.map(lambda _: whole, out_shape),
        out_shape=out_shape,
        compiler_params=pltpu.CompilerParams(vmem_limit_bytes=vmem or SMALL),
        cost_estimate=pl.CostEstimate(flops=flops, bytes_accessed=moved, transcendentals=0),
        name=name,
        **options,
    )(*scalars, *operands)


def owner_block(owners_ref, grad_ref, rows, width, target):
    column = 0
    for index in range(1, grad_ref.shape[1] // width):
        column = column + jnp.where(owners_ref[index] == target, index * width, 0)
    columns = pl.ds(pl.multiple_of(column, width), width)
    return grad_ref[rows, columns].astype(F32)


def rows_of(half, width):
    return pl.ds(0, width) if half is None else pl.ds(half * (width // 2), width // 2)


def piece_shape(half, width):
    return jax.ShapeDtypeStruct((width if half is None else width // 2, width), F32)


def piece_of(ref, half, width):
    return ref[rows_of(half, width), :] if ref.shape[0] == width else ref[...]


def pack_call(owners, me, grads, pieces, width):
    def kernel(owners_ref, me_ref, grad_ref, *out_refs):
        for (kind, half), out_ref in zip(pieces, out_refs):
            target = piece_target(kind, me_ref[0] ^ 1)
            out_ref[...] = owner_block(owners_ref, grad_ref, rows_of(half, width), width, target)

    shapes = [piece_shape(half, width) for _, half in pieces]
    return local_call(kernel, "pack", shapes, (grads,), (owners, me))


def add_call(owners, me, grads, kind, half, arrivals, width):
    flat = [value for arrival in arrivals for value in (arrival if isinstance(arrival, list) else [arrival])]

    def kernel(owners_ref, me_ref, grad_ref, *refs):
        target = piece_target(kind, me_ref[0])
        for part in HALVES if half is None else (half,):
            total = owner_block(owners_ref, grad_ref, rows_of(part, width), width, target)
            place = 0
            for arrival in arrivals:
                if isinstance(arrival, list):
                    total = total + refs[place + part][...]
                    place += 2
                else:
                    total = total + piece_of(refs[place], part, width)
                    place += 1
            if half is None:
                refs[-1][rows_of(part, width), :] = total
            else:
                refs[-1][...] = total

    return local_call(kernel, "add", piece_shape(half, width), (grads, *flat), (owners, me))


def join_call(owners, me, total, half, arrival, norm, block_count):
    width = total.shape[1]

    def kernel(owners_ref, me_ref, total_ref, arrival_ref, *refs):
        block_ref, norm_ref = refs[-2:]
        block = piece_of(total_ref, half, width) + arrival_ref[...]
        block_ref[...] = block
        owned = 0
        for index in range(block_count):
            owned = owned + jnp.where(owners_ref[index] == me_ref[0], 1, 0)
        squares = jnp.sum(block * block, keepdims=True).reshape(1, 1) * owned.astype(F32)
        total_squares = jnp.broadcast_to(squares, norm_ref.shape)
        norm_ref[...] = total_squares if norm is None else total_squares + refs[0][...]

    shapes = [piece_shape(half, width), jax.ShapeDtypeStruct((8, 128), F32)]
    operands = (total, arrival) if norm is None else (total, arrival, norm)
    return local_call(kernel, "join", shapes, operands, (owners, me))


def sum_kernel(*refs):
    total = refs[0][...]
    for ref in refs[1:-1]:
        total = total + ref[...]
    refs[-1][...] = total


def sum_call(*tiles):
    return local_call(sum_kernel, "sum", jax.ShapeDtypeStruct(tiles[0].shape, F32), tiles)


def whole_block(block_refs):
    return jnp.concatenate([ref[...] for ref in block_refs], axis=0)


def gram_kernel(upper_ref, lower_ref, left_ref, right_ref):
    block = whole_block((upper_ref, lower_ref))
    high, low = split(block)
    across = jnp.concatenate([high, high, low], axis=1)
    across_other = jnp.concatenate([high, low, high], axis=1)
    down = jnp.concatenate([high, high, low], axis=0)
    down_other = jnp.concatenate([high, low, high], axis=0)
    left_ref[...] = lax.dot_general(across, across_other, (((1,), (1,)), ((), ())), preferred_element_type=F32)
    right_ref[...] = lax.dot_general(down, down_other, (((0,), (0,)), ((), ())), preferred_element_type=F32)


def gram_call(block):
    width = block[0].shape[1]
    shape = jax.ShapeDtypeStruct((width, width), F32)
    return local_call(gram_kernel, "gram", [shape, shape], block, flops=12 * width**3, vmem=LARGE)


def roots_of(previous, grams, gram_scale):
    statistics = [0.5 * prev + gram * gram_scale for prev, gram in zip(previous, grams)]
    frobenius = [jnp.sqrt(jnp.sum(value * value, keepdims=True).reshape(1, 1)) for value in statistics]
    scaled = [value * (1.0 / norm) for value, norm in zip(statistics, frobenius)]
    square = [triple_dot(left_operand(value), right_operand(value)) for value in scaled]
    factor_square = [add_identity(0.0625 * q - 0.625 * m, 1.5625) for q, m in zip(square, scaled)]
    factor_scaled = [1.25 * m - 0.25 * q for q, m in zip(square, scaled)]
    fourth = [triple_dot(left_operand(value), right_operand(value)) for value in factor_square]
    tail = [triple_dot(left_operand(f), right_operand(m)) for f, m in zip(fourth, factor_scaled)]
    roots = [add_identity(-1.25 * m - t, 6.25) for m, t in zip(scaled, tail)]
    return roots, [0.25 * lax.rsqrt(jnp.sqrt(norm)) for norm in frobenius]


def update_call(block, block_norm, left_gram, right_gram, left_prev, right_prev, norms, entry_count):
    width = block[0].shape[1]

    def kernel(upper_ref, lower_ref, block_norm_ref, left_gram_ref, right_gram_ref, left_ref, right_ref, *refs):
        norm_refs, out_refs = refs[:-3], refs[-3:]
        squares = sum(ref[:1, :1] for ref in norm_refs)
        clip_factor = jnp.minimum(1.0, clip_level / jnp.sqrt(squares / entry_count))
        gram_scale = clip_factor * clip_factor / width
        previous, grams = (left_ref[...], right_ref[...]), (left_gram_ref[...], right_gram_ref[...])
        roots, scales = roots_of(previous, grams, gram_scale)
        halfway = triple_dot(left_operand(roots[0]), right_operand(whole_block((upper_ref, lower_ref))))
        pre = triple_dot(left_operand(halfway), right_operand(roots[1]))
        pre_scale = scales[0] * scales[1] * clip_factor
        pre_norm = jnp.sum(pre * pre, keepdims=True).reshape(1, 1) * (pre_scale * pre_scale)
        clipped_norm = block_norm_ref[:1, :1] * (clip_factor * clip_factor)
        update = pre * (pre_scale * jnp.sqrt(clipped_norm / (pre_norm + graft_eps)))
        out_refs[0][...] = update
        for half in HALVES:
            out_refs[1 + half][...] = update[half * (width // 2) : (half + 1) * (width // 2)]

    operands = (*block, block_norm, left_gram, right_gram, left_prev, right_prev, *norms)
    shapes = [piece_shape(half, width) for half in (None, *HALVES)]
    return local_call(kernel, "update", shapes, operands, flops=48 * width**3, vmem=LARGE)


def assemble_call(owners, me, places, slots, block_count, started):
    width = slots[0].shape[1]

    def kernel(owners_ref, me_ref, *refs):
        out_ref, sem = refs[-2:]
        copies = []
        for number, (kind, flip, half) in enumerate(places):
            target = piece_target(kind, me_ref[0] ^ flip)
            owned, column = 0, 0
            for index in range(block_count):
                matches = owners_ref[index] == target
                owned = owned + jnp.where(matches, 1, 0)
                column = column + jnp.where(matches, index * width, 0)
            columns = pl.ds(pl.multiple_of(column, width), width)
            spot = out_ref.at[rows_of(half, width), columns]
            copies.append((owned, pltpu.make_async_copy(refs[number], spot, sem.at[number])))
        for owned, copy in copies:
            pl.when(owned == 1)(copy.start)
        for owned, copy in copies:
            pl.when(owned == 1)(copy.wait)

    in_specs = [pl.BlockSpec(memory_space=pltpu.SMEM)] * 2
    in_specs += [pl.BlockSpec(memory_space=pltpu.VMEM)] * len(slots)
    operands = [owners, me, *slots]
    aliases = {}
    if started is not None:
        aliases = {len(operands): 0}
        in_specs.append(pl.BlockSpec(memory_space=pltpu.HBM))
        operands.append(started)
    return pl.pallas_call(
        kernel,
        in_specs=in_specs,
        out_specs=pl.BlockSpec(memory_space=pltpu.HBM),
        out_shape=jax.ShapeDtypeStruct((width, block_count * width), F32),
        scratch_shapes=[pltpu.SemaphoreType.DMA((len(slots),))],
        input_output_aliases=aliases,
        compiler_params=pltpu.CompilerParams(vmem_limit_bytes=SMALL),
        cost_estimate=pl.CostEstimate(
            flops=0, bytes_accessed=8 * slots[0].size * len(slots), transcendentals=0
        ),
        name="assemble",
    )(*operands)


def paired_body(replica_grads, owners, left_stats, right_stats):
    width = left_stats.shape[1]
    owner_row = owners[0]
    block_count = owner_row.shape[0]
    me = lax.axis_index("dp").astype(jnp.int32).reshape(1)
    group_count = lax.axis_size("mp")
    entry_count = width * block_count * width * group_count
    grads = replica_grads[0]

    def flipped(mask):
        return [(i, i ^ mask) for i in range(8)]

    def over(pairs, value, label):
        with jax.named_scope(label):
            return lax.ppermute(value, "dp", pairs)

    def to_core(value, label):
        return over(flipped(1), value, "core_" + label)

    def to_link(value, label):
        return over([(i, i ^ (2 + 2 * (i % 2))) for i in range(8)], value, "link_" + label)

    def to_side(value, label):
        return over([(i, i ^ (4 - 2 * (i % 2))) for i in range(8)], value, "side_" + label)

    def own_plus(kind, half, *arrivals):
        return add_call(owner_row, me, grads, kind, half, arrivals, width)

    def assemble(result, *pieces):
        return assemble_call(owner_row, me, *zip(*pieces), block_count, result)

    def after(value, *others):
        return lax.optimization_barrier((value, *others))[0]

    kinds = ("corner", "straight", "side", "self")
    pieces = []
    for pair in (kinds[:2], kinds[2:]):
        pieces += pack_call(owner_row, me, grads, [(kind, half) for kind in pair for half in HALVES], width)
    keys = [(kind, half) for kind in kinds for half in HALVES]
    from_core = {key: to_core(value, key[0]) for key, value in zip(keys, pieces)}
    from_link = {
        key: to_link(own_plus(*key, from_core[key]), key[0]) for key in keys if key[0] in kinds[:2]
    }
    arrived = [
        to_side(own_plus("side", half, from_core["side", half], from_link["corner", half]), "side")
        for half in HALVES
    ]
    totals = [
        own_plus("self", half, from_core["self", half], from_link["straight", half]) for half in HALVES
    ]
    norm, block = None, []
    for half in HALVES:
        joined, norm = join_call(owner_row, me, totals[half], half, arrived[half], norm, block_count)
        block.append(joined)
    block_norm = norm
    norm = sum_call(norm, to_core(norm, "norm"))
    norm = sum_call(norm, *[over(flipped(mask), norm, "chip_norm") for mask in (2, 4, 6)])
    norms = [norm]
    for shift in range(1, group_count):
        both_ways = group_count & (group_count - 1) == 0
        pairs = [(i, i ^ shift if both_ways else (i + shift) % group_count) for i in range(group_count)]
        with jax.named_scope("group_norm"):
            norms.append(lax.ppermute(norm, "mp", pairs))
    left_gram, right_gram = gram_call(block)
    whole, *own = update_call(
        block, block_norm, left_gram, right_gram, left_stats[0], right_stats[0], norms, entry_count
    )

    core_own = to_core(whole, "own")
    first = [to_link(value, "own") for value in own]
    core_first = [to_core(after(value, core_own), "first") for value in first]
    second = to_link(after(core_own, first[0]), "sibling")
    core_second = to_core(second, "second")
    relayed = [to_link(value, "relayed") for value in core_first]
    held = [(("self", 0, None), whole), (("self", 1, None), core_own)]
    held += [(("straight", 0, half), first[half]) for half in HALVES]
    held += [(("straight", 1, half), core_first[half]) for half in HALVES]
    crossed = [(("cross", 0, None), second), (("cross", 1, None), core_second)]
    result = assemble(None, *held)
    core_relayed = [to_core(after(relayed[0], result), "relayed"), to_core(relayed[1], "relayed")]
    result = assemble(result, *crossed, *[(("diagonal", 0, half), relayed[half]) for half in HALVES])
    return assemble(result, *[(("diagonal", 1, half), core_relayed[half]) for half in HALVES])


def solution(mesh):
    return jax.shard_map(
        paired_body if mesh.shape["dp"] == 8 else general_body,
        mesh=mesh,
        in_specs=(P("dp", None, "mp"), P("mp", None), P("dp", None, "mp"), P("dp", None, "mp")),
        out_specs=P(None, "mp"),
        check_vma=False,
    )
```

```python
import functools

import jax
import jax.numpy as jnp
from jax import lax
from jax.experimental import pallas as pl
from jax.experimental.pallas import tpu as pltpu
from jax.sharding import PartitionSpec as P

clip_level = 1.0
graft_eps = 1e-06


def mat_product(left_side, right_side):
    return jnp.matmul(left_side, right_side, precision=lax.Precision.HIGH)


def inverse_root(statistic):
    order_size = statistic.shape[-1]
    identity = jnp.eye(order_size, dtype=jnp.float32)
    frobenius = jnp.sqrt(jnp.sum(statistic * statistic))
    scaled = statistic / frobenius
    square = mat_product(scaled, scaled)
    factor_square = (25.0 * identity - 10.0 * scaled + square) * 0.0625
    factor_scaled = (5.0 * scaled - square) * 0.25
    fourth = mat_product(factor_square, factor_square)
    tail = mat_product(fourth, factor_scaled)
    return (6.25 * identity - 1.25 * scaled - tail) * (0.25 * frobenius ** (-0.25))


def general_body(replica_grads, owners, left_stats, right_stats):
    width = left_stats.shape[1]
    owner_row = owners[0]
    block_count = owner_row.shape[0]
    replica = lax.axis_index("dp")
    replica_count = lax.axis_size("dp")
    entry_count = width * block_count * width * lax.axis_size("mp")
    share_rows = width // replica_count
    share = lax.psum_scatter(
        replica_grads[0].astype(jnp.float32), "dp", scatter_dimension=0, tiled=True
    )
    squares = lax.psum(jnp.sum(share * share), ("dp", "mp"))
    clip_factor = jnp.minimum(1.0, clip_level / jnp.sqrt(squares / entry_count))
    share_blocks = jnp.transpose(share.reshape(share_rows, block_count, width), (1, 0, 2))
    targets = jnp.arange(replica_count, dtype=jnp.int32)
    routing = (owner_row[None, :] == targets[:, None]).astype(jnp.float32)
    outgoing = jnp.einsum("db,brc->drc", routing, share_blocks, precision=lax.Precision.HIGHEST)
    arrived = lax.all_to_all(outgoing, "dp", split_axis=0, concat_axis=0, tiled=True)
    block = arrived.reshape(width, width) * clip_factor
    update = block_update(block, jnp.sum(block * block), 1.0, left_stats[0], right_stats[0])
    chosen = (owner_row == replica).astype(jnp.float32)
    whole = lax.psum(chosen[:, None, None] * update[None], "dp")
    return jnp.transpose(whole, (1, 0, 2)).reshape(width, block_count * width)


def block_update(block, block_norm, clip_factor, left_prev, right_prev):
    order_size = block.shape[-1]
    stat_scale = clip_factor * clip_factor / order_size
    transposed = block.T
    left = 0.5 * left_prev + mat_product(block, transposed) * stat_scale
    right = 0.5 * right_prev + mat_product(transposed, block) * stat_scale
    pre = mat_product(mat_product(inverse_root(left), block), inverse_root(right)) * clip_factor
    pre_norm = jnp.sum(pre * pre)
    return pre * (clip_factor * jnp.sqrt(block_norm / (pre_norm + graft_eps)))


SMALL = 2 << 20
LARGE = 20 << 20
F32 = jnp.float32
HALVES = (0, 1)


def split(value):
    high = value.astype(jnp.bfloat16)
    return high, (value - high.astype(F32)).astype(jnp.bfloat16)


def left_operand(value):
    high, low = split(value)
    return jnp.concatenate([high, high, low], axis=1)


def right_operand(value):
    high, low = split(value)
    return jnp.concatenate([high, low, high], axis=0)


def triple_dot(left_side, right_side):
    return jnp.dot(left_side, right_side, preferred_element_type=F32)


def mirrored(upper, corner):
    half = corner.shape[0]
    lower = jnp.concatenate([upper[:, half:].T, corner], axis=1)
    return jnp.concatenate([upper, lower], axis=0)


def symmetric_dot(left_side, right_side):
    half = left_side.shape[0] // 2
    upper = triple_dot(left_side[:half], right_side)
    return mirrored(upper, triple_dot(left_side[half:], right_side[:, half:]))


def add_identity(value, amount):
    tile = 128
    rows = lax.broadcasted_iota(jnp.int32, (tile, tile), 0)
    columns = lax.broadcasted_iota(jnp.int32, (tile, tile), 1)
    diagonal = jnp.where(rows == columns, amount, 0.0)
    lines = []
    for i in range(value.shape[0] // tile):
        line = value[i * tile : (i + 1) * tile]
        parts = [line[:, j * tile : (j + 1) * tile] for j in range(value.shape[1] // tile)]
        parts[i] = parts[i] + diagonal
        lines.append(jnp.concatenate(parts, axis=1))
    return jnp.concatenate(lines, axis=0)


def piece_target(kind, device):
    along = 2 + 2 * (device & 1)
    flips = {"self": 0, "straight": along, "side": 6 - along, "corner": 6, "cross": along ^ 1, "diagonal": 7}
    return device ^ flips[kind]


def local_call(kernel, name, out_shape, operands, scalars=(), flops=0, vmem=None, **options):
    whole = pl.BlockSpec(memory_space=pltpu.VMEM)
    arrays = list(operands) + (list(out_shape) if isinstance(out_shape, (list, tuple)) else [out_shape])
    moved = sum(array.size * array.dtype.itemsize for array in arrays)
    return pl.pallas_call(
        kernel,
        in_specs=[pl.BlockSpec(memory_space=pltpu.SMEM)] * len(scalars) + [whole] * len(operands),
        out_specs=jax.tree.map(lambda _: whole, out_shape),
        out_shape=out_shape,
        compiler_params=pltpu.CompilerParams(vmem_limit_bytes=vmem or SMALL),
        cost_estimate=pl.CostEstimate(flops=flops, bytes_accessed=moved, transcendentals=0),
        name=name,
        **options,
    )(*scalars, *operands)


def owner_block(owners_ref, grad_ref, rows, width, target):
    column = 0
    for index in range(1, grad_ref.shape[1] // width):
        column = column + jnp.where(owners_ref[index] == target, index * width, 0)
    columns = pl.ds(pl.multiple_of(column, width), width)
    return grad_ref[rows, columns].astype(F32)


def rows_of(half, width):
    return pl.ds(0, width) if half is None else pl.ds(half * (width // 2), width // 2)


def piece_shape(half, width):
    return jax.ShapeDtypeStruct((width if half is None else width // 2, width), F32)


def piece_of(ref, half, width):
    return ref[rows_of(half, width), :] if ref.shape[0] == width else ref[...]


def pack_call(owners, me, grads, pieces, width):
    def kernel(owners_ref, me_ref, grad_ref, *out_refs):
        for (kind, half), out_ref in zip(pieces, out_refs):
            target = piece_target(kind, me_ref[0] ^ 1)
            out_ref[...] = owner_block(owners_ref, grad_ref, rows_of(half, width), width, target)

    shapes = [piece_shape(half, width) for _, half in pieces]
    return local_call(kernel, "pack", shapes, (grads,), (owners, me))


def add_call(owners, me, grads, kind, half, arrivals, width):
    flat = [value for arrival in arrivals for value in (arrival if isinstance(arrival, list) else [arrival])]

    def kernel(owners_ref, me_ref, grad_ref, *refs):
        target = piece_target(kind, me_ref[0])
        for part in HALVES if half is None else (half,):
            total = owner_block(owners_ref, grad_ref, rows_of(part, width), width, target)
            place = 0
            for arrival in arrivals:
                if isinstance(arrival, list):
                    total = total + refs[place + part][...]
                    place += 2
                else:
                    total = total + piece_of(refs[place], part, width)
                    place += 1
            if half is None:
                refs[-1][rows_of(part, width), :] = total
            else:
                refs[-1][...] = total

    return local_call(kernel, "add", piece_shape(half, width), (grads, *flat), (owners, me))


def join_call(owners, me, total, half, arrival, norm, block_count):
    width = total.shape[1]

    def kernel(owners_ref, me_ref, total_ref, arrival_ref, *refs):
        block_ref, norm_ref = refs[-2:]
        block = piece_of(total_ref, half, width) + arrival_ref[...]
        block_ref[...] = block
        owned = 0
        for index in range(block_count):
            owned = owned + jnp.where(owners_ref[index] == me_ref[0], 1, 0)
        squares = jnp.sum(block * block, keepdims=True).reshape(1, 1) * owned.astype(F32)
        total_squares = jnp.broadcast_to(squares, norm_ref.shape)
        norm_ref[...] = total_squares if norm is None else total_squares + refs[0][...]

    shapes = [piece_shape(half, width), jax.ShapeDtypeStruct((8, 128), F32)]
    operands = (total, arrival) if norm is None else (total, arrival, norm)
    return local_call(kernel, "join", shapes, operands, (owners, me))


def sum_kernel(*refs):
    total = refs[0][...]
    for ref in refs[1:-1]:
        total = total + ref[...]
    refs[-1][...] = total


def sum_call(*tiles):
    return local_call(sum_kernel, "sum", jax.ShapeDtypeStruct(tiles[0].shape, F32), tiles)


def whole_block(block_refs):
    return jnp.concatenate([ref[...] for ref in block_refs], axis=0)


def gram_kernel(upper_ref, lower_ref, left_ref, right_ref):
    high, low = split(whole_block((upper_ref, lower_ref)))
    for axis, out_ref in ((1, left_ref), (0, right_ref)):
        first = jnp.concatenate([high, high, low], axis=axis)
        second = jnp.concatenate([high, low, high], axis=axis)
        half = high.shape[0] // 2
        dims = (((axis,), (axis,)), ((), ()))
        first_upper = first[:half] if axis == 1 else first[:, :half]
        first_lower = first[half:] if axis == 1 else first[:, half:]
        second_lower = second[half:] if axis == 1 else second[:, half:]
        upper = lax.dot_general(first_upper, second, dims, preferred_element_type=F32)
        corner = lax.dot_general(first_lower, second_lower, dims, preferred_element_type=F32)
        out_ref[...] = mirrored(upper, corner)


def gram_call(block):
    width = block[0].shape[1]
    shape = jax.ShapeDtypeStruct((width, width), F32)
    return local_call(gram_kernel, "gram", [shape, shape], block, flops=12 * width**3, vmem=LARGE)


def square_kernel(*refs):
    for ref, out_ref in zip(refs[: len(refs) // 2], refs[len(refs) // 2 :]):
        value = ref[...]
        out_ref[...] = symmetric_dot(left_operand(value), right_operand(value))


def square_call(*statistics):
    shapes = [jax.ShapeDtypeStruct(value.shape, F32) for value in statistics]
    flops = 6 * len(statistics) * statistics[0].shape[0] ** 3
    return local_call(square_kernel, "square", shapes, statistics, flops=flops, vmem=LARGE)


def mix_kernel(previous_ref, gram_ref, mixed_ref, square_ref):
    gram = gram_ref[...]
    gram_right = right_operand(gram)
    product = triple_dot(left_operand(previous_ref[...]), gram_right)
    square_ref[...] = symmetric_dot(left_operand(gram), gram_right)
    mixed_ref[...] = product + product.T


def mix_call(previous, gram):
    shape = jax.ShapeDtypeStruct(gram.shape, F32)
    flops = 12 * gram.shape[0] ** 3
    return local_call(mix_kernel, "mix", [shape, shape], (previous, gram), flops=flops, vmem=LARGE)


def roots_of(sides, gram_scale):
    statistics = [0.5 * previous[...] + gram[...] * gram_scale for previous, gram, _, _, _ in sides]
    norms = [jnp.sum(value * value, keepdims=True).reshape(1, 1) for value in statistics]
    factor_square, factor_scaled, kept = [], [], []
    for statistic, norm, (_, _, previous_square, mixed, gram_square) in zip(statistics, norms, sides):
        inverse = 1.0 / norm
        scaled = statistic * jnp.sqrt(inverse)
        square = previous_square[...] * (0.25 * inverse) + mixed[...] * (0.5 * gram_scale * inverse)
        square = square + gram_square[...] * (gram_scale * gram_scale * inverse)
        factor_square.append(add_identity(0.0625 * square - 0.625 * scaled, 1.5625))
        factor_scaled.append(1.25 * scaled - 0.25 * square)
        kept.append(scaled)
    fourth = [symmetric_dot(left_operand(value), right_operand(value)) for value in factor_square]
    tail = [symmetric_dot(left_operand(f), right_operand(m)) for f, m in zip(fourth, factor_scaled)]
    roots = [add_identity(-1.25 * m - t, 6.25) for m, t in zip(kept, tail)]
    return roots, [0.25 * lax.rsqrt(jnp.sqrt(jnp.sqrt(norm))) for norm in norms]


def update_call(block, block_norm, left, right, norms, entry_count):
    width = block[0].shape[1]

    def kernel(upper_ref, lower_ref, block_norm_ref, *refs):
        left_refs, right_refs, norm_refs, out_refs = refs[:5], refs[5:10], refs[10:-3], refs[-3:]
        squares = sum(ref[:1, :1] for ref in norm_refs)
        clip_factor = jnp.minimum(1.0, clip_level / jnp.sqrt(squares / entry_count))
        gram_scale = clip_factor * clip_factor / width
        roots, scales = roots_of((left_refs, right_refs), gram_scale)
        halfway = triple_dot(left_operand(roots[0]), right_operand(whole_block((upper_ref, lower_ref))))
        pre = triple_dot(left_operand(halfway), right_operand(roots[1]))
        pre_scale = scales[0] * scales[1] * clip_factor
        pre_norm = jnp.sum(pre * pre, keepdims=True).reshape(1, 1) * (pre_scale * pre_scale)
        clipped_norm = block_norm_ref[:1, :1] * (clip_factor * clip_factor)
        update = pre * (pre_scale * jnp.sqrt(clipped_norm / (pre_norm + graft_eps)))
        out_refs[0][...] = update
        for half in HALVES:
            out_refs[1 + half][...] = update[half * (width // 2) : (half + 1) * (width // 2)]

    operands = (*block, block_norm, *left, *right, *norms)
    shapes = [piece_shape(half, width) for half in (None, *HALVES)]
    return local_call(kernel, "update", shapes, operands, flops=36 * width**3, vmem=LARGE)


def assemble_call(owners, me, places, slots, block_count, started):
    width = slots[0].shape[1]

    def kernel(owners_ref, me_ref, *refs):
        out_ref, sem = refs[-2:]
        copies = []
        for number, (kind, flip, half) in enumerate(places):
            target = piece_target(kind, me_ref[0] ^ flip)
            owned, column = 0, 0
            for index in range(block_count):
                matches = owners_ref[index] == target
                owned = owned + jnp.where(matches, 1, 0)
                column = column + jnp.where(matches, index * width, 0)
            columns = pl.ds(pl.multiple_of(column, width), width)
            spot = out_ref.at[rows_of(half, width), columns]
            copies.append((owned, pltpu.make_async_copy(refs[number], spot, sem.at[number])))
        for owned, copy in copies:
            pl.when(owned == 1)(copy.start)
        for owned, copy in copies:
            pl.when(owned == 1)(copy.wait)

    in_specs = [pl.BlockSpec(memory_space=pltpu.SMEM)] * 2
    in_specs += [pl.BlockSpec(memory_space=pltpu.VMEM)] * len(slots)
    operands = [owners, me, *slots]
    aliases = {}
    if started is not None:
        aliases = {len(operands): 0}
        in_specs.append(pl.BlockSpec(memory_space=pltpu.HBM))
        operands.append(started)
    return pl.pallas_call(
        kernel,
        in_specs=in_specs,
        out_specs=pl.BlockSpec(memory_space=pltpu.HBM),
        out_shape=jax.ShapeDtypeStruct((width, block_count * width), F32),
        scratch_shapes=[pltpu.SemaphoreType.DMA((len(slots),))],
        input_output_aliases=aliases,
        compiler_params=pltpu.CompilerParams(vmem_limit_bytes=SMALL),
        cost_estimate=pl.CostEstimate(
            flops=0, bytes_accessed=8 * slots[0].size * len(slots), transcendentals=0
        ),
        name="assemble",
    )(*operands)


def paired_body(replica_grads, owners, left_stats, right_stats):
    width = left_stats.shape[1]
    owner_row = owners[0]
    block_count = owner_row.shape[0]
    me = lax.axis_index("dp").astype(jnp.int32).reshape(1)
    group_count = lax.axis_size("mp")
    entry_count = width * block_count * width * group_count
    grads = replica_grads[0]

    def flipped(mask):
        return [(i, i ^ mask) for i in range(8)]

    def over(pairs, value, label):
        with jax.named_scope(label):
            return lax.ppermute(value, "dp", pairs)

    def to_core(value, label):
        return over(flipped(1), value, "core_" + label)

    def to_link(value, label):
        return over([(i, i ^ (2 + 2 * (i % 2))) for i in range(8)], value, "link_" + label)

    def to_side(value, label):
        return over([(i, i ^ (4 - 2 * (i % 2))) for i in range(8)], value, "side_" + label)

    def own_plus(kind, half, *arrivals):
        return add_call(owner_row, me, grads, kind, half, arrivals, width)

    def assemble(result, *pieces):
        return assemble_call(owner_row, me, *zip(*pieces), block_count, result)

    def after(value, *others):
        return lax.optimization_barrier((value, *others))[0]

    kinds = ("corner", "straight", "side", "self")
    pieces = []
    for pair in (kinds[:2], kinds[2:]):
        pieces += pack_call(owner_row, me, grads, [(kind, half) for kind in pair for half in HALVES], width)
    keys = [(kind, half) for kind in kinds for half in HALVES]
    from_core = {key: to_core(value, key[0]) for key, value in zip(keys, pieces)}
    from_link = {
        key: to_link(own_plus(*key, from_core[key]), key[0]) for key in keys if key[0] in kinds[:2]
    }
    arrived = [
        to_side(own_plus("side", half, from_core["side", half], from_link["corner", half]), "side")
        for half in HALVES
    ]
    totals = [
        own_plus("self", half, from_core["self", half], from_link["straight", half]) for half in HALVES
    ]
    sides = [(left_stats[0],), (right_stats[0],)]
    squares = square_call(*[after(previous, totals[0]) for previous, in sides])
    totals[0] = after(totals[0], *squares)
    norm, block = None, []
    for half in HALVES:
        joined, norm = join_call(owner_row, me, totals[half], half, arrived[half], norm, block_count)
        block.append(joined)
    block_norm = norm
    norm = sum_call(norm, to_core(norm, "norm"))
    chip_norms = [over(flipped(mask), norm, "chip_norm") for mask in (2, 4, 6)]
    grams = gram_call([after(block[0], norm), block[1]])
    sides = [(previous, gram, square) for (previous,), gram, square in zip(sides, grams, squares)]
    sides[0] += tuple(mix_call(*sides[0][:2]))
    norm = sum_call(after(norm, sides[0][4]), *chip_norms)
    norms = [norm]
    for shift in range(1, group_count):
        pairs = [(i, (i + shift) % group_count) for i in range(group_count)]
        with jax.named_scope("group_norm"):
            norms.append(lax.ppermute(norm, "mp", pairs))
    sides[1] += tuple(mix_call(*sides[1][:2]))
    whole, *own = update_call(block, block_norm, *sides, norms, entry_count)

    core_own = to_core(whole, "own")
    first = [to_link(value, "own") for value in own]
    core_first = [to_core(after(value, core_own), "first") for value in first]
    second = to_link(after(core_own, first[0]), "sibling")
    core_second = to_core(second, "second")
    relayed = [to_link(value, "relayed") for value in core_first]
    held = [(("self", 0, None), whole), (("self", 1, None), core_own)]
    held += [(("straight", 0, half), first[half]) for half in HALVES]
    held += [(("straight", 1, half), core_first[half]) for half in HALVES]
    crossed = [(("cross", 0, None), second), (("cross", 1, None), core_second)]
    result = assemble(None, *held)
    core_relayed = [to_core(after(relayed[0], result), "relayed"), to_core(relayed[1], "relayed")]
    result = assemble(result, *crossed, *[(("diagonal", 0, half), relayed[half]) for half in HALVES])
    return assemble(result, *[(("diagonal", 1, half), core_relayed[half]) for half in HALVES])


def solution(mesh):
    return jax.shard_map(
        paired_body if mesh.shape["dp"] == 8 else general_body,
        mesh=mesh,
        in_specs=(P("dp", None, "mp"), P("mp", None), P("dp", None, "mp"), P("dp", None, "mp")),
        out_specs=P(None, "mp"),
        check_vma=False,
    )
```

```python
import functools

import jax
import jax.numpy as jnp
from jax import lax
from jax.experimental import pallas as pl
from jax.experimental.pallas import tpu as pltpu
from jax.sharding import PartitionSpec as P

clip_level = 1.0
graft_eps = 1e-06


def mat_product(left_side, right_side):
    return jnp.matmul(left_side, right_side, precision=lax.Precision.HIGH)


def inverse_root(statistic):
    order_size = statistic.shape[-1]
    identity = jnp.eye(order_size, dtype=jnp.float32)
    frobenius = jnp.sqrt(jnp.sum(statistic * statistic))
    scaled = statistic / frobenius
    square = mat_product(scaled, scaled)
    factor_square = (25.0 * identity - 10.0 * scaled + square) * 0.0625
    factor_scaled = (5.0 * scaled - square) * 0.25
    fourth = mat_product(factor_square, factor_square)
    tail = mat_product(fourth, factor_scaled)
    return (6.25 * identity - 1.25 * scaled - tail) * (0.25 * frobenius ** (-0.25))


def general_body(replica_grads, owners, left_stats, right_stats):
    width = left_stats.shape[1]
    owner_row = owners[0]
    block_count = owner_row.shape[0]
    replica = lax.axis_index("dp")
    replica_count = lax.axis_size("dp")
    entry_count = width * block_count * width * lax.axis_size("mp")
    share_rows = width // replica_count
    share = lax.psum_scatter(
        replica_grads[0].astype(jnp.float32), "dp", scatter_dimension=0, tiled=True
    )
    squares = lax.psum(jnp.sum(share * share), ("dp", "mp"))
    clip_factor = jnp.minimum(1.0, clip_level / jnp.sqrt(squares / entry_count))
    share_blocks = jnp.transpose(share.reshape(share_rows, block_count, width), (1, 0, 2))
    targets = jnp.arange(replica_count, dtype=jnp.int32)
    routing = (owner_row[None, :] == targets[:, None]).astype(jnp.float32)
    outgoing = jnp.einsum("db,brc->drc", routing, share_blocks, precision=lax.Precision.HIGHEST)
    arrived = lax.all_to_all(outgoing, "dp", split_axis=0, concat_axis=0, tiled=True)
    block = arrived.reshape(width, width) * clip_factor
    update = block_update(block, jnp.sum(block * block), 1.0, left_stats[0], right_stats[0])
    chosen = (owner_row == replica).astype(jnp.float32)
    whole = lax.psum(chosen[:, None, None] * update[None], "dp")
    return jnp.transpose(whole, (1, 0, 2)).reshape(width, block_count * width)


def block_update(block, block_norm, clip_factor, left_prev, right_prev):
    order_size = block.shape[-1]
    stat_scale = clip_factor * clip_factor / order_size
    transposed = block.T
    left = 0.5 * left_prev + mat_product(block, transposed) * stat_scale
    right = 0.5 * right_prev + mat_product(transposed, block) * stat_scale
    pre = mat_product(mat_product(inverse_root(left), block), inverse_root(right)) * clip_factor
    pre_norm = jnp.sum(pre * pre)
    return pre * (clip_factor * jnp.sqrt(block_norm / (pre_norm + graft_eps)))


SMALL = 2 << 20
LARGE = 20 << 20
F32 = jnp.float32
HALVES = (0, 1)


def split(value):
    high = value.astype(jnp.bfloat16)
    return high, (value - high.astype(F32)).astype(jnp.bfloat16)


def left_operand(value):
    high, low = split(value)
    return jnp.concatenate([high, high, low], axis=1)


def right_operand(value):
    high, low = split(value)
    return jnp.concatenate([high, low, high], axis=0)


def triple_dot(left_side, right_side):
    return jnp.dot(left_side, right_side, preferred_element_type=F32)


def mirrored(upper, corner):
    half = corner.shape[0]
    lower = jnp.concatenate([upper[:, half:].T, corner], axis=1)
    return jnp.concatenate([upper, lower], axis=0)


def symmetric_dot(left_side, right_side):
    half = left_side.shape[0] // 2
    upper = triple_dot(left_side[:half], right_side)
    return mirrored(upper, triple_dot(left_side[half:], right_side[:, half:]))


def add_identity(value, amount):
    tile = 128
    rows = lax.broadcasted_iota(jnp.int32, (tile, tile), 0)
    columns = lax.broadcasted_iota(jnp.int32, (tile, tile), 1)
    diagonal = jnp.where(rows == columns, amount, 0.0)
    lines = []
    for i in range(value.shape[0] // tile):
        line = value[i * tile : (i + 1) * tile]
        parts = [line[:, j * tile : (j + 1) * tile] for j in range(value.shape[1] // tile)]
        parts[i] = parts[i] + diagonal
        lines.append(jnp.concatenate(parts, axis=1))
    return jnp.concatenate(lines, axis=0)


def piece_target(kind, device):
    along = 2 + 2 * (device & 1)
    flips = {"self": 0, "straight": along, "side": 6 - along, "corner": 6, "cross": along ^ 1, "diagonal": 7}
    return device ^ flips[kind]


def local_call(kernel, name, out_shape, operands, scalars=(), flops=0, vmem=None, **options):
    whole = pl.BlockSpec(memory_space=pltpu.VMEM)
    arrays = list(operands) + (list(out_shape) if isinstance(out_shape, (list, tuple)) else [out_shape])
    moved = sum(array.size * array.dtype.itemsize for array in arrays)
    return pl.pallas_call(
        kernel,
        in_specs=[pl.BlockSpec(memory_space=pltpu.SMEM)] * len(scalars) + [whole] * len(operands),
        out_specs=jax.tree.map(lambda _: whole, out_shape),
        out_shape=out_shape,
        compiler_params=pltpu.CompilerParams(vmem_limit_bytes=vmem or SMALL),
        cost_estimate=pl.CostEstimate(flops=flops, bytes_accessed=moved, transcendentals=0),
        name=name,
        **options,
    )(*scalars, *operands)


def owner_block(owners_ref, grad_ref, rows, width, target):
    column = 0
    for index in range(1, grad_ref.shape[1] // width):
        column = column + jnp.where(owners_ref[index] == target, index * width, 0)
    columns = pl.ds(pl.multiple_of(column, width), width)
    return grad_ref[rows, columns].astype(F32)


def rows_of(half, width):
    return pl.ds(0, width) if half is None else pl.ds(half * (width // 2), width // 2)


def piece_shape(half, width):
    return jax.ShapeDtypeStruct((width if half is None else width // 2, width), F32)


def piece_of(ref, half, width):
    return ref[rows_of(half, width), :] if ref.shape[0] == width else ref[...]


def pack_call(owners, me, grads, pieces, width):
    def kernel(owners_ref, me_ref, grad_ref, *out_refs):
        for (kind, half), out_ref in zip(pieces, out_refs):
            target = piece_target(kind, me_ref[0] ^ 1)
            out_ref[...] = owner_block(owners_ref, grad_ref, rows_of(half, width), width, target)

    shapes = [piece_shape(half, width) for _, half in pieces]
    return local_call(kernel, "pack", shapes, (grads,), (owners, me))


def add_call(owners, me, grads, kind, half, arrivals, width):
    flat = [value for arrival in arrivals for value in (arrival if isinstance(arrival, list) else [arrival])]

    def kernel(owners_ref, me_ref, grad_ref, *refs):
        target = piece_target(kind, me_ref[0])
        for part in HALVES if half is None else (half,):
            total = owner_block(owners_ref, grad_ref, rows_of(part, width), width, target)
            place = 0
            for arrival in arrivals:
                if isinstance(arrival, list):
                    total = total + refs[place + part][...]
                    place += 2
                else:
                    total = total + piece_of(refs[place], part, width)
                    place += 1
            if half is None:
                refs[-1][rows_of(part, width), :] = total
            else:
                refs[-1][...] = total

    return local_call(kernel, "add", piece_shape(half, width), (grads, *flat), (owners, me))


def join_call(owners, me, total, half, arrival, norm, block_count):
    width = total.shape[1]

    def kernel(owners_ref, me_ref, total_ref, arrival_ref, *refs):
        block_ref, norm_ref = refs[-2:]
        block = piece_of(total_ref, half, width) + arrival_ref[...]
        block_ref[...] = block
        owned = 0
        for index in range(block_count):
            owned = owned + jnp.where(owners_ref[index] == me_ref[0], 1, 0)
        squares = jnp.sum(block * block, keepdims=True).reshape(1, 1) * owned.astype(F32)
        total_squares = jnp.broadcast_to(squares, norm_ref.shape)
        norm_ref[...] = total_squares if norm is None else total_squares + refs[0][...]

    shapes = [piece_shape(half, width), jax.ShapeDtypeStruct((8, 128), F32)]
    operands = (total, arrival) if norm is None else (total, arrival, norm)
    return local_call(kernel, "join", shapes, operands, (owners, me))


def sum_kernel(*refs):
    total = refs[0][...]
    for ref in refs[1:-1]:
        total = total + ref[...]
    refs[-1][...] = total


def sum_call(*tiles):
    return local_call(sum_kernel, "sum", jax.ShapeDtypeStruct(tiles[0].shape, F32), tiles)


def whole_block(block_refs):
    return jnp.concatenate([ref[...] for ref in block_refs], axis=0)


def gram_kernel(upper_ref, lower_ref, left_ref, right_ref):
    high, low = split(whole_block((upper_ref, lower_ref)))
    for axis, out_ref in ((1, left_ref), (0, right_ref)):
        first = jnp.concatenate([high, high, low], axis=axis)
        second = jnp.concatenate([high, low, high], axis=axis)
        half = high.shape[0] // 2
        dims = (((axis,), (axis,)), ((), ()))
        first_upper = first[:half] if axis == 1 else first[:, :half]
        first_lower = first[half:] if axis == 1 else first[:, half:]
        second_lower = second[half:] if axis == 1 else second[:, half:]
        upper = lax.dot_general(first_upper, second, dims, preferred_element_type=F32)
        corner = lax.dot_general(first_lower, second_lower, dims, preferred_element_type=F32)
        out_ref[...] = mirrored(upper, corner)


def gram_call(block):
    width = block[0].shape[1]
    shape = jax.ShapeDtypeStruct((width, width), F32)
    return local_call(gram_kernel, "gram", [shape, shape], block, flops=12 * width**3, vmem=LARGE)


def square_kernel(*refs):
    for ref, out_ref in zip(refs[: len(refs) // 2], refs[len(refs) // 2 :]):
        value = ref[...]
        out_ref[...] = symmetric_dot(left_operand(value), right_operand(value))


def square_call(*statistics):
    shapes = [jax.ShapeDtypeStruct(value.shape, F32) for value in statistics]
    flops = 6 * len(statistics) * statistics[0].shape[0] ** 3
    return local_call(square_kernel, "square", shapes, statistics, flops=flops, vmem=LARGE)


def mix_kernel(previous_ref, gram_ref, mixed_ref, square_ref):
    gram = gram_ref[...]
    gram_right = right_operand(gram)
    product = triple_dot(left_operand(previous_ref[...]), gram_right)
    square_ref[...] = symmetric_dot(left_operand(gram), gram_right)
    mixed_ref[...] = product + product.T


def mix_call(previous, gram):
    shape = jax.ShapeDtypeStruct(gram.shape, F32)
    flops = 12 * gram.shape[0] ** 3
    return local_call(mix_kernel, "mix", [shape, shape], (previous, gram), flops=flops, vmem=LARGE)


def roots_of(sides, gram_scale):
    statistics = [0.5 * previous[...] + gram[...] * gram_scale for previous, gram, _, _, _ in sides]
    norms = [jnp.sum(value * value, keepdims=True).reshape(1, 1) for value in statistics]
    factor_square, factor_scaled, kept = [], [], []
    for statistic, norm, (_, _, previous_square, mixed, gram_square) in zip(statistics, norms, sides):
        inverse = 1.0 / norm
        scaled = statistic * jnp.sqrt(inverse)
        square = previous_square[...] * (0.25 * inverse) + mixed[...] * (0.5 * gram_scale * inverse)
        square = square + gram_square[...] * (gram_scale * gram_scale * inverse)
        factor_square.append(add_identity(0.0625 * square - 0.625 * scaled, 1.5625))
        factor_scaled.append(1.25 * scaled - 0.25 * square)
        kept.append(scaled)
    fourth = [symmetric_dot(left_operand(value), right_operand(value)) for value in factor_square]
    tail = [symmetric_dot(left_operand(f), right_operand(m)) for f, m in zip(fourth, factor_scaled)]
    roots = [add_identity(-1.25 * m - t, 6.25) for m, t in zip(kept, tail)]
    return roots, [0.25 * lax.rsqrt(jnp.sqrt(jnp.sqrt(norm))) for norm in norms]


def update_call(block, block_norm, left, right, norms, entry_count):
    width = block[0].shape[1]

    def kernel(upper_ref, lower_ref, block_norm_ref, *refs):
        left_refs, right_refs, norm_refs, out_refs = refs[:5], refs[5:10], refs[10:-3], refs[-3:]
        squares = sum(ref[:1, :1] for ref in norm_refs)
        clip_factor = jnp.minimum(1.0, clip_level / jnp.sqrt(squares / entry_count))
        gram_scale = clip_factor * clip_factor / width
        roots, scales = roots_of((left_refs, right_refs), gram_scale)
        halfway = triple_dot(left_operand(roots[0]), right_operand(whole_block((upper_ref, lower_ref))))
        pre = triple_dot(left_operand(halfway), right_operand(roots[1]))
        pre_scale = scales[0] * scales[1] * clip_factor
        pre_norm = jnp.sum(pre * pre, keepdims=True).reshape(1, 1) * (pre_scale * pre_scale)
        clipped_norm = block_norm_ref[:1, :1] * (clip_factor * clip_factor)
        update = pre * (pre_scale * jnp.sqrt(clipped_norm / (pre_norm + graft_eps)))
        out_refs[0][...] = update
        for half in HALVES:
            out_refs[1 + half][...] = update[half * (width // 2) : (half + 1) * (width // 2)]

    operands = (*block, block_norm, *left, *right, *norms)
    shapes = [piece_shape(half, width) for half in (None, *HALVES)]
    return local_call(kernel, "update", shapes, operands, flops=36 * width**3, vmem=LARGE)


def assemble_call(owners, me, places, slots, block_count, started):
    width = slots[0].shape[1]

    def kernel(owners_ref, me_ref, *refs):
        out_ref, sem = refs[-2:]
        copies = []
        for number, (kind, flip, half) in enumerate(places):
            target = piece_target(kind, me_ref[0] ^ flip)
            owned, column = 0, 0
            for index in range(block_count):
                matches = owners_ref[index] == target
                owned = owned + jnp.where(matches, 1, 0)
                column = column + jnp.where(matches, index * width, 0)
            columns = pl.ds(pl.multiple_of(column, width), width)
            spot = out_ref.at[rows_of(half, width), columns]
            copies.append((owned, pltpu.make_async_copy(refs[number], spot, sem.at[number])))
        for owned, copy in copies:
            pl.when(owned == 1)(copy.start)
        for owned, copy in copies:
            pl.when(owned == 1)(copy.wait)

    in_specs = [pl.BlockSpec(memory_space=pltpu.SMEM)] * 2
    in_specs += [pl.BlockSpec(memory_space=pltpu.VMEM)] * len(slots)
    operands = [owners, me, *slots]
    aliases = {}
    if started is not None:
        aliases = {len(operands): 0}
        in_specs.append(pl.BlockSpec(memory_space=pltpu.HBM))
        operands.append(started)
    return pl.pallas_call(
        kernel,
        in_specs=in_specs,
        out_specs=pl.BlockSpec(memory_space=pltpu.HBM),
        out_shape=jax.ShapeDtypeStruct((width, block_count * width), F32),
        scratch_shapes=[pltpu.SemaphoreType.DMA((len(slots),))],
        input_output_aliases=aliases,
        compiler_params=pltpu.CompilerParams(vmem_limit_bytes=SMALL),
        cost_estimate=pl.CostEstimate(
            flops=0, bytes_accessed=8 * slots[0].size * len(slots), transcendentals=0
        ),
        name="assemble",
    )(*operands)


def paired_body(replica_grads, owners, left_stats, right_stats):
    width = left_stats.shape[1]
    owner_row = owners[0]
    block_count = owner_row.shape[0]
    me = lax.axis_index("dp").astype(jnp.int32).reshape(1)
    group_count = lax.axis_size("mp")
    entry_count = width * block_count * width * group_count
    grads = replica_grads[0]

    def flipped(mask):
        return [(i, i ^ mask) for i in range(8)]

    def over(pairs, value, label):
        with jax.named_scope(label):
            return lax.ppermute(value, "dp", pairs)

    def to_core(value, label):
        return over(flipped(1), value, "core_" + label)

    def to_link(value, label):
        return over([(i, i ^ (2 + 2 * (i % 2))) for i in range(8)], value, "link_" + label)

    def to_side(value, label):
        return over([(i, i ^ (4 - 2 * (i % 2))) for i in range(8)], value, "side_" + label)

    def own_plus(kind, half, *arrivals):
        return add_call(owner_row, me, grads, kind, half, arrivals, width)

    def assemble(result, *pieces):
        return assemble_call(owner_row, me, *zip(*pieces), block_count, result)

    def after(value, *others):
        return lax.optimization_barrier((value, *others))[0]

    kinds = ("corner", "straight", "side", "self")
    pieces = []
    for pair in (kinds[:2], kinds[2:]):
        pieces += pack_call(owner_row, me, grads, [(kind, half) for kind in pair for half in HALVES], width)
    keys = [(kind, half) for kind in kinds for half in HALVES]
    from_core = {key: to_core(value, key[0]) for key, value in zip(keys, pieces)}
    from_link = {
        key: to_link(own_plus(*key, from_core[key]), key[0]) for key in keys if key[0] in kinds[:2]
    }
    arrived = [
        to_side(own_plus("side", half, from_core["side", half], from_link["corner", half]), "side")
        for half in HALVES
    ]
    totals = [
        own_plus("self", half, from_core["self", half], from_link["straight", half]) for half in HALVES
    ]
    sides = [(left_stats[0],), (right_stats[0],)]
    squares = square_call(*[after(previous, totals[0]) for previous, in sides])
    totals[0] = after(totals[0], *squares)
    norm, block = None, []
    for half in HALVES:
        joined, norm = join_call(owner_row, me, totals[half], half, arrived[half], norm, block_count)
        block.append(joined)
    block_norm = norm
    norm = sum_call(norm, to_core(norm, "norm"))
    def group_over(step, value):
        with jax.named_scope("group_norm"):
            return lax.ppermute(value, "mp", [(i, step(i)) for i in range(group_count)])

    chip_norm = over(flipped(2), norm, "x_norm")
    grams = gram_call([after(block[0], norm), block[1]])
    norm = sum_call(after(norm, grams[0]), chip_norm)
    chip_norm = over(flipped(4), norm, "y_norm")
    sides = [(previous, gram, square) for (previous,), gram, square in zip(sides, grams, squares)]
    sides[0] += tuple(mix_call(sides[0][0], after(sides[0][1], norm)))
    norm = sum_call(after(norm, sides[0][3]), chip_norm)
    if group_count & (group_count - 1) == 0:
        step = 1
        right_gram = sides[1][1]
        while step < group_count:
            other = group_over(lambda i: i ^ step, norm)
            if step == 1:
                sides[1] += tuple(mix_call(sides[1][0], after(right_gram, norm)))
                norm = after(norm, sides[1][3])
            norm = sum_call(norm, other)
            step *= 2
        norms = [norm]
    else:
        norms = [norm]
        for shift in range(1, group_count):
            norms.append(group_over(lambda i: (i + shift) % group_count, norm))
        sides[1] += tuple(mix_call(*sides[1][:2]))
    whole, *own = update_call(block, block_norm, *sides, norms, entry_count)

    core_own = to_core(whole, "own")
    first = [to_link(value, "own") for value in own]
    core_first = [to_core(after(value, core_own), "first") for value in first]
    second = to_link(after(core_own, first[0]), "sibling")
    core_second = to_core(second, "second")
    relayed = [to_link(value, "relayed") for value in core_first]
    held = [(("self", 0, None), whole), (("self", 1, None), core_own)]
    held += [(("straight", 0, half), first[half]) for half in HALVES]
    held += [(("straight", 1, half), core_first[half]) for half in HALVES]
    crossed = [(("cross", 0, None), second), (("cross", 1, None), core_second)]
    result = assemble(None, *held)
    core_relayed = [to_core(after(relayed[0], result), "relayed"), to_core(relayed[1], "relayed")]
    result = assemble(result, *crossed, *[(("diagonal", 0, half), relayed[half]) for half in HALVES], (("diagonal", 1, 0), core_relayed[0]))
    return assemble(result, (("diagonal", 1, 1), core_relayed[1]))


def solution(mesh):
    return jax.shard_map(
        paired_body if mesh.shape["dp"] == 8 else general_body,
        mesh=mesh,
        in_specs=(P("dp", None, "mp"), P("mp", None), P("dp", None, "mp"), P("dp", None, "mp")),
        out_specs=P(None, "mp"),
        check_vma=False,
    )
```

```python
import functools

import jax
import jax.numpy as jnp
from jax import lax
from jax.experimental import pallas as pl
from jax.experimental.pallas import tpu as pltpu
from jax.sharding import PartitionSpec as P

clip_level = 1.0
graft_eps = 1e-06


def mat_product(left_side, right_side):
    return jnp.matmul(left_side, right_side, precision=lax.Precision.HIGH)


def inverse_root(statistic):
    order_size = statistic.shape[-1]
    identity = jnp.eye(order_size, dtype=jnp.float32)
    frobenius = jnp.sqrt(jnp.sum(statistic * statistic))
    scaled = statistic / frobenius
    square = mat_product(scaled, scaled)
    factor_square = (25.0 * identity - 10.0 * scaled + square) * 0.0625
    factor_scaled = (5.0 * scaled - square) * 0.25
    fourth = mat_product(factor_square, factor_square)
    tail = mat_product(fourth, factor_scaled)
    return (6.25 * identity - 1.25 * scaled - tail) * (0.25 * frobenius ** (-0.25))


def general_body(replica_grads, owners, left_stats, right_stats):
    width = left_stats.shape[1]
    owner_row = owners[0]
    block_count = owner_row.shape[0]
    replica = lax.axis_index("dp")
    replica_count = lax.axis_size("dp")
    entry_count = width * block_count * width * lax.axis_size("mp")
    share_rows = width // replica_count
    share = lax.psum_scatter(
        replica_grads[0].astype(jnp.float32), "dp", scatter_dimension=0, tiled=True
    )
    squares = lax.psum(jnp.sum(share * share), ("dp", "mp"))
    clip_factor = jnp.minimum(1.0, clip_level / jnp.sqrt(squares / entry_count))
    share_blocks = jnp.transpose(share.reshape(share_rows, block_count, width), (1, 0, 2))
    targets = jnp.arange(replica_count, dtype=jnp.int32)
    routing = (owner_row[None, :] == targets[:, None]).astype(jnp.float32)
    outgoing = jnp.einsum("db,brc->drc", routing, share_blocks, precision=lax.Precision.HIGHEST)
    arrived = lax.all_to_all(outgoing, "dp", split_axis=0, concat_axis=0, tiled=True)
    block = arrived.reshape(width, width) * clip_factor
    update = block_update(block, jnp.sum(block * block), 1.0, left_stats[0], right_stats[0])
    chosen = (owner_row == replica).astype(jnp.float32)
    whole = lax.psum(chosen[:, None, None] * update[None], "dp")
    return jnp.transpose(whole, (1, 0, 2)).reshape(width, block_count * width)


def block_update(block, block_norm, clip_factor, left_prev, right_prev):
    order_size = block.shape[-1]
    stat_scale = clip_factor * clip_factor / order_size
    transposed = block.T
    left = 0.5 * left_prev + mat_product(block, transposed) * stat_scale
    right = 0.5 * right_prev + mat_product(transposed, block) * stat_scale
    pre = mat_product(mat_product(inverse_root(left), block), inverse_root(right)) * clip_factor
    pre_norm = jnp.sum(pre * pre)
    return pre * (clip_factor * jnp.sqrt(block_norm / (pre_norm + graft_eps)))


SMALL = 2 << 20
LARGE = 20 << 20
F32 = jnp.float32
HALVES = (0, 1)


def split(value):
    high = value.astype(jnp.bfloat16)
    return high, (value - high.astype(F32)).astype(jnp.bfloat16)


def left_operand(value):
    high, low = split(value)
    return jnp.concatenate([high, high, low], axis=1)


def right_operand(value):
    high, low = split(value)
    return jnp.concatenate([high, low, high], axis=0)


def triple_dot(left_side, right_side):
    return jnp.dot(left_side, right_side, preferred_element_type=F32)


def mirrored(upper, corner):
    half = corner.shape[0]
    lower = jnp.concatenate([upper[:, half:].T, corner], axis=1)
    return jnp.concatenate([upper, lower], axis=0)


def symmetric_dot(left_side, right_side):
    half = left_side.shape[0] // 2
    upper = triple_dot(left_side[:half], right_side)
    return mirrored(upper, triple_dot(left_side[half:], right_side[:, half:]))


def add_identity(value, amount):
    tile = 128
    rows = lax.broadcasted_iota(jnp.int32, (tile, tile), 0)
    columns = lax.broadcasted_iota(jnp.int32, (tile, tile), 1)
    diagonal = jnp.where(rows == columns, amount, 0.0)
    lines = []
    for i in range(value.shape[0] // tile):
        line = value[i * tile : (i + 1) * tile]
        parts = [line[:, j * tile : (j + 1) * tile] for j in range(value.shape[1] // tile)]
        parts[i] = parts[i] + diagonal
        lines.append(jnp.concatenate(parts, axis=1))
    return jnp.concatenate(lines, axis=0)


def piece_target(kind, device):
    along = 2 + 2 * (device & 1)
    flips = {"self": 0, "straight": along, "side": 6 - along, "corner": 6, "cross": along ^ 1, "diagonal": 7}
    return device ^ flips[kind]


def local_call(kernel, name, out_shape, operands, scalars=(), flops=0, vmem=None, **options):
    whole = pl.BlockSpec(memory_space=pltpu.VMEM)
    arrays = list(operands) + (list(out_shape) if isinstance(out_shape, (list, tuple)) else [out_shape])
    moved = sum(array.size * array.dtype.itemsize for array in arrays)
    return pl.pallas_call(
        kernel,
        in_specs=[pl.BlockSpec(memory_space=pltpu.SMEM)] * len(scalars) + [whole] * len(operands),
        out_specs=jax.tree.map(lambda _: whole, out_shape),
        out_shape=out_shape,
        compiler_params=pltpu.CompilerParams(vmem_limit_bytes=vmem or SMALL),
        cost_estimate=pl.CostEstimate(flops=flops, bytes_accessed=moved, transcendentals=0),
        name=name,
        **options,
    )(*scalars, *operands)


def owner_block(owners_ref, grad_ref, rows, width, target):
    column = 0
    for index in range(1, grad_ref.shape[1] // width):
        column = column + jnp.where(owners_ref[index] == target, index * width, 0)
    columns = pl.ds(pl.multiple_of(column, width), width)
    return grad_ref[rows, columns].astype(F32)


def rows_of(half, width):
    return pl.ds(0, width) if half is None else pl.ds(half * (width // 2), width // 2)


def piece_shape(half, width):
    return jax.ShapeDtypeStruct((width if half is None else width // 2, width), F32)


def piece_of(ref, half, width):
    return ref[rows_of(half, width), :] if ref.shape[0] == width else ref[...]


def pack_call(owners, me, grads, pieces, width):
    def kernel(owners_ref, me_ref, grad_ref, *out_refs):
        for (kind, half), out_ref in zip(pieces, out_refs):
            target = piece_target(kind, me_ref[0] ^ 1)
            out_ref[...] = owner_block(owners_ref, grad_ref, rows_of(half, width), width, target)

    shapes = [piece_shape(half, width) for _, half in pieces]
    return local_call(kernel, "pack", shapes, (grads,), (owners, me))


def add_call(owners, me, grads, kind, half, arrivals, width):
    flat = [value for arrival in arrivals for value in (arrival if isinstance(arrival, list) else [arrival])]

    def kernel(owners_ref, me_ref, grad_ref, *refs):
        target = piece_target(kind, me_ref[0])
        for part in HALVES if half is None else (half,):
            total = owner_block(owners_ref, grad_ref, rows_of(part, width), width, target)
            place = 0
            for arrival in arrivals:
                if isinstance(arrival, list):
                    total = total + refs[place + part][...]
                    place += 2
                else:
                    total = total + piece_of(refs[place], part, width)
                    place += 1
            if half is None:
                refs[-1][rows_of(part, width), :] = total
            else:
                refs[-1][...] = total

    return local_call(kernel, "add", piece_shape(half, width), (grads, *flat), (owners, me))


def join_call(owners, me, total, half, arrival, norm, block_count):
    width = total.shape[1]

    def kernel(owners_ref, me_ref, total_ref, arrival_ref, *refs):
        block_ref, norm_ref = refs[-2:]
        block = piece_of(total_ref, half, width) + arrival_ref[...]
        block_ref[...] = block
        owned = 0
        for index in range(block_count):
            owned = owned + jnp.where(owners_ref[index] == me_ref[0], 1, 0)
        squares = jnp.sum(block * block, keepdims=True).reshape(1, 1) * owned.astype(F32)
        total_squares = jnp.broadcast_to(squares, norm_ref.shape)
        norm_ref[...] = total_squares if norm is None else total_squares + refs[0][...]

    shapes = [piece_shape(half, width), jax.ShapeDtypeStruct((8, 128), F32)]
    operands = (total, arrival) if norm is None else (total, arrival, norm)
    return local_call(kernel, "join", shapes, operands, (owners, me))


def sum_kernel(*refs):
    total = refs[0][...]
    for ref in refs[1:-1]:
        total = total + ref[...]
    refs[-1][...] = total


def sum_call(*tiles):
    return local_call(sum_kernel, "sum", jax.ShapeDtypeStruct(tiles[0].shape, F32), tiles)


def whole_block(block_refs):
    return jnp.concatenate([ref[...] for ref in block_refs], axis=0)


def gram_kernel(upper_ref, lower_ref, left_ref, right_ref):
    high, low = split(whole_block((upper_ref, lower_ref)))
    for axis, out_ref in ((1, left_ref), (0, right_ref)):
        first = jnp.concatenate([high, high, low], axis=axis)
        second = jnp.concatenate([high, low, high], axis=axis)
        half = high.shape[0] // 2
        dims = (((axis,), (axis,)), ((), ()))
        first_upper = first[:half] if axis == 1 else first[:, :half]
        first_lower = first[half:] if axis == 1 else first[:, half:]
        second_lower = second[half:] if axis == 1 else second[:, half:]
        upper = lax.dot_general(first_upper, second, dims, preferred_element_type=F32)
        corner = lax.dot_general(first_lower, second_lower, dims, preferred_element_type=F32)
        out_ref[...] = mirrored(upper, corner)


def gram_call(block):
    width = block[0].shape[1]
    shape = jax.ShapeDtypeStruct((width, width), F32)
    return local_call(gram_kernel, "gram", [shape, shape], block, flops=12 * width**3, vmem=LARGE)


def square_kernel(*refs):
    for ref, out_ref in zip(refs[: len(refs) // 2], refs[len(refs) // 2 :]):
        value = ref[...]
        out_ref[...] = symmetric_dot(left_operand(value), right_operand(value))


def square_call(*statistics):
    shapes = [jax.ShapeDtypeStruct(value.shape, F32) for value in statistics]
    flops = 6 * len(statistics) * statistics[0].shape[0] ** 3
    return local_call(square_kernel, "square", shapes, statistics, flops=flops, vmem=LARGE)


def mix_kernel(previous_ref, gram_ref, mixed_ref, square_ref):
    gram = gram_ref[...]
    gram_right = right_operand(gram)
    product = triple_dot(left_operand(previous_ref[...]), gram_right)
    square_ref[...] = symmetric_dot(left_operand(gram), gram_right)
    mixed_ref[...] = product + product.T


def mix_call(previous, gram):
    shape = jax.ShapeDtypeStruct(gram.shape, F32)
    flops = 12 * gram.shape[0] ** 3
    return local_call(mix_kernel, "mix", [shape, shape], (previous, gram), flops=flops, vmem=LARGE)


def roots_of(sides, gram_scale):
    statistics = [0.5 * previous[...] + gram[...] * gram_scale for previous, gram, _, _, _ in sides]
    norms = [jnp.sum(value * value, keepdims=True).reshape(1, 1) for value in statistics]
    factor_square, factor_scaled, kept = [], [], []
    for statistic, norm, (_, _, previous_square, mixed, gram_square) in zip(statistics, norms, sides):
        inverse = 1.0 / norm
        scaled = statistic * jnp.sqrt(inverse)
        square = previous_square[...] * (0.25 * inverse) + mixed[...] * (0.5 * gram_scale * inverse)
        square = square + gram_square[...] * (gram_scale * gram_scale * inverse)
        factor_square.append(add_identity(0.0625 * square - 0.625 * scaled, 1.5625))
        factor_scaled.append(1.25 * scaled - 0.25 * square)
        kept.append(scaled)
    fourth = [symmetric_dot(left_operand(value), right_operand(value)) for value in factor_square]
    tail = [symmetric_dot(left_operand(f), right_operand(m)) for f, m in zip(fourth, factor_scaled)]
    roots = [add_identity(-1.25 * m - t, 6.25) for m, t in zip(kept, tail)]
    return roots, [0.25 * lax.rsqrt(jnp.sqrt(jnp.sqrt(norm))) for norm in norms]


def update_call(block, block_norm, left, right, norms, entry_count):
    width = block[0].shape[1]

    def kernel(upper_ref, lower_ref, block_norm_ref, *refs):
        left_refs, right_refs, norm_refs, out_refs = refs[:5], refs[5:10], refs[10:-3], refs[-3:]
        squares = sum(ref[:1, :1] for ref in norm_refs)
        clip_factor = jnp.minimum(1.0, clip_level / jnp.sqrt(squares / entry_count))
        gram_scale = clip_factor * clip_factor / width
        roots, scales = roots_of((left_refs, right_refs), gram_scale)
        halfway = triple_dot(left_operand(roots[0]), right_operand(whole_block((upper_ref, lower_ref))))
        pre = triple_dot(left_operand(halfway), right_operand(roots[1]))
        pre_scale = scales[0] * scales[1] * clip_factor
        pre_norm = jnp.sum(pre * pre, keepdims=True).reshape(1, 1) * (pre_scale * pre_scale)
        clipped_norm = block_norm_ref[:1, :1] * (clip_factor * clip_factor)
        update = pre * (pre_scale * jnp.sqrt(clipped_norm / (pre_norm + graft_eps)))
        out_refs[0][...] = update
        for half in HALVES:
            out_refs[1 + half][...] = update[half * (width // 2) : (half + 1) * (width // 2)]

    operands = (*block, block_norm, *left, *right, *norms)
    shapes = [piece_shape(half, width) for half in (None, *HALVES)]
    return local_call(kernel, "update", shapes, operands, flops=36 * width**3, vmem=LARGE)


def assemble_call(owners, me, places, slots, block_count, started):
    width = slots[0].shape[1]

    def kernel(owners_ref, me_ref, *refs):
        out_ref, sem = refs[-2:]
        copies = []
        for number, (kind, flip, half) in enumerate(places):
            target = piece_target(kind, me_ref[0] ^ flip)
            owned, column = 0, 0
            for index in range(block_count):
                matches = owners_ref[index] == target
                owned = owned + jnp.where(matches, 1, 0)
                column = column + jnp.where(matches, index * width, 0)
            columns = pl.ds(pl.multiple_of(column, width), width)
            spot = out_ref.at[rows_of(half, width), columns]
            copies.append((owned, pltpu.make_async_copy(refs[number], spot, sem.at[number])))
        for owned, copy in copies:
            pl.when(owned == 1)(copy.start)
        for owned, copy in copies:
            pl.when(owned == 1)(copy.wait)

    in_specs = [pl.BlockSpec(memory_space=pltpu.SMEM)] * 2
    in_specs += [pl.BlockSpec(memory_space=pltpu.VMEM)] * len(slots)
    operands = [owners, me, *slots]
    aliases = {}
    if started is not None:
        aliases = {len(operands): 0}
        in_specs.append(pl.BlockSpec(memory_space=pltpu.HBM))
        operands.append(started)
    return pl.pallas_call(
        kernel,
        in_specs=in_specs,
        out_specs=pl.BlockSpec(memory_space=pltpu.HBM),
        out_shape=jax.ShapeDtypeStruct((width, block_count * width), F32),
        scratch_shapes=[pltpu.SemaphoreType.DMA((len(slots),))],
        input_output_aliases=aliases,
        compiler_params=pltpu.CompilerParams(vmem_limit_bytes=SMALL),
        cost_estimate=pl.CostEstimate(
            flops=0, bytes_accessed=8 * slots[0].size * len(slots), transcendentals=0
        ),
        name="assemble",
    )(*operands)


def paired_body(replica_grads, owners, left_stats, right_stats):
    width = left_stats.shape[1]
    owner_row = owners[0]
    block_count = owner_row.shape[0]
    me = lax.axis_index("dp").astype(jnp.int32).reshape(1)
    group_count = lax.axis_size("mp")
    entry_count = width * block_count * width * group_count
    grads = replica_grads[0]

    def flipped(mask):
        return [(i, i ^ mask) for i in range(8)]

    def over(pairs, value, label):
        with jax.named_scope(label):
            return lax.ppermute(value, "dp", pairs)

    def to_core(value, label):
        return over(flipped(1), value, "core_" + label)

    def to_link(value, label):
        return over([(i, i ^ (2 + 2 * (i % 2))) for i in range(8)], value, "link_" + label)

    def to_side(value, label):
        return over([(i, i ^ (4 - 2 * (i % 2))) for i in range(8)], value, "side_" + label)

    def own_plus(kind, half, *arrivals):
        return add_call(owner_row, me, grads, kind, half, arrivals, width)

    def assemble(result, *pieces):
        return assemble_call(owner_row, me, *zip(*pieces), block_count, result)

    def after(value, *others):
        return lax.optimization_barrier((value, *others))[0]

    kinds = ("corner", "straight", "side", "self")
    from_core, sums, from_link = {}, {}, {}

    def exchange(kind, gate):
        pieces = pack_call(owner_row, gate, grads, [(kind, half) for half in HALVES], width)
        for half, value in zip(HALVES, pieces):
            from_core[kind, half] = to_core(value, kind)

    exchange("corner", me)
    exchange("straight", after(me, from_core["corner", 0]))
    for kind in kinds[:2]:
        for half in HALVES:
            sums[kind, half] = own_plus(kind, half, from_core[kind, half])
            from_link[kind, half] = to_link(sums[kind, half], kind)
    exchange("side", after(me, sums["corner", 1]))
    exchange("self", after(me, from_link["corner", 0]))
    arrived = [
        to_side(own_plus("side", half, from_core["side", half], from_link["corner", half]), "side")
        for half in HALVES
    ]
    totals = [
        own_plus("self", half, from_core["self", half], from_link["straight", half]) for half in HALVES
    ]
    sides = [(left_stats[0],), (right_stats[0],)]
    squares = square_call(*[after(previous, totals[0]) for previous, in sides])
    totals[0] = after(totals[0], *squares)
    norm, block = None, []
    for half in HALVES:
        joined, norm = join_call(owner_row, me, totals[half], half, arrived[half], norm, block_count)
        block.append(joined)
    block_norm = norm
    norm = sum_call(norm, to_core(norm, "norm"))
    chip_norms = [over(flipped(mask), norm, "chip_norm") for mask in (2, 4, 6)]
    grams = gram_call([after(block[0], norm), block[1]])
    sides = [(previous, gram, square) for (previous,), gram, square in zip(sides, grams, squares)]
    sides[0] += tuple(mix_call(*sides[0][:2]))
    norm = sum_call(after(norm, sides[0][4]), *chip_norms)
    norms = [norm]
    for shift in range(1, group_count):
        pairs = [(i, (i + shift) % group_count) for i in range(group_count)]
        with jax.named_scope("group_norm"):
            norms.append(lax.ppermute(norm, "mp", pairs))
    sides[1] += tuple(mix_call(*sides[1][:2]))
    whole, *own = update_call(block, block_norm, *sides, norms, entry_count)

    core_own = to_core(whole, "own")
    first = [to_link(value, "own") for value in own]
    core_first = [to_core(after(value, core_own), "first") for value in first]
    second = to_link(after(core_own, first[0]), "sibling")
    core_second = to_core(second, "second")
    relayed = [to_link(value, "relayed") for value in core_first]
    held = [(("self", 0, None), whole), (("self", 1, None), core_own)]
    held += [(("straight", 0, half), first[half]) for half in HALVES]
    held += [(("straight", 1, half), core_first[half]) for half in HALVES]
    crossed = [(("cross", 0, None), second), (("cross", 1, None), core_second)]
    result = assemble(None, *held)
    core_relayed = [to_core(after(relayed[0], result), "relayed"), to_core(relayed[1], "relayed")]
    result = assemble(result, *crossed, *[(("diagonal", 0, half), relayed[half]) for half in HALVES])
    return assemble(result, *[(("diagonal", 1, half), core_relayed[half]) for half in HALVES])


def solution(mesh):
    return jax.shard_map(
        paired_body if mesh.shape["dp"] == 8 else general_body,
        mesh=mesh,
        in_specs=(P("dp", None, "mp"), P("mp", None), P("dp", None, "mp"), P("dp", None, "mp")),
        out_specs=P(None, "mp"),
        check_vma=False,
    )
```

```python
import functools

import jax
import jax.numpy as jnp
from jax import lax
from jax.experimental import pallas as pl
from jax.experimental.pallas import tpu as pltpu
from jax.sharding import PartitionSpec as P

clip_level = 1.0
graft_eps = 1e-06


def mat_product(left_side, right_side):
    return jnp.matmul(left_side, right_side, precision=lax.Precision.HIGH)


def inverse_root(statistic):
    order_size = statistic.shape[-1]
    identity = jnp.eye(order_size, dtype=jnp.float32)
    frobenius = jnp.sqrt(jnp.sum(statistic * statistic))
    scaled = statistic / frobenius
    square = mat_product(scaled, scaled)
    factor_square = (25.0 * identity - 10.0 * scaled + square) * 0.0625
    factor_scaled = (5.0 * scaled - square) * 0.25
    fourth = mat_product(factor_square, factor_square)
    tail = mat_product(fourth, factor_scaled)
    return (6.25 * identity - 1.25 * scaled - tail) * (0.25 * frobenius ** (-0.25))


def general_body(replica_grads, owners, left_stats, right_stats):
    width = left_stats.shape[1]
    owner_row = owners[0]
    block_count = owner_row.shape[0]
    replica = lax.axis_index("dp")
    replica_count = lax.axis_size("dp")
    entry_count = width * block_count * width * lax.axis_size("mp")
    share_rows = width // replica_count
    share = lax.psum_scatter(
        replica_grads[0].astype(jnp.float32), "dp", scatter_dimension=0, tiled=True
    )
    squares = lax.psum(jnp.sum(share * share), ("dp", "mp"))
    clip_factor = jnp.minimum(1.0, clip_level / jnp.sqrt(squares / entry_count))
    share_blocks = jnp.transpose(share.reshape(share_rows, block_count, width), (1, 0, 2))
    targets = jnp.arange(replica_count, dtype=jnp.int32)
    routing = (owner_row[None, :] == targets[:, None]).astype(jnp.float32)
    outgoing = jnp.einsum("db,brc->drc", routing, share_blocks, precision=lax.Precision.HIGHEST)
    arrived = lax.all_to_all(outgoing, "dp", split_axis=0, concat_axis=0, tiled=True)
    block = arrived.reshape(width, width) * clip_factor
    update = block_update(block, jnp.sum(block * block), 1.0, left_stats[0], right_stats[0])
    chosen = (owner_row == replica).astype(jnp.float32)
    whole = lax.psum(chosen[:, None, None] * update[None], "dp")
    return jnp.transpose(whole, (1, 0, 2)).reshape(width, block_count * width)


def block_update(block, block_norm, clip_factor, left_prev, right_prev):
    order_size = block.shape[-1]
    stat_scale = clip_factor * clip_factor / order_size
    transposed = block.T
    left = 0.5 * left_prev + mat_product(block, transposed) * stat_scale
    right = 0.5 * right_prev + mat_product(transposed, block) * stat_scale
    pre = mat_product(mat_product(inverse_root(left), block), inverse_root(right)) * clip_factor
    pre_norm = jnp.sum(pre * pre)
    return pre * (clip_factor * jnp.sqrt(block_norm / (pre_norm + graft_eps)))


SMALL = 2 << 20
LARGE = 20 << 20
F32 = jnp.float32
HALVES = (0, 1)


def split(value):
    high = value.astype(jnp.bfloat16)
    return high, (value - high.astype(F32)).astype(jnp.bfloat16)


def left_operand(value):
    high, low = split(value)
    return jnp.concatenate([high, high, low], axis=1)


def right_operand(value):
    high, low = split(value)
    return jnp.concatenate([high, low, high], axis=0)


def triple_dot(left_side, right_side):
    return jnp.dot(left_side, right_side, preferred_element_type=F32)


def mirrored(upper, corner):
    half = corner.shape[0]
    lower = jnp.concatenate([upper[:, half:].T, corner], axis=1)
    return jnp.concatenate([upper, lower], axis=0)


def symmetric_dot(left_side, right_side):
    half = left_side.shape[0] // 2
    upper = triple_dot(left_side[:half], right_side)
    return mirrored(upper, triple_dot(left_side[half:], right_side[:, half:]))


def add_identity(value, amount):
    tile = 128
    rows = lax.broadcasted_iota(jnp.int32, (tile, tile), 0)
    columns = lax.broadcasted_iota(jnp.int32, (tile, tile), 1)
    diagonal = jnp.where(rows == columns, amount, 0.0)
    lines = []
    for i in range(value.shape[0] // tile):
        line = value[i * tile : (i + 1) * tile]
        parts = [line[:, j * tile : (j + 1) * tile] for j in range(value.shape[1] // tile)]
        parts[i] = parts[i] + diagonal
        lines.append(jnp.concatenate(parts, axis=1))
    return jnp.concatenate(lines, axis=0)


def piece_target(kind, device):
    along = 2 + 2 * (device & 1)
    flips = {"self": 0, "straight": along, "side": 6 - along, "corner": 6, "cross": along ^ 1, "diagonal": 7}
    return device ^ flips[kind]


def local_call(kernel, name, out_shape, operands, scalars=(), flops=0, vmem=None, **options):
    whole = pl.BlockSpec(memory_space=pltpu.VMEM)
    arrays = list(operands) + (list(out_shape) if isinstance(out_shape, (list, tuple)) else [out_shape])
    moved = sum(array.size * array.dtype.itemsize for array in arrays)
    return pl.pallas_call(
        kernel,
        in_specs=[pl.BlockSpec(memory_space=pltpu.SMEM)] * len(scalars) + [whole] * len(operands),
        out_specs=jax.tree.map(lambda _: whole, out_shape),
        out_shape=out_shape,
        compiler_params=pltpu.CompilerParams(vmem_limit_bytes=vmem or SMALL),
        cost_estimate=pl.CostEstimate(flops=flops, bytes_accessed=moved, transcendentals=0),
        name=name,
        **options,
    )(*scalars, *operands)


def owner_block(owners_ref, grad_ref, rows, width, target):
    column = 0
    for index in range(1, grad_ref.shape[1] // width):
        column = column + jnp.where(owners_ref[index] == target, index * width, 0)
    columns = pl.ds(pl.multiple_of(column, width), width)
    return grad_ref[rows, columns].astype(F32)


def rows_of(half, width):
    return pl.ds(0, width) if half is None else pl.ds(half * (width // 2), width // 2)


def piece_shape(half, width):
    return jax.ShapeDtypeStruct((width if half is None else width // 2, width), F32)


def piece_of(ref, half, width):
    return ref[rows_of(half, width), :] if ref.shape[0] == width else ref[...]


def pack_call(owners, me, grads, pieces, width):
    def kernel(owners_ref, me_ref, grad_ref, *out_refs):
        for (kind, half), out_ref in zip(pieces, out_refs):
            target = piece_target(kind, me_ref[0] ^ 1)
            out_ref[...] = owner_block(owners_ref, grad_ref, rows_of(half, width), width, target)

    shapes = [piece_shape(half, width) for _, half in pieces]
    return local_call(kernel, "pack", shapes, (grads,), (owners, me))


def add_call(owners, me, grads, kind, half, arrivals, width):
    flat = [value for arrival in arrivals for value in (arrival if isinstance(arrival, list) else [arrival])]

    def kernel(owners_ref, me_ref, grad_ref, *refs):
        target = piece_target(kind, me_ref[0])
        for part in HALVES if half is None else (half,):
            total = owner_block(owners_ref, grad_ref, rows_of(part, width), width, target)
            place = 0
            for arrival in arrivals:
                if isinstance(arrival, list):
                    total = total + refs[place + part][...]
                    place += 2
                else:
                    total = total + piece_of(refs[place], part, width)
                    place += 1
            if half is None:
                refs[-1][rows_of(part, width), :] = total
            else:
                refs[-1][...] = total

    return local_call(kernel, "add", piece_shape(half, width), (grads, *flat), (owners, me))


def join_call(owners, me, total, half, arrival, norm, block_count):
    width = total.shape[1]

    def kernel(owners_ref, me_ref, total_ref, arrival_ref, *refs):
        block_ref, norm_ref = refs[-2:]
        block = piece_of(total_ref, half, width) + arrival_ref[...]
        block_ref[...] = block
        owned = 0
        for index in range(block_count):
            owned = owned + jnp.where(owners_ref[index] == me_ref[0], 1, 0)
        squares = jnp.sum(block * block, keepdims=True).reshape(1, 1) * owned.astype(F32)
        total_squares = jnp.broadcast_to(squares, norm_ref.shape)
        norm_ref[...] = total_squares if norm is None else total_squares + refs[0][...]

    shapes = [piece_shape(half, width), jax.ShapeDtypeStruct((8, 128), F32)]
    operands = (total, arrival) if norm is None else (total, arrival, norm)
    return local_call(kernel, "join", shapes, operands, (owners, me))


def sum_kernel(*refs):
    total = refs[0][...]
    for ref in refs[1:-1]:
        total = total + ref[...]
    refs[-1][...] = total


def sum_call(*tiles):
    return local_call(sum_kernel, "sum", jax.ShapeDtypeStruct(tiles[0].shape, F32), tiles)


def whole_block(block_refs):
    return jnp.concatenate([ref[...] for ref in block_refs], axis=0)


def gram_kernel(upper_ref, lower_ref, left_ref, right_ref):
    high, low = split(whole_block((upper_ref, lower_ref)))
    for axis, out_ref in ((1, left_ref), (0, right_ref)):
        first = jnp.concatenate([high, high, low], axis=axis)
        second = jnp.concatenate([high, low, high], axis=axis)
        half = high.shape[0] // 2
        dims = (((axis,), (axis,)), ((), ()))
        first_upper = first[:half] if axis == 1 else first[:, :half]
        first_lower = first[half:] if axis == 1 else first[:, half:]
        second_lower = second[half:] if axis == 1 else second[:, half:]
        upper = lax.dot_general(first_upper, second, dims, preferred_element_type=F32)
        corner = lax.dot_general(first_lower, second_lower, dims, preferred_element_type=F32)
        out_ref[...] = mirrored(upper, corner)


def gram_call(block):
    width = block[0].shape[1]
    shape = jax.ShapeDtypeStruct((width, width), F32)
    return local_call(gram_kernel, "gram", [shape, shape], block, flops=12 * width**3, vmem=LARGE)


def square_kernel(*refs):
    for ref, out_ref in zip(refs[: len(refs) // 2], refs[len(refs) // 2 :]):
        value = ref[...]
        out_ref[...] = symmetric_dot(left_operand(value), right_operand(value))


def square_call(*statistics):
    shapes = [jax.ShapeDtypeStruct(value.shape, F32) for value in statistics]
    flops = 6 * len(statistics) * statistics[0].shape[0] ** 3
    return local_call(square_kernel, "square", shapes, statistics, flops=flops, vmem=LARGE)


def mix_kernel(previous_ref, gram_ref, mixed_ref, square_ref):
    gram = gram_ref[...]
    gram_right = right_operand(gram)
    product = triple_dot(left_operand(previous_ref[...]), gram_right)
    square_ref[...] = symmetric_dot(left_operand(gram), gram_right)
    mixed_ref[...] = product + product.T


def mix_call(previous, gram):
    shape = jax.ShapeDtypeStruct(gram.shape, F32)
    flops = 12 * gram.shape[0] ** 3
    return local_call(mix_kernel, "mix", [shape, shape], (previous, gram), flops=flops, vmem=LARGE)


def roots_of(sides, gram_scale):
    statistics = [0.5 * previous[...] + gram[...] * gram_scale for previous, gram, _, _, _ in sides]
    norms = [jnp.sum(value * value, keepdims=True).reshape(1, 1) for value in statistics]
    factor_square, factor_scaled, kept = [], [], []
    for statistic, norm, (_, _, previous_square, mixed, gram_square) in zip(statistics, norms, sides):
        inverse = 1.0 / norm
        scaled = statistic * jnp.sqrt(inverse)
        square = previous_square[...] * (0.25 * inverse) + mixed[...] * (0.5 * gram_scale * inverse)
        square = square + gram_square[...] * (gram_scale * gram_scale * inverse)
        factor_square.append(add_identity(0.0625 * square - 0.625 * scaled, 1.5625))
        factor_scaled.append(1.25 * scaled - 0.25 * square)
        kept.append(scaled)
    fourth = [symmetric_dot(left_operand(value), right_operand(value)) for value in factor_square]
    tail = [symmetric_dot(left_operand(f), right_operand(m)) for f, m in zip(fourth, factor_scaled)]
    roots = [add_identity(-1.25 * m - t, 6.25) for m, t in zip(kept, tail)]
    return roots, [0.25 * lax.rsqrt(jnp.sqrt(jnp.sqrt(norm))) for norm in norms]


def update_call(block, block_norm, left, right, norms, entry_count):
    width = block[0].shape[1]

    def kernel(upper_ref, lower_ref, block_norm_ref, *refs):
        left_refs, right_refs, norm_refs, out_refs = refs[:5], refs[5:10], refs[10:-3], refs[-3:]
        squares = sum(ref[:1, :1] for ref in norm_refs)
        clip_factor = jnp.minimum(1.0, clip_level / jnp.sqrt(squares / entry_count))
        gram_scale = clip_factor * clip_factor / width
        roots, scales = roots_of((left_refs, right_refs), gram_scale)
        halfway = triple_dot(left_operand(roots[0]), right_operand(whole_block((upper_ref, lower_ref))))
        pre = triple_dot(left_operand(halfway), right_operand(roots[1]))
        pre_scale = scales[0] * scales[1] * clip_factor
        pre_norm = jnp.sum(pre * pre, keepdims=True).reshape(1, 1) * (pre_scale * pre_scale)
        clipped_norm = block_norm_ref[:1, :1] * (clip_factor * clip_factor)
        update = pre * (pre_scale * jnp.sqrt(clipped_norm / (pre_norm + graft_eps)))
        out_refs[0][...] = update
        for half in HALVES:
            out_refs[1 + half][...] = update[half * (width // 2) : (half + 1) * (width // 2)]

    operands = (*block, block_norm, *left, *right, *norms)
    shapes = [piece_shape(half, width) for half in (None, *HALVES)]
    return local_call(kernel, "update", shapes, operands, flops=36 * width**3, vmem=LARGE)


def assemble_call(owners, me, places, slots, block_count, started):
    width = slots[0].shape[1]

    def kernel(owners_ref, me_ref, *refs):
        out_ref, sem = refs[-2:]
        copies = []
        for number, (kind, flip, half) in enumerate(places):
            target = piece_target(kind, me_ref[0] ^ flip)
            owned, column = 0, 0
            for index in range(block_count):
                matches = owners_ref[index] == target
                owned = owned + jnp.where(matches, 1, 0)
                column = column + jnp.where(matches, index * width, 0)
            columns = pl.ds(pl.multiple_of(column, width), width)
            spot = out_ref.at[rows_of(half, width), columns]
            copies.append((owned, pltpu.make_async_copy(refs[number], spot, sem.at[number])))
        for owned, copy in copies:
            pl.when(owned == 1)(copy.start)
        for owned, copy in copies:
            pl.when(owned == 1)(copy.wait)

    in_specs = [pl.BlockSpec(memory_space=pltpu.SMEM)] * 2
    in_specs += [pl.BlockSpec(memory_space=pltpu.VMEM)] * len(slots)
    operands = [owners, me, *slots]
    aliases = {}
    if started is not None:
        aliases = {len(operands): 0}
        in_specs.append(pl.BlockSpec(memory_space=pltpu.HBM))
        operands.append(started)
    return pl.pallas_call(
        kernel,
        in_specs=in_specs,
        out_specs=pl.BlockSpec(memory_space=pltpu.HBM),
        out_shape=jax.ShapeDtypeStruct((width, block_count * width), F32),
        scratch_shapes=[pltpu.SemaphoreType.DMA((len(slots),))],
        input_output_aliases=aliases,
        compiler_params=pltpu.CompilerParams(vmem_limit_bytes=SMALL),
        cost_estimate=pl.CostEstimate(
            flops=0, bytes_accessed=8 * slots[0].size * len(slots), transcendentals=0
        ),
        name="assemble",
    )(*operands)


def paired_body(replica_grads, owners, left_stats, right_stats):
    width = left_stats.shape[1]
    owner_row = owners[0]
    block_count = owner_row.shape[0]
    me = lax.axis_index("dp").astype(jnp.int32).reshape(1)
    group_count = lax.axis_size("mp")
    entry_count = width * block_count * width * group_count
    grads = replica_grads[0]

    def flipped(mask):
        return [(i, i ^ mask) for i in range(8)]

    def over(pairs, value, label):
        with jax.named_scope(label):
            return lax.ppermute(value, "dp", pairs)

    def to_core(value, label):
        return over(flipped(1), value, "core_" + label)

    def to_link(value, label):
        return over([(i, i ^ (2 + 2 * (i % 2))) for i in range(8)], value, "link_" + label)

    def to_side(value, label):
        return over([(i, i ^ (4 - 2 * (i % 2))) for i in range(8)], value, "side_" + label)

    def own_plus(kind, half, *arrivals):
        return add_call(owner_row, me, grads, kind, half, arrivals, width)

    def assemble(result, *pieces):
        return assemble_call(owner_row, me, *zip(*pieces), block_count, result)

    def after(value, *others):
        return lax.optimization_barrier((value, *others))[0]

    kinds = ("corner", "straight", "side", "self")
    pieces = []
    for pair in (kinds[:2], kinds[2:]):
        pieces += pack_call(owner_row, me, grads, [(kind, half) for kind in pair for half in HALVES], width)
    keys = [(kind, half) for kind in kinds for half in HALVES]
    from_core = {key: to_core(value, key[0]) for key, value in zip(keys, pieces)}
    from_link = {
        key: to_link(own_plus(*key, from_core[key]), key[0]) for key in keys if key[0] in kinds[:2]
    }
    arrived = [
        to_side(own_plus("side", half, from_core["side", half], from_link["corner", half]), "side")
        for half in HALVES
    ]
    totals = [
        own_plus("self", half, from_core["self", half], from_link["straight", half]) for half in HALVES
    ]
    sides = [(left_stats[0],), (right_stats[0],)]
    squares = square_call(*[after(previous, totals[0]) for previous, in sides])
    totals[0] = after(totals[0], *squares)
    norm, block = None, []
    for half in HALVES:
        joined, norm = join_call(owner_row, me, totals[half], half, arrived[half], norm, block_count)
        block.append(joined)
    block_norm = norm
    norm = sum_call(norm, to_core(norm, "norm"))
    chip_norms = [over(flipped(mask), norm, "chip_norm") for mask in (2, 4, 6)]
    grams = gram_call([after(block[0], norm), block[1]])
    sides = [(previous, gram, square) for (previous,), gram, square in zip(sides, grams, squares)]
    sides[0] += tuple(mix_call(*sides[0][:2]))
    norm = sum_call(after(norm, sides[0][4]), *chip_norms)
    norms = [norm]
    for shift in range(1, group_count):
        both_ways = group_count & (group_count - 1) == 0
        pairs = [(i, i ^ shift if both_ways else (i + shift) % group_count) for i in range(group_count)]
        with jax.named_scope("group_norm"):
            norms.append(lax.ppermute(norm, "mp", pairs))
    sides[1] += tuple(mix_call(*sides[1][:2]))
    whole, *own = update_call(block, block_norm, *sides, norms, entry_count)

    core_own = to_core(whole, "own")
    first = [to_link(value, "own") for value in own]
    core_first = [to_core(after(value, core_own), "first") for value in first]
    second = to_link(after(core_own, first[0]), "sibling")
    core_second = to_core(second, "second")
    relayed = [to_link(value, "relayed") for value in core_first]
    held = [(("self", 0, None), whole), (("self", 1, None), core_own)]
    held += [(("straight", 0, half), first[half]) for half in HALVES]
    held += [(("straight", 1, half), core_first[half]) for half in HALVES]
    crossed = [(("cross", 0, None), second), (("cross", 1, None), core_second)]
    result = assemble(None, *held)
    core_relayed = [to_core(after(relayed[0], result), "relayed"), to_core(relayed[1], "relayed")]
    result = assemble(result, *crossed, *[(("diagonal", 0, half), relayed[half]) for half in HALVES])
    return assemble(result, *[(("diagonal", 1, half), core_relayed[half]) for half in HALVES])


def solution(mesh):
    return jax.shard_map(
        paired_body if mesh.shape["dp"] == 8 else general_body,
        mesh=mesh,
        in_specs=(P("dp", None, "mp"), P("mp", None), P("dp", None, "mp"), P("dp", None, "mp")),
        out_specs=P(None, "mp"),
        check_vma=False,
    )
```

```python
import functools

import jax
import jax.numpy as jnp
from jax import lax
from jax.experimental import pallas as pl
from jax.experimental.pallas import tpu as pltpu
from jax.sharding import PartitionSpec as P

clip_level = 1.0
graft_eps = 1e-06


def mat_product(left_side, right_side):
    return jnp.matmul(left_side, right_side, precision=lax.Precision.HIGH)


def inverse_root(statistic):
    order_size = statistic.shape[-1]
    identity = jnp.eye(order_size, dtype=jnp.float32)
    frobenius = jnp.sqrt(jnp.sum(statistic * statistic))
    scaled = statistic / frobenius
    square = mat_product(scaled, scaled)
    factor_square = (25.0 * identity - 10.0 * scaled + square) * 0.0625
    factor_scaled = (5.0 * scaled - square) * 0.25
    fourth = mat_product(factor_square, factor_square)
    tail = mat_product(fourth, factor_scaled)
    return (6.25 * identity - 1.25 * scaled - tail) * (0.25 * frobenius ** (-0.25))


def general_body(replica_grads, owners, left_stats, right_stats):
    width = left_stats.shape[1]
    owner_row = owners[0]
    block_count = owner_row.shape[0]
    replica = lax.axis_index("dp")
    replica_count = lax.axis_size("dp")
    entry_count = width * block_count * width * lax.axis_size("mp")
    share_rows = width // replica_count
    share = lax.psum_scatter(
        replica_grads[0].astype(jnp.float32), "dp", scatter_dimension=0, tiled=True
    )
    squares = lax.psum(jnp.sum(share * share), ("dp", "mp"))
    clip_factor = jnp.minimum(1.0, clip_level / jnp.sqrt(squares / entry_count))
    share_blocks = jnp.transpose(share.reshape(share_rows, block_count, width), (1, 0, 2))
    targets = jnp.arange(replica_count, dtype=jnp.int32)
    routing = (owner_row[None, :] == targets[:, None]).astype(jnp.float32)
    outgoing = jnp.einsum("db,brc->drc", routing, share_blocks, precision=lax.Precision.HIGHEST)
    arrived = lax.all_to_all(outgoing, "dp", split_axis=0, concat_axis=0, tiled=True)
    block = arrived.reshape(width, width) * clip_factor
    update = block_update(block, jnp.sum(block * block), 1.0, left_stats[0], right_stats[0])
    chosen = (owner_row == replica).astype(jnp.float32)
    whole = lax.psum(chosen[:, None, None] * update[None], "dp")
    return jnp.transpose(whole, (1, 0, 2)).reshape(width, block_count * width)


def block_update(block, block_norm, clip_factor, left_prev, right_prev):
    order_size = block.shape[-1]
    stat_scale = clip_factor * clip_factor / order_size
    transposed = block.T
    left = 0.5 * left_prev + mat_product(block, transposed) * stat_scale
    right = 0.5 * right_prev + mat_product(transposed, block) * stat_scale
    pre = mat_product(mat_product(inverse_root(left), block), inverse_root(right)) * clip_factor
    pre_norm = jnp.sum(pre * pre)
    return pre * (clip_factor * jnp.sqrt(block_norm / (pre_norm + graft_eps)))


SMALL = 2 << 20
LARGE = 20 << 20
F32 = jnp.float32
HALVES = (0, 1)


def split(value):
    high = value.astype(jnp.bfloat16)
    return high, (value - high.astype(F32)).astype(jnp.bfloat16)


def left_operand(value):
    high, low = split(value)
    return jnp.concatenate([high, high, low], axis=1)


def right_operand(value):
    high, low = split(value)
    return jnp.concatenate([high, low, high], axis=0)


def triple_dot(left_side, right_side):
    return jnp.dot(left_side, right_side, preferred_element_type=F32)


def mirrored(upper, corner):
    half = corner.shape[0]
    lower = jnp.concatenate([upper[:, half:].T, corner], axis=1)
    return jnp.concatenate([upper, lower], axis=0)


def symmetric_dot(left_side, right_side):
    half = left_side.shape[0] // 2
    upper = triple_dot(left_side[:half], right_side)
    return mirrored(upper, triple_dot(left_side[half:], right_side[:, half:]))


def add_identity(value, amount):
    tile = 128
    rows = lax.broadcasted_iota(jnp.int32, (tile, tile), 0)
    columns = lax.broadcasted_iota(jnp.int32, (tile, tile), 1)
    diagonal = jnp.where(rows == columns, amount, 0.0)
    lines = []
    for i in range(value.shape[0] // tile):
        line = value[i * tile : (i + 1) * tile]
        parts = [line[:, j * tile : (j + 1) * tile] for j in range(value.shape[1] // tile)]
        parts[i] = parts[i] + diagonal
        lines.append(jnp.concatenate(parts, axis=1))
    return jnp.concatenate(lines, axis=0)


def piece_target(kind, device):
    along = 2 + 2 * (device & 1)
    flips = {"self": 0, "straight": along, "side": 6 - along, "corner": 6, "cross": along ^ 1, "diagonal": 7}
    return device ^ flips[kind]


def local_call(kernel, name, out_shape, operands, scalars=(), flops=0, vmem=None, **options):
    whole = pl.BlockSpec(memory_space=pltpu.VMEM)
    arrays = list(operands) + (list(out_shape) if isinstance(out_shape, (list, tuple)) else [out_shape])
    moved = sum(array.size * array.dtype.itemsize for array in arrays)
    return pl.pallas_call(
        kernel,
        in_specs=[pl.BlockSpec(memory_space=pltpu.SMEM)] * len(scalars) + [whole] * len(operands),
        out_specs=jax.tree.map(lambda _: whole, out_shape),
        out_shape=out_shape,
        compiler_params=pltpu.CompilerParams(vmem_limit_bytes=vmem or SMALL),
        cost_estimate=pl.CostEstimate(flops=flops, bytes_accessed=moved, transcendentals=0),
        name=name,
        **options,
    )(*scalars, *operands)


def owner_block(owners_ref, grad_ref, rows, width, target):
    column = 0
    for index in range(1, grad_ref.shape[1] // width):
        column = column + jnp.where(owners_ref[index] == target, index * width, 0)
    columns = pl.ds(pl.multiple_of(column, width), width)
    return grad_ref[rows, columns].astype(F32)


def rows_of(half, width):
    return pl.ds(0, width) if half is None else pl.ds(half * (width // 2), width // 2)


def piece_shape(half, width):
    return jax.ShapeDtypeStruct((width if half is None else width // 2, width), F32)


def piece_of(ref, half, width):
    return ref[rows_of(half, width), :] if ref.shape[0] == width else ref[...]


def pack_call(owners, me, grads, pieces, width):
    def kernel(owners_ref, me_ref, grad_ref, *out_refs):
        for (kind, half), out_ref in zip(pieces, out_refs):
            target = piece_target(kind, me_ref[0] ^ 1)
            out_ref[...] = owner_block(owners_ref, grad_ref, rows_of(half, width), width, target)

    shapes = [piece_shape(half, width) for _, half in pieces]
    return local_call(kernel, "pack", shapes, (grads,), (owners, me))


def add_call(owners, me, grads, kind, half, arrivals, width):
    flat = [value for arrival in arrivals for value in (arrival if isinstance(arrival, list) else [arrival])]

    def kernel(owners_ref, me_ref, grad_ref, *refs):
        target = piece_target(kind, me_ref[0])
        for part in HALVES if half is None else (half,):
            total = owner_block(owners_ref, grad_ref, rows_of(part, width), width, target)
            place = 0
            for arrival in arrivals:
                if isinstance(arrival, list):
                    total = total + refs[place + part][...]
                    place += 2
                else:
                    total = total + piece_of(refs[place], part, width)
                    place += 1
            if half is None:
                refs[-1][rows_of(part, width), :] = total
            else:
                refs[-1][...] = total

    return local_call(kernel, "add", piece_shape(half, width), (grads, *flat), (owners, me))


def join_call(owners, me, total, half, arrival, norm, block_count):
    width = total.shape[1]

    def kernel(owners_ref, me_ref, total_ref, arrival_ref, *refs):
        block_ref, norm_ref = refs[-2:]
        block = piece_of(total_ref, half, width) + arrival_ref[...]
        block_ref[...] = block
        owned = 0
        for index in range(block_count):
            owned = owned + jnp.where(owners_ref[index] == me_ref[0], 1, 0)
        squares = jnp.sum(block * block, keepdims=True).reshape(1, 1) * owned.astype(F32)
        total_squares = jnp.broadcast_to(squares, norm_ref.shape)
        norm_ref[...] = total_squares if norm is None else total_squares + refs[0][...]

    shapes = [piece_shape(half, width), jax.ShapeDtypeStruct((8, 128), F32)]
    operands = (total, arrival) if norm is None else (total, arrival, norm)
    return local_call(kernel, "join", shapes, operands, (owners, me))


def sum_kernel(*refs):
    total = refs[0][...]
    for ref in refs[1:-1]:
        total = total + ref[...]
    refs[-1][...] = total


def sum_call(*tiles):
    return local_call(sum_kernel, "sum", jax.ShapeDtypeStruct(tiles[0].shape, F32), tiles)


def whole_block(block_refs):
    return jnp.concatenate([ref[...] for ref in block_refs], axis=0)


def gram_kernel(upper_ref, lower_ref, left_ref, right_ref):
    high, low = split(whole_block((upper_ref, lower_ref)))
    for axis, out_ref in ((1, left_ref), (0, right_ref)):
        first = jnp.concatenate([high, high, low], axis=axis)
        second = jnp.concatenate([high, low, high], axis=axis)
        half = high.shape[0] // 2
        dims = (((axis,), (axis,)), ((), ()))
        first_upper = first[:half] if axis == 1 else first[:, :half]
        first_lower = first[half:] if axis == 1 else first[:, half:]
        second_lower = second[half:] if axis == 1 else second[:, half:]
        upper = lax.dot_general(first_upper, second, dims, preferred_element_type=F32)
        corner = lax.dot_general(first_lower, second_lower, dims, preferred_element_type=F32)
        out_ref[...] = mirrored(upper, corner)


def gram_call(block):
    width = block[0].shape[1]
    shape = jax.ShapeDtypeStruct((width, width), F32)
    return local_call(gram_kernel, "gram", [shape, shape], block, flops=12 * width**3, vmem=LARGE)


def square_kernel(*refs):
    for ref, out_ref in zip(refs[: len(refs) // 2], refs[len(refs) // 2 :]):
        value = ref[...]
        out_ref[...] = symmetric_dot(left_operand(value), right_operand(value))


def square_call(*statistics):
    shapes = [jax.ShapeDtypeStruct(value.shape, F32) for value in statistics]
    flops = 6 * len(statistics) * statistics[0].shape[0] ** 3
    return local_call(square_kernel, "square", shapes, statistics, flops=flops, vmem=LARGE)


def mix_kernel(previous_ref, gram_ref, mixed_ref, square_ref):
    gram = gram_ref[...]
    gram_right = right_operand(gram)
    product = triple_dot(left_operand(previous_ref[...]), gram_right)
    square_ref[...] = symmetric_dot(left_operand(gram), gram_right)
    mixed_ref[...] = product + product.T


def mix_call(previous, gram):
    shape = jax.ShapeDtypeStruct(gram.shape, F32)
    flops = 12 * gram.shape[0] ** 3
    return local_call(mix_kernel, "mix", [shape, shape], (previous, gram), flops=flops, vmem=LARGE)


def roots_of(sides, gram_scale):
    statistics = [0.5 * previous[...] + gram[...] * gram_scale for previous, gram, _, _, _ in sides]
    norms = [jnp.sum(value * value, keepdims=True).reshape(1, 1) for value in statistics]
    factor_square, factor_scaled, kept = [], [], []
    for statistic, norm, (_, _, previous_square, mixed, gram_square) in zip(statistics, norms, sides):
        inverse = 1.0 / norm
        scaled = statistic * jnp.sqrt(inverse)
        square = previous_square[...] * (0.25 * inverse) + mixed[...] * (0.5 * gram_scale * inverse)
        square = square + gram_square[...] * (gram_scale * gram_scale * inverse)
        factor_square.append(add_identity(0.0625 * square - 0.625 * scaled, 1.5625))
        factor_scaled.append(1.25 * scaled - 0.25 * square)
        kept.append(scaled)
    fourth = [symmetric_dot(left_operand(value), right_operand(value)) for value in factor_square]
    tail = [symmetric_dot(left_operand(f), right_operand(m)) for f, m in zip(fourth, factor_scaled)]
    roots = [add_identity(-1.25 * m - t, 6.25) for m, t in zip(kept, tail)]
    return roots, [0.25 * lax.rsqrt(jnp.sqrt(jnp.sqrt(norm))) for norm in norms]


def update_call(block, block_norm, left, right, norms, entry_count):
    width = block[0].shape[1]

    def kernel(upper_ref, lower_ref, block_norm_ref, *refs):
        left_refs, right_refs, norm_refs, out_refs = refs[:5], refs[5:10], refs[10:-3], refs[-3:]
        squares = sum(ref[:1, :1] for ref in norm_refs)
        clip_factor = jnp.minimum(1.0, clip_level / jnp.sqrt(squares / entry_count))
        gram_scale = clip_factor * clip_factor / width
        roots, scales = roots_of((left_refs, right_refs), gram_scale)
        halfway = triple_dot(left_operand(roots[0]), right_operand(whole_block((upper_ref, lower_ref))))
        pre = triple_dot(left_operand(halfway), right_operand(roots[1]))
        pre_scale = scales[0] * scales[1] * clip_factor
        pre_norm = jnp.sum(pre * pre, keepdims=True).reshape(1, 1) * (pre_scale * pre_scale)
        clipped_norm = block_norm_ref[:1, :1] * (clip_factor * clip_factor)
        update = pre * (pre_scale * jnp.sqrt(clipped_norm / (pre_norm + graft_eps)))
        out_refs[0][...] = update
        for half in HALVES:
            out_refs[1 + half][...] = update[half * (width // 2) : (half + 1) * (width // 2)]

    operands = (*block, block_norm, *left, *right, *norms)
    shapes = [piece_shape(half, width) for half in (None, *HALVES)]
    return local_call(kernel, "update", shapes, operands, flops=36 * width**3, vmem=LARGE)


def assemble_call(owners, me, places, slots, block_count, started):
    width = slots[0].shape[1]

    def kernel(owners_ref, me_ref, *refs):
        out_ref, sem = refs[-2:]
        copies = []
        for number, (kind, flip, half) in enumerate(places):
            target = piece_target(kind, me_ref[0] ^ flip)
            owned, column = 0, 0
            for index in range(block_count):
                matches = owners_ref[index] == target
                owned = owned + jnp.where(matches, 1, 0)
                column = column + jnp.where(matches, index * width, 0)
            columns = pl.ds(pl.multiple_of(column, width), width)
            spot = out_ref.at[rows_of(half, width), columns]
            copies.append((owned, pltpu.make_async_copy(refs[number], spot, sem.at[number])))
        for owned, copy in copies:
            pl.when(owned == 1)(copy.start)
        for owned, copy in copies:
            pl.when(owned == 1)(copy.wait)

    in_specs = [pl.BlockSpec(memory_space=pltpu.SMEM)] * 2
    in_specs += [pl.BlockSpec(memory_space=pltpu.VMEM)] * len(slots)
    operands = [owners, me, *slots]
    aliases = {}
    if started is not None:
        aliases = {len(operands): 0}
        in_specs.append(pl.BlockSpec(memory_space=pltpu.HBM))
        operands.append(started)
    return pl.pallas_call(
        kernel,
        in_specs=in_specs,
        out_specs=pl.BlockSpec(memory_space=pltpu.HBM),
        out_shape=jax.ShapeDtypeStruct((width, block_count * width), F32),
        scratch_shapes=[pltpu.SemaphoreType.DMA((len(slots),))],
        input_output_aliases=aliases,
        compiler_params=pltpu.CompilerParams(vmem_limit_bytes=SMALL),
        cost_estimate=pl.CostEstimate(
            flops=0, bytes_accessed=8 * slots[0].size * len(slots), transcendentals=0
        ),
        name="assemble",
    )(*operands)


def paired_body(replica_grads, owners, left_stats, right_stats):
    width = left_stats.shape[1]
    owner_row = owners[0]
    block_count = owner_row.shape[0]
    me = lax.axis_index("dp").astype(jnp.int32).reshape(1)
    group_count = lax.axis_size("mp")
    entry_count = width * block_count * width * group_count
    grads = replica_grads[0]

    def flipped(mask):
        return [(i, i ^ mask) for i in range(8)]

    def over(pairs, value, label):
        with jax.named_scope(label):
            return lax.ppermute(value, "dp", pairs)

    def to_core(value, label):
        return over(flipped(1), value, "core_" + label)

    def to_link(value, label):
        return over([(i, i ^ (2 + 2 * (i % 2))) for i in range(8)], value, "link_" + label)

    def to_side(value, label):
        return over([(i, i ^ (4 - 2 * (i % 2))) for i in range(8)], value, "side_" + label)

    def own_plus(kind, half, *arrivals):
        return add_call(owner_row, me, grads, kind, half, arrivals, width)

    def assemble(result, *pieces):
        return assemble_call(owner_row, me, *zip(*pieces), block_count, result)

    def after(value, *others):
        return lax.optimization_barrier((value, *others))[0]

    kinds = ("corner", "straight", "side", "self")
    pieces = []
    for pair in (kinds[:2], kinds[2:]):
        pieces += pack_call(owner_row, me, grads, [(kind, half) for kind in pair for half in HALVES], width)
    keys = [(kind, half) for kind in kinds for half in HALVES]
    from_core = {key: to_core(value, key[0]) for key, value in zip(keys, pieces)}
    from_link = {
        key: to_link(own_plus(*key, from_core[key]), key[0]) for key in keys if key[0] in kinds[:2]
    }
    arrived = [
        to_side(own_plus("side", half, from_core["side", half], from_link["corner", half]), "side")
        for half in HALVES
    ]
    totals = [
        own_plus("self", half, from_core["self", half], from_link["straight", half]) for half in HALVES
    ]
    sides = [(left_stats[0],), (right_stats[0],)]
    squares = square_call(*[after(previous, totals[0]) for previous, in sides])
    totals[0] = after(totals[0], *squares)
    norm, block = None, []
    for half in HALVES:
        joined, norm = join_call(owner_row, me, totals[half], half, arrived[half], norm, block_count)
        block.append(joined)
    block_norm = norm
    norm = sum_call(norm, to_core(norm, "norm"))
    chip_norms = [over(flipped(mask), norm, "chip_norm") for mask in (6, 4, 2)]
    grams = gram_call([after(block[0], norm), block[1]])
    sides = [(previous, gram, square) for (previous,), gram, square in zip(sides, grams, squares)]
    sides[0] += tuple(mix_call(*sides[0][:2]))
    norm = sum_call(after(norm, sides[0][4]), *chip_norms)
    norms = [norm]
    for shift in reversed(range(1, group_count)):
        both_ways = group_count & (group_count - 1) == 0
        pairs = [(i, i ^ shift if both_ways else (i + shift) % group_count) for i in range(group_count)]
        with jax.named_scope("group_norm"):
            norms.append(lax.ppermute(norm, "mp", pairs))
    sides[1] += tuple(mix_call(*sides[1][:2]))
    whole, *own = update_call(block, block_norm, *sides, norms, entry_count)

    core_own = to_core(whole, "own")
    first = [to_link(value, "own") for value in own]
    core_first = [to_core(after(value, core_own), "first") for value in first]
    second = to_link(after(core_own, first[0]), "sibling")
    core_second = to_core(second, "second")
    relayed = [to_link(value, "relayed") for value in core_first]
    held = [(("self", 0, None), whole), (("self", 1, None), core_own)]
    held += [(("straight", 0, half), first[half]) for half in HALVES]
    held += [(("straight", 1, half), core_first[half]) for half in HALVES]
    crossed = [(("cross", 0, None), second), (("cross", 1, None), core_second)]
    result = assemble(None, *held)
    core_relayed = [to_core(after(relayed[0], result), "relayed"), to_core(relayed[1], "relayed")]
    result = assemble(result, *crossed, *[(("diagonal", 0, half), relayed[half]) for half in HALVES])
    return assemble(result, *[(("diagonal", 1, half), core_relayed[half]) for half in HALVES])


def solution(mesh):
    return jax.shard_map(
        paired_body if mesh.shape["dp"] == 8 else general_body,
        mesh=mesh,
        in_specs=(P("dp", None, "mp"), P("mp", None), P("dp", None, "mp"), P("dp", None, "mp")),
        out_specs=P(None, "mp"),
        check_vma=False,
    )
```

```python
import functools

import jax
import jax.numpy as jnp
from jax import lax
from jax.experimental import pallas as pl
from jax.experimental.pallas import tpu as pltpu
from jax.sharding import PartitionSpec as P

clip_level = 1.0
graft_eps = 1e-06


def mat_product(left_side, right_side):
    return jnp.matmul(left_side, right_side, precision=lax.Precision.HIGH)


def inverse_root(statistic):
    order_size = statistic.shape[-1]
    identity = jnp.eye(order_size, dtype=jnp.float32)
    frobenius = jnp.sqrt(jnp.sum(statistic * statistic))
    scaled = statistic / frobenius
    square = mat_product(scaled, scaled)
    factor_square = (25.0 * identity - 10.0 * scaled + square) * 0.0625
    factor_scaled = (5.0 * scaled - square) * 0.25
    fourth = mat_product(factor_square, factor_square)
    tail = mat_product(fourth, factor_scaled)
    return (6.25 * identity - 1.25 * scaled - tail) * (0.25 * frobenius ** (-0.25))


def general_body(replica_grads, owners, left_stats, right_stats):
    width = left_stats.shape[1]
    owner_row = owners[0]
    block_count = owner_row.shape[0]
    replica = lax.axis_index("dp")
    replica_count = lax.axis_size("dp")
    entry_count = width * block_count * width * lax.axis_size("mp")
    share_rows = width // replica_count
    share = lax.psum_scatter(
        replica_grads[0].astype(jnp.float32), "dp", scatter_dimension=0, tiled=True
    )
    squares = lax.psum(jnp.sum(share * share), ("dp", "mp"))
    clip_factor = jnp.minimum(1.0, clip_level / jnp.sqrt(squares / entry_count))
    share_blocks = jnp.transpose(share.reshape(share_rows, block_count, width), (1, 0, 2))
    targets = jnp.arange(replica_count, dtype=jnp.int32)
    routing = (owner_row[None, :] == targets[:, None]).astype(jnp.float32)
    outgoing = jnp.einsum("db,brc->drc", routing, share_blocks, precision=lax.Precision.HIGHEST)
    arrived = lax.all_to_all(outgoing, "dp", split_axis=0, concat_axis=0, tiled=True)
    block = arrived.reshape(width, width) * clip_factor
    update = block_update(block, jnp.sum(block * block), 1.0, left_stats[0], right_stats[0])
    chosen = (owner_row == replica).astype(jnp.float32)
    whole = lax.psum(chosen[:, None, None] * update[None], "dp")
    return jnp.transpose(whole, (1, 0, 2)).reshape(width, block_count * width)


def block_update(block, block_norm, clip_factor, left_prev, right_prev):
    order_size = block.shape[-1]
    stat_scale = clip_factor * clip_factor / order_size
    transposed = block.T
    left = 0.5 * left_prev + mat_product(block, transposed) * stat_scale
    right = 0.5 * right_prev + mat_product(transposed, block) * stat_scale
    pre = mat_product(mat_product(inverse_root(left), block), inverse_root(right)) * clip_factor
    pre_norm = jnp.sum(pre * pre)
    return pre * (clip_factor * jnp.sqrt(block_norm / (pre_norm + graft_eps)))


SMALL = 2 << 20
CHUNK = 32
LARGE = 20 << 20
F32 = jnp.float32
HALVES = (0, 1)


def split(value):
    high = value.astype(jnp.bfloat16)
    return high, (value - high.astype(F32)).astype(jnp.bfloat16)


def left_operand(value):
    high, low = split(value)
    return jnp.concatenate([high, high, low], axis=1)


def right_operand(value):
    high, low = split(value)
    return jnp.concatenate([high, low, high], axis=0)


def triple_dot(left_side, right_side):
    return jnp.dot(left_side, right_side, preferred_element_type=F32)


def mirrored(upper, corner):
    half = corner.shape[0]
    lower = jnp.concatenate([upper[:, half:].T, corner], axis=1)
    return jnp.concatenate([upper, lower], axis=0)


def symmetric_dot(left_side, right_side):
    half = left_side.shape[0] // 2
    upper = triple_dot(left_side[:half], right_side)
    return mirrored(upper, triple_dot(left_side[half:], right_side[:, half:]))


def add_identity(value, amount):
    tile = 128
    rows = lax.broadcasted_iota(jnp.int32, (tile, tile), 0)
    columns = lax.broadcasted_iota(jnp.int32, (tile, tile), 1)
    diagonal = jnp.where(rows == columns, amount, 0.0)
    lines = []
    for i in range(value.shape[0] // tile):
        line = value[i * tile : (i + 1) * tile]
        parts = [line[:, j * tile : (j + 1) * tile] for j in range(value.shape[1] // tile)]
        parts[i] = parts[i] + diagonal
        lines.append(jnp.concatenate(parts, axis=1))
    return jnp.concatenate(lines, axis=0)


def piece_target(kind, device):
    along = 2 + 2 * (device & 1)
    flips = {"self": 0, "straight": along, "side": 6 - along, "corner": 6, "cross": along ^ 1, "diagonal": 7}
    return device ^ flips[kind]


def local_call(kernel, name, out_shape, operands, scalars=(), flops=0, vmem=None, **options):
    whole = pl.BlockSpec(memory_space=pltpu.VMEM)
    arrays = list(operands) + (list(out_shape) if isinstance(out_shape, (list, tuple)) else [out_shape])
    moved = sum(array.size * array.dtype.itemsize for array in arrays)
    return pl.pallas_call(
        kernel,
        in_specs=[pl.BlockSpec(memory_space=pltpu.SMEM)] * len(scalars) + [whole] * len(operands),
        out_specs=jax.tree.map(lambda _: whole, out_shape),
        out_shape=out_shape,
        compiler_params=pltpu.CompilerParams(vmem_limit_bytes=vmem or SMALL),
        cost_estimate=pl.CostEstimate(flops=flops, bytes_accessed=moved, transcendentals=0),
        name=name,
        **options,
    )(*scalars, *operands)


def owner_columns(owners_ref, grad_ref, width, target):
    column = 0
    for index in range(1, grad_ref.shape[1] // width):
        column = column + jnp.where(owners_ref[index] == target, index * width, 0)
    return pl.ds(pl.multiple_of(column, width), width)


def row_chunks(half, width):
    first = 0 if half is None else half * (width // 2)
    count = width if half is None else width // 2
    return [(pl.ds(first + row, CHUNK), pl.ds(row, CHUNK)) for row in range(0, count, CHUNK)]


def rows_of(half, width):
    return pl.ds(0, width) if half is None else pl.ds(half * (width // 2), width // 2)


def piece_shape(half, width):
    return jax.ShapeDtypeStruct((width if half is None else width // 2, width), F32)


def pack_call(owners, me, grads, pieces, width):
    def kernel(owners_ref, me_ref, grad_ref, *out_refs):
        for (kind, half), out_ref in zip(pieces, out_refs):
            columns = owner_columns(owners_ref, grad_ref, width, piece_target(kind, me_ref[0] ^ 1))
            for block_rows, piece_rows in row_chunks(half, width):
                out_ref[piece_rows, :] = grad_ref[block_rows, columns].astype(F32)

    shapes = [piece_shape(half, width) for _, half in pieces]
    return local_call(kernel, "pack", shapes, (grads,), (owners, me))


def add_call(owners, me, grads, kind, half, arrivals, width):
    def kernel(owners_ref, me_ref, grad_ref, *refs):
        columns = owner_columns(owners_ref, grad_ref, width, piece_target(kind, me_ref[0]))
        for block_rows, piece_rows in row_chunks(half, width):
            total = grad_ref[block_rows, columns].astype(F32)
            for ref in refs[:-1]:
                total = total + ref[piece_rows, :]
            refs[-1][piece_rows, :] = total

    return local_call(kernel, "add", piece_shape(half, width), (grads, *arrivals), (owners, me))


def join_call(owners, me, total, arrival, norm, block_count):
    rows, width = total.shape

    def kernel(owners_ref, me_ref, total_ref, arrival_ref, *refs):
        block_ref, norm_ref = refs[-2:]
        squares = jnp.zeros((8, width), F32)
        for row in range(0, rows, CHUNK):
            block = total_ref[row : row + CHUNK, :] + arrival_ref[row : row + CHUNK, :]
            block_ref[row : row + CHUNK, :] = block
            squares = squares + jnp.sum((block * block).reshape(CHUNK // 8, 8, width), axis=0)
        owned = 0
        for index in range(block_count):
            owned = owned + jnp.where(owners_ref[index] == me_ref[0], 1, 0)
        squares = jnp.sum(squares, keepdims=True).reshape(1, 1) * owned.astype(F32)
        total_squares = jnp.broadcast_to(squares, norm_ref.shape)
        norm_ref[...] = total_squares if norm is None else total_squares + refs[0][...]

    shapes = [jax.ShapeDtypeStruct((rows, width), F32), jax.ShapeDtypeStruct((8, 128), F32)]
    operands = (total, arrival) if norm is None else (total, arrival, norm)
    return local_call(kernel, "join", shapes, operands, (owners, me))


def sum_kernel(*refs):
    total = refs[0][...]
    for ref in refs[1:-1]:
        total = total + ref[...]
    refs[-1][...] = total


def sum_call(*tiles):
    return local_call(sum_kernel, "sum", jax.ShapeDtypeStruct(tiles[0].shape, F32), tiles)


def whole_block(block_refs):
    return jnp.concatenate([ref[...] for ref in block_refs], axis=0)


def gram_kernel(upper_ref, lower_ref, left_ref, right_ref):
    high, low = split(whole_block((upper_ref, lower_ref)))
    for axis, out_ref in ((1, left_ref), (0, right_ref)):
        first = jnp.concatenate([high, high, low], axis=axis)
        second = jnp.concatenate([high, low, high], axis=axis)
        half = high.shape[0] // 2
        dims = (((axis,), (axis,)), ((), ()))
        first_upper = first[:half] if axis == 1 else first[:, :half]
        first_lower = first[half:] if axis == 1 else first[:, half:]
        second_lower = second[half:] if axis == 1 else second[:, half:]
        upper = lax.dot_general(first_upper, second, dims, preferred_element_type=F32)
        corner = lax.dot_general(first_lower, second_lower, dims, preferred_element_type=F32)
        out_ref[...] = mirrored(upper, corner)


def gram_call(block):
    width = block[0].shape[1]
    shape = jax.ShapeDtypeStruct((width, width), F32)
    return local_call(gram_kernel, "gram", [shape, shape], block, flops=12 * width**3, vmem=LARGE)


def square_kernel(value_ref, out_ref):
    value = value_ref[...]
    out_ref[...] = symmetric_dot(left_operand(value), right_operand(value))


def square_call(value):
    shape = jax.ShapeDtypeStruct(value.shape, F32)
    return local_call(square_kernel, "square", shape, (value,), flops=6 * value.shape[0] ** 3, vmem=LARGE)


def mix_kernel(previous_ref, gram_ref, mixed_ref, square_ref):
    gram = gram_ref[...]
    gram_right = right_operand(gram)
    product = triple_dot(left_operand(previous_ref[...]), gram_right)
    square_ref[...] = symmetric_dot(left_operand(gram), gram_right)
    mixed_ref[...] = product + product.T


def mix_call(previous, gram):
    shape = jax.ShapeDtypeStruct(gram.shape, F32)
    flops = 12 * gram.shape[0] ** 3
    return local_call(mix_kernel, "mix", [shape, shape], (previous, gram), flops=flops, vmem=LARGE)


def roots_of(left, right, gram_scale):
    statistics = [0.5 * side[0][...] + side[1][...] * gram_scale for side in (left, right)]
    norms = [jnp.sum(value * value, keepdims=True).reshape(1, 1) for value in statistics]
    inverses = [1.0 / norm for norm in norms]
    scaled = [value * jnp.sqrt(inverse) for value, inverse in zip(statistics, inverses)]
    left_square = symmetric_dot(left_operand(scaled[0]), right_operand(scaled[0]))
    right_square = right[2][...] * (0.25 * inverses[1]) + right[3][...] * (0.5 * gram_scale * inverses[1])
    right_square = right_square + right[4][...] * (gram_scale * gram_scale * inverses[1])
    square = (left_square, right_square)
    factor_square = [add_identity(0.0625 * q - 0.625 * m, 1.5625) for q, m in zip(square, scaled)]
    factor_scaled = [1.25 * m - 0.25 * q for q, m in zip(square, scaled)]
    fourth, tail = [None, None], [None, None]
    for side in (1, 0):
        fourth[side] = symmetric_dot(left_operand(factor_square[side]), right_operand(factor_square[side]))
    for side in (1, 0):
        tail[side] = symmetric_dot(left_operand(fourth[side]), right_operand(factor_scaled[side]))
    roots = [add_identity(-1.25 * m - t, 6.25) for m, t in zip(scaled, tail)]
    return roots, [0.25 * lax.rsqrt(jnp.sqrt(jnp.sqrt(norm))) for norm in norms]


def update_call(block, block_norm, left, right, norms, entry_count):
    width = block[0].shape[1]

    def kernel(upper_ref, lower_ref, block_norm_ref, *refs):
        left_refs, right_refs, norm_refs, out_refs = refs[:2], refs[2:7], refs[7:-3], refs[-3:]
        squares = sum(ref[:1, :1] for ref in norm_refs)
        clip_factor = jnp.minimum(1.0, clip_level / jnp.sqrt(squares / entry_count))
        gram_scale = clip_factor * clip_factor / width
        roots, scales = roots_of(left_refs, right_refs, gram_scale)
        halfway = triple_dot(left_operand(roots[0]), right_operand(whole_block((upper_ref, lower_ref))))
        pre = triple_dot(left_operand(halfway), right_operand(roots[1]))
        pre_scale = scales[0] * scales[1] * clip_factor
        pre_norm = jnp.sum(pre * pre, keepdims=True).reshape(1, 1) * (pre_scale * pre_scale)
        clipped_norm = block_norm_ref[:1, :1] * (clip_factor * clip_factor)
        update = pre * (pre_scale * jnp.sqrt(clipped_norm / (pre_norm + graft_eps)))
        out_refs[0][...] = update
        for half in HALVES:
            out_refs[1 + half][...] = update[half * (width // 2) : (half + 1) * (width // 2)]

    operands = (*block, block_norm, *left, *right, *norms)
    shapes = [piece_shape(half, width) for half in (None, *HALVES)]
    return local_call(kernel, "update", shapes, operands, flops=36 * width**3, vmem=LARGE)


def assemble_call(owners, me, places, slots, block_count, started):
    width = slots[0].shape[1]

    def kernel(owners_ref, me_ref, *refs):
        out_ref, sem = refs[-2:]
        copies = []
        for number, (kind, flip, half) in enumerate(places):
            target = piece_target(kind, me_ref[0] ^ flip)
            owned, column = 0, 0
            for index in range(block_count):
                matches = owners_ref[index] == target
                owned = owned + jnp.where(matches, 1, 0)
                column = column + jnp.where(matches, index * width, 0)
            columns = pl.ds(pl.multiple_of(column, width), width)
            spot = out_ref.at[rows_of(half, width), columns]
            copies.append((owned, pltpu.make_async_copy(refs[number], spot, sem.at[number])))
        for owned, copy in copies:
            pl.when(owned == 1)(copy.start)
        for owned, copy in copies:
            pl.when(owned == 1)(copy.wait)

    in_specs = [pl.BlockSpec(memory_space=pltpu.SMEM)] * 2
    in_specs += [pl.BlockSpec(memory_space=pltpu.VMEM)] * len(slots)
    operands = [owners, me, *slots]
    aliases = {}
    if started is not None:
        aliases = {len(operands): 0}
        in_specs.append(pl.BlockSpec(memory_space=pltpu.HBM))
        operands.append(started)
    return pl.pallas_call(
        kernel,
        in_specs=in_specs,
        out_specs=pl.BlockSpec(memory_space=pltpu.HBM),
        out_shape=jax.ShapeDtypeStruct((width, block_count * width), F32),
        scratch_shapes=[pltpu.SemaphoreType.DMA((len(slots),))],
        input_output_aliases=aliases,
        compiler_params=pltpu.CompilerParams(vmem_limit_bytes=SMALL),
        cost_estimate=pl.CostEstimate(
            flops=0, bytes_accessed=8 * slots[0].size * len(slots), transcendentals=0
        ),
        name="assemble",
    )(*operands)


def paired_body(replica_grads, owners, left_stats, right_stats):
    width = left_stats.shape[1]
    owner_row = owners[0]
    block_count = owner_row.shape[0]
    me = lax.axis_index("dp").astype(jnp.int32).reshape(1)
    group_count = lax.axis_size("mp")
    entry_count = width * block_count * width * group_count
    grads = replica_grads[0]

    def flipped(mask):
        return [(i, i ^ mask) for i in range(8)]

    def over(pairs, value, label):
        with jax.named_scope(label):
            return lax.ppermute(value, "dp", pairs)

    def to_core(value, label):
        return over(flipped(1), value, "core_" + label)

    def to_link(value, label):
        return over([(i, i ^ (2 + 2 * (i % 2))) for i in range(8)], value, "link_" + label)

    def to_side(value, label):
        return over([(i, i ^ (4 - 2 * (i % 2))) for i in range(8)], value, "side_" + label)

    def own_plus(kind, half, *arrivals):
        return add_call(owner_row, me, grads, kind, half, arrivals, width)

    def assemble(result, *pieces):
        return assemble_call(owner_row, me, *zip(*pieces), block_count, result)

    def after(value, *others):
        return lax.optimization_barrier((value, *others))[0]

    kinds = ("corner", "straight", "side", "self")
    pieces = []
    for pair in (kinds[:2], kinds[2:]):
        pieces += pack_call(owner_row, me, grads, [(kind, half) for kind in pair for half in HALVES], width)
    keys = [(kind, half) for kind in kinds for half in HALVES]
    from_core = {key: to_core(value, key[0]) for key, value in zip(keys, pieces)}
    from_link = {
        key: to_link(own_plus(*key, from_core[key]), key[0]) for key in keys if key[0] in kinds[:2]
    }
    arrived = [
        to_side(own_plus("side", half, from_core["side", half], from_link["corner", half]), "side")
        for half in HALVES
    ]
    totals = [
        own_plus("self", half, from_core["self", half], from_link["straight", half]) for half in HALVES
    ]
    right_square = square_call(after(right_stats[0], totals[0]))
    totals[0] = after(totals[0], right_square)
    norm, block = None, []
    for half in HALVES:
        joined, norm = join_call(owner_row, me, totals[half], arrived[half], norm, block_count)
        block.append(joined)
    block_norm = norm
    norm = sum_call(norm, to_core(norm, "norm"))
    chip_norms = [over(flipped(mask), norm, "chip_norm") for mask in (6, 4, 2)]
    grams = gram_call([after(block[0], norm), block[1]])
    norm = sum_call(after(norm, grams[0]), *chip_norms)
    norms = [norm]
    for shift in reversed(range(1, group_count)):
        both_ways = group_count & (group_count - 1) == 0
        pairs = [(i, i ^ shift if both_ways else (i + shift) % group_count) for i in range(group_count)]
        with jax.named_scope("group_norm"):
            norms.append(lax.ppermute(norm, "mp", pairs))
    left = (left_stats[0], grams[0])
    right = (right_stats[0], grams[1], right_square, *mix_call(right_stats[0], grams[1]))
    whole, *own = update_call(block, block_norm, left, right, norms, entry_count)

    core_own = to_core(whole, "own")
    first = [to_link(value, "own") for value in own]
    core_first = [to_core(after(value, core_own), "first") for value in first]
    second = to_link(after(core_own, first[0]), "sibling")
    core_second = to_core(second, "second")
    relayed = [to_link(value, "relayed") for value in core_first]
    held = [(("self", 0, None), whole), (("self", 1, None), core_own)]
    held += [(("straight", 0, half), first[half]) for half in HALVES]
    held += [(("straight", 1, half), core_first[half]) for half in HALVES]
    crossed = [(("cross", 0, None), second), (("cross", 1, None), core_second)]
    result = assemble(None, *held)
    core_relayed = [to_core(after(relayed[0], result), "relayed"), to_core(relayed[1], "relayed")]
    result = assemble(result, *crossed, *[(("diagonal", 0, half), relayed[half]) for half in HALVES])
    return assemble(result, *[(("diagonal", 1, half), core_relayed[half]) for half in HALVES])


def solution(mesh):
    return jax.shard_map(
        paired_body if mesh.shape["dp"] == 8 else general_body,
        mesh=mesh,
        in_specs=(P("dp", None, "mp"), P("mp", None), P("dp", None, "mp"), P("dp", None, "mp")),
        out_specs=P(None, "mp"),
        check_vma=False,
    )
```

```python
import functools

import jax
import jax.numpy as jnp
from jax import lax
from jax.experimental import pallas as pl
from jax.experimental.pallas import tpu as pltpu
from jax.sharding import PartitionSpec as P

clip_level = 1.0
graft_eps = 1e-06


def mat_product(left_side, right_side):
    return jnp.matmul(left_side, right_side, precision=lax.Precision.HIGH)


def inverse_root(statistic):
    order_size = statistic.shape[-1]
    identity = jnp.eye(order_size, dtype=jnp.float32)
    frobenius = jnp.sqrt(jnp.sum(statistic * statistic))
    scaled = statistic / frobenius
    square = mat_product(scaled, scaled)
    factor_square = (25.0 * identity - 10.0 * scaled + square) * 0.0625
    factor_scaled = (5.0 * scaled - square) * 0.25
    fourth = mat_product(factor_square, factor_square)
    tail = mat_product(fourth, factor_scaled)
    return (6.25 * identity - 1.25 * scaled - tail) * (0.25 * frobenius ** (-0.25))


def general_body(replica_grads, owners, left_stats, right_stats):
    width = left_stats.shape[1]
    owner_row = owners[0]
    block_count = owner_row.shape[0]
    replica = lax.axis_index("dp")
    replica_count = lax.axis_size("dp")
    entry_count = width * block_count * width * lax.axis_size("mp")
    share_rows = width // replica_count
    share = lax.psum_scatter(
        replica_grads[0].astype(jnp.float32), "dp", scatter_dimension=0, tiled=True
    )
    squares = lax.psum(jnp.sum(share * share), ("dp", "mp"))
    clip_factor = jnp.minimum(1.0, clip_level / jnp.sqrt(squares / entry_count))
    share_blocks = jnp.transpose(share.reshape(share_rows, block_count, width), (1, 0, 2))
    targets = jnp.arange(replica_count, dtype=jnp.int32)
    routing = (owner_row[None, :] == targets[:, None]).astype(jnp.float32)
    outgoing = jnp.einsum("db,brc->drc", routing, share_blocks, precision=lax.Precision.HIGHEST)
    arrived = lax.all_to_all(outgoing, "dp", split_axis=0, concat_axis=0, tiled=True)
    block = arrived.reshape(width, width) * clip_factor
    update = block_update(block, jnp.sum(block * block), 1.0, left_stats[0], right_stats[0])
    chosen = (owner_row == replica).astype(jnp.float32)
    whole = lax.psum(chosen[:, None, None] * update[None], "dp")
    return jnp.transpose(whole, (1, 0, 2)).reshape(width, block_count * width)


def block_update(block, block_norm, clip_factor, left_prev, right_prev):
    order_size = block.shape[-1]
    stat_scale = clip_factor * clip_factor / order_size
    transposed = block.T
    left = 0.5 * left_prev + mat_product(block, transposed) * stat_scale
    right = 0.5 * right_prev + mat_product(transposed, block) * stat_scale
    pre = mat_product(mat_product(inverse_root(left), block), inverse_root(right)) * clip_factor
    pre_norm = jnp.sum(pre * pre)
    return pre * (clip_factor * jnp.sqrt(block_norm / (pre_norm + graft_eps)))


SMALL = 2 << 20
CHUNK = 32
LARGE = 20 << 20
F32 = jnp.float32
HALVES = (0, 1)


def split(value):
    high = value.astype(jnp.bfloat16)
    return high, (value - high.astype(F32)).astype(jnp.bfloat16)


def left_operand(value):
    high, low = split(value)
    return jnp.concatenate([high, high, low], axis=1)


def right_operand(value):
    high, low = split(value)
    return jnp.concatenate([high, low, high], axis=0)


def triple_dot(left_side, right_side):
    return jnp.dot(left_side, right_side, preferred_element_type=F32)


def mirrored(upper, corner):
    half = corner.shape[0]
    lower = jnp.concatenate([upper[:, half:].T, corner], axis=1)
    return jnp.concatenate([upper, lower], axis=0)


def symmetric_dot(left_side, right_side):
    half = left_side.shape[0] // 2
    upper = triple_dot(left_side[:half], right_side)
    return mirrored(upper, triple_dot(left_side[half:], right_side[:, half:]))


def add_identity(value, amount):
    tile = 128
    rows = lax.broadcasted_iota(jnp.int32, (tile, tile), 0)
    columns = lax.broadcasted_iota(jnp.int32, (tile, tile), 1)
    diagonal = jnp.where(rows == columns, amount, 0.0)
    lines = []
    for i in range(value.shape[0] // tile):
        line = value[i * tile : (i + 1) * tile]
        parts = [line[:, j * tile : (j + 1) * tile] for j in range(value.shape[1] // tile)]
        parts[i] = parts[i] + diagonal
        lines.append(jnp.concatenate(parts, axis=1))
    return jnp.concatenate(lines, axis=0)


def piece_target(kind, device):
    along = 2 + 2 * (device & 1)
    flips = {"self": 0, "straight": along, "side": 6 - along, "corner": 6, "cross": along ^ 1, "diagonal": 7}
    return device ^ flips[kind]


def local_call(kernel, name, out_shape, operands, scalars=(), flops=0, vmem=None, **options):
    whole = pl.BlockSpec(memory_space=pltpu.VMEM)
    arrays = list(operands) + (list(out_shape) if isinstance(out_shape, (list, tuple)) else [out_shape])
    moved = sum(array.size * array.dtype.itemsize for array in arrays)
    return pl.pallas_call(
        kernel,
        in_specs=[pl.BlockSpec(memory_space=pltpu.SMEM)] * len(scalars) + [whole] * len(operands),
        out_specs=jax.tree.map(lambda _: whole, out_shape),
        out_shape=out_shape,
        compiler_params=pltpu.CompilerParams(vmem_limit_bytes=vmem or SMALL),
        cost_estimate=pl.CostEstimate(flops=flops, bytes_accessed=moved, transcendentals=0),
        name=name,
        **options,
    )(*scalars, *operands)


def owner_columns(places_ref, grad_ref, width, target):
    column = 0
    for index in range(1, grad_ref.shape[1] // width):
        column = column + jnp.where(places_ref[index] == target, index * width, 0)
    return pl.ds(pl.multiple_of(column, width), width)


def row_chunks(half, width):
    first = 0 if half is None else half * (width // 2)
    count = width if half is None else width // 2
    return [(pl.ds(first + row, CHUNK), pl.ds(row, CHUNK)) for row in range(0, count, CHUNK)]


def rows_of(half, width):
    return pl.ds(0, width) if half is None else pl.ds(half * (width // 2), width // 2)


def piece_shape(half, width):
    return jax.ShapeDtypeStruct((width if half is None else width // 2, width), F32)


def pack_call(places, grads, pieces, width, with_owned=False):
    block_count = grads.shape[1] // width

    def kernel(places_ref, grad_ref, *out_refs):
        me = places_ref[block_count]
        for (kind, flip, half), out_ref in zip(pieces, out_refs):
            columns = owner_columns(places_ref, grad_ref, width, piece_target(kind, me ^ flip))
            for block_rows, piece_rows in row_chunks(half, width):
                out_ref[piece_rows, :] = grad_ref[block_rows, columns].astype(F32)
        if with_owned:
            owned = 0
            for index in range(block_count):
                owned = owned + jnp.where(places_ref[index] == me, 1, 0)
            out_refs[-1][...] = jnp.full((8, 128), owned.astype(F32))

    shapes = [piece_shape(half, width) for _, _, half in pieces]
    if with_owned:
        shapes.append(jax.ShapeDtypeStruct((8, 128), F32))
    return local_call(kernel, "pack", shapes, (grads,), (places,))


def add_kernel(*refs):
    for row in range(0, refs[-1].shape[0], CHUNK):
        total = refs[0][row : row + CHUNK, :]
        for ref in refs[1:-1]:
            total = total + ref[row : row + CHUNK, :]
        refs[-1][row : row + CHUNK, :] = total


def add_call(*pieces):
    return local_call(add_kernel, "add", jax.ShapeDtypeStruct(pieces[0].shape, F32), pieces)


def join_call(total, arrival, owned, norm):
    rows, width = total.shape

    def kernel(total_ref, arrival_ref, owned_ref, *refs):
        block_ref, norm_ref = refs[-2:]
        squares = jnp.zeros((8, width), F32)
        for row in range(0, rows, CHUNK):
            block = total_ref[row : row + CHUNK, :] + arrival_ref[row : row + CHUNK, :]
            block_ref[row : row + CHUNK, :] = block
            squares = squares + jnp.sum((block * block).reshape(CHUNK // 8, 8, width), axis=0)
        squares = jnp.sum(squares, keepdims=True).reshape(1, 1)
        total_squares = squares * owned_ref[...]
        norm_ref[...] = total_squares if norm is None else total_squares + refs[0][...]

    shapes = [jax.ShapeDtypeStruct((rows, width), F32), jax.ShapeDtypeStruct((8, 128), F32)]
    operands = (total, arrival, owned) if norm is None else (total, arrival, owned, norm)
    return local_call(kernel, "join", shapes, operands)


def sum_kernel(*refs):
    total = refs[0][...]
    for ref in refs[1:-1]:
        total = total + ref[...]
    refs[-1][...] = total


def sum_call(*tiles):
    return local_call(sum_kernel, "sum", jax.ShapeDtypeStruct(tiles[0].shape, F32), tiles)


def whole_block(block_refs):
    return jnp.concatenate([ref[...] for ref in block_refs], axis=0)


def gram_kernel(upper_ref, lower_ref, left_ref, right_ref):
    high, low = split(whole_block((upper_ref, lower_ref)))
    for axis, out_ref in ((1, left_ref), (0, right_ref)):
        first = jnp.concatenate([high, high, low], axis=axis)
        second = jnp.concatenate([high, low, high], axis=axis)
        half = high.shape[0] // 2
        dims = (((axis,), (axis,)), ((), ()))
        first_upper = first[:half] if axis == 1 else first[:, :half]
        first_lower = first[half:] if axis == 1 else first[:, half:]
        second_lower = second[half:] if axis == 1 else second[:, half:]
        upper = lax.dot_general(first_upper, second, dims, preferred_element_type=F32)
        corner = lax.dot_general(first_lower, second_lower, dims, preferred_element_type=F32)
        out_ref[...] = mirrored(upper, corner)


def gram_call(block):
    width = block[0].shape[1]
    shape = jax.ShapeDtypeStruct((width, width), F32)
    return local_call(gram_kernel, "gram", [shape, shape], block, flops=12 * width**3, vmem=LARGE)


def square_kernel(*refs):
    for ref, out_ref in zip(refs[: len(refs) // 2], refs[len(refs) // 2 :]):
        value = ref[...]
        out_ref[...] = symmetric_dot(left_operand(value), right_operand(value))


def square_call(*statistics):
    shapes = [jax.ShapeDtypeStruct(value.shape, F32) for value in statistics]
    flops = 6 * len(statistics) * statistics[0].shape[0] ** 3
    return local_call(square_kernel, "square", shapes, statistics, flops=flops, vmem=LARGE)


def mix_kernel(previous_ref, gram_ref, mixed_ref, square_ref):
    gram = gram_ref[...]
    gram_right = right_operand(gram)
    product = triple_dot(left_operand(previous_ref[...]), gram_right)
    square_ref[...] = symmetric_dot(left_operand(gram), gram_right)
    mixed_ref[...] = product + product.T


def mix_call(previous, gram):
    shape = jax.ShapeDtypeStruct(gram.shape, F32)
    flops = 12 * gram.shape[0] ** 3
    return local_call(mix_kernel, "mix", [shape, shape], (previous, gram), flops=flops, vmem=LARGE)


def roots_of(sides, gram_scale):
    statistics = [0.5 * previous[...] + gram[...] * gram_scale for previous, gram, _, _, _ in sides]
    norms = [jnp.sum(value * value, keepdims=True).reshape(1, 1) for value in statistics]
    factor_square, factor_scaled, kept = [], [], []
    for statistic, norm, (_, _, previous_square, mixed, gram_square) in zip(statistics, norms, sides):
        inverse = 1.0 / norm
        scaled = statistic * jnp.sqrt(inverse)
        square = previous_square[...] * (0.25 * inverse) + mixed[...] * (0.5 * gram_scale * inverse)
        square = square + gram_square[...] * (gram_scale * gram_scale * inverse)
        factor_square.append(add_identity(0.0625 * square - 0.625 * scaled, 1.5625))
        factor_scaled.append(1.25 * scaled - 0.25 * square)
        kept.append(scaled)
    fourth = [symmetric_dot(left_operand(value), right_operand(value)) for value in factor_square]
    tail = [symmetric_dot(left_operand(f), right_operand(m)) for f, m in zip(fourth, factor_scaled)]
    roots = [add_identity(-1.25 * m - t, 6.25) for m, t in zip(kept, tail)]
    return roots, [0.25 * lax.rsqrt(jnp.sqrt(jnp.sqrt(norm))) for norm in norms]


def update_call(block, block_norm, left, right, norms, entry_count):
    width = block[0].shape[1]

    def kernel(upper_ref, lower_ref, block_norm_ref, *refs):
        left_refs, right_refs, norm_refs, out_refs = refs[:5], refs[5:10], refs[10:-3], refs[-3:]
        squares = sum(ref[:1, :1] for ref in norm_refs)
        clip_factor = jnp.minimum(1.0, clip_level / jnp.sqrt(squares / entry_count))
        gram_scale = clip_factor * clip_factor / width
        roots, scales = roots_of((left_refs, right_refs), gram_scale)
        halfway = triple_dot(left_operand(roots[0]), right_operand(whole_block((upper_ref, lower_ref))))
        pre = triple_dot(left_operand(halfway), right_operand(roots[1]))
        pre_scale = scales[0] * scales[1] * clip_factor
        pre_norm = jnp.sum(pre * pre, keepdims=True).reshape(1, 1) * (pre_scale * pre_scale)
        clipped_norm = block_norm_ref[:1, :1] * (clip_factor * clip_factor)
        update = pre * (pre_scale * jnp.sqrt(clipped_norm / (pre_norm + graft_eps)))
        out_refs[0][...] = update
        for half in HALVES:
            out_refs[1 + half][...] = update[half * (width // 2) : (half + 1) * (width // 2)]

    operands = (*block, block_norm, *left, *right, *norms)
    shapes = [piece_shape(half, width) for half in (None, *HALVES)]
    return local_call(kernel, "update", shapes, operands, flops=36 * width**3, vmem=LARGE)


def assemble_call(places, sources, slots, block_count, started):
    width = slots[0].shape[1]

    def kernel(places_ref, *refs):
        out_ref, sem = refs[-2:]
        copies = []
        for number, (kind, flip, half) in enumerate(sources):
            target = piece_target(kind, places_ref[block_count] ^ flip)
            owned, column = 0, 0
            for index in range(block_count):
                matches = places_ref[index] == target
                owned = owned + jnp.where(matches, 1, 0)
                column = column + jnp.where(matches, index * width, 0)
            columns = pl.ds(pl.multiple_of(column, width), width)
            spot = out_ref.at[rows_of(half, width), columns]
            copies.append((owned, pltpu.make_async_copy(refs[number], spot, sem.at[number])))
        for owned, copy in copies:
            pl.when(owned == 1)(copy.start)
        for owned, copy in copies:
            pl.when(owned == 1)(copy.wait)

    in_specs = [pl.BlockSpec(memory_space=pltpu.SMEM)]
    in_specs += [pl.BlockSpec(memory_space=pltpu.VMEM)] * len(slots)
    operands = [places, *slots]
    aliases = {}
    if started is not None:
        aliases = {len(operands): 0}
        in_specs.append(pl.BlockSpec(memory_space=pltpu.HBM))
        operands.append(started)
    return pl.pallas_call(
        kernel,
        in_specs=in_specs,
        out_specs=pl.BlockSpec(memory_space=pltpu.HBM),
        out_shape=jax.ShapeDtypeStruct((width, block_count * width), F32),
        scratch_shapes=[pltpu.SemaphoreType.DMA((len(slots),))],
        input_output_aliases=aliases,
        compiler_params=pltpu.CompilerParams(vmem_limit_bytes=SMALL),
        cost_estimate=pl.CostEstimate(
            flops=0, bytes_accessed=8 * slots[0].size * len(slots), transcendentals=0
        ),
        name="assemble",
    )(*operands)


def paired_body(replica_grads, owners, left_stats, right_stats):
    width = left_stats.shape[1]
    owner_row = owners[0]
    block_count = owner_row.shape[0]
    places = jnp.concatenate([owner_row, lax.axis_index("dp").astype(jnp.int32).reshape(1)])
    group_count = lax.axis_size("mp")
    entry_count = width * block_count * width * group_count
    grads = replica_grads[0]

    def flipped(mask):
        return [(i, i ^ mask) for i in range(8)]

    def over(pairs, value, label):
        with jax.named_scope(label):
            return lax.ppermute(value, "dp", pairs)

    def to_core(value, label):
        return over(flipped(1), value, "core_" + label)

    def to_link(value, label):
        return over([(i, i ^ (2 + 2 * (i % 2))) for i in range(8)], value, "link_" + label)

    def to_side(value, label):
        return over([(i, i ^ (4 - 2 * (i % 2))) for i in range(8)], value, "side_" + label)

    def assemble(result, *pieces):
        return assemble_call(places, *zip(*pieces), block_count, result)

    def after(value, *others):
        return lax.optimization_barrier((value, *others))[0]

    kinds = ("corner", "straight", "side", "self")
    keys = [(kind, half) for kind in kinds for half in HALVES]

    def cut(gate, for_other, for_own, **options):
        pieces = [(kind, 1, half) for kind, half in for_other] + [(kind, 0, half) for kind, half in for_own]
        return pack_call(gate, grads, pieces, width, **options)

    *pieces, own_first, own_second = cut(places, keys[:4], keys[:2])
    pieces += cut(places, keys[4:], [])
    from_core = {key: to_core(value, key[0]) for key, value in zip(keys, pieces)}
    sums = [add_call(own_first, from_core[keys[0]]), add_call(own_second, from_core[keys[1]])]
    *own, owned = cut(after(places, sums[1]), [], keys[2:], with_owned=True)
    own = dict(zip(keys[2:], own))
    sums += [add_call(own[key], from_core[key]) for key in keys[2:4]]
    from_link = {key: to_link(value, key[0]) for key, value in zip(keys[:4], sums)}
    arrived = [
        to_side(add_call(own["side", half], from_core["side", half], from_link["corner", half]), "side")
        for half in HALVES
    ]
    totals = [add_call(own["self", half], from_core["self", half], from_link["straight", half]) for half in HALVES]
    sides = [(left_stats[0],), (right_stats[0],)]
    squares = square_call(*[after(previous, totals[0]) for previous, in sides])
    totals[0] = after(totals[0], *squares)
    norm, block = None, []
    for half in HALVES:
        joined, norm = join_call(totals[half], arrived[half], owned, norm)
        block.append(joined)
    block_norm = norm
    norm = sum_call(norm, to_core(norm, "norm"))
    chip_norms = [over(flipped(mask), norm, "chip_norm") for mask in (6, 4, 2)]
    grams = gram_call([after(block[0], norm), block[1]])
    sides = [(previous, gram, square) for (previous,), gram, square in zip(sides, grams, squares)]
    sides[0] += tuple(mix_call(*sides[0][:2]))
    norm = sum_call(after(norm, sides[0][4]), *chip_norms)
    norms = [norm]
    for shift in reversed(range(1, group_count)):
        both_ways = group_count & (group_count - 1) == 0
        pairs = [(i, i ^ shift if both_ways else (i + shift) % group_count) for i in range(group_count)]
        with jax.named_scope("group_norm"):
            norms.append(lax.ppermute(norm, "mp", pairs))
    sides[1] += tuple(mix_call(*sides[1][:2]))
    whole, *own = update_call(block, block_norm, *sides, norms, entry_count)

    core_own = to_core(whole, "own")
    first = [to_link(value, "own") for value in own]
    core_first = [to_core(after(value, core_own), "first") for value in first]
    second = to_link(after(core_own, first[0]), "sibling")
    core_second = to_core(second, "second")
    relayed = [to_link(value, "relayed") for value in core_first]
    held = [(("self", 0, None), whole), (("self", 1, None), core_own)]
    held += [(("straight", 0, half), first[half]) for half in HALVES]
    held += [(("straight", 1, half), core_first[half]) for half in HALVES]
    crossed = [(("cross", 0, None), second), (("cross", 1, None), core_second)]
    result = assemble(None, *held)
    core_relayed = [to_core(after(relayed[0], result), "relayed"), to_core(relayed[1], "relayed")]
    result = assemble(result, *crossed, *[(("diagonal", 0, half), relayed[half]) for half in HALVES])
    return assemble(result, *[(("diagonal", 1, half), core_relayed[half]) for half in HALVES])


def solution(mesh):
    return jax.shard_map(
        paired_body if mesh.shape["dp"] == 8 else general_body,
        mesh=mesh,
        in_specs=(P("dp", None, "mp"), P("mp", None), P("dp", None, "mp"), P("dp", None, "mp")),
        out_specs=P(None, "mp"),
        check_vma=False,
    )
```

```python
import functools

import jax
import jax.numpy as jnp
from jax import lax
from jax.experimental import pallas as pl
from jax.experimental.pallas import tpu as pltpu
from jax.sharding import PartitionSpec as P

clip_level = 1.0
graft_eps = 1e-06


def mat_product(left_side, right_side):
    return jnp.matmul(left_side, right_side, precision=lax.Precision.HIGH)


def inverse_root(statistic):
    order_size = statistic.shape[-1]
    identity = jnp.eye(order_size, dtype=jnp.float32)
    frobenius = jnp.sqrt(jnp.sum(statistic * statistic))
    scaled = statistic / frobenius
    square = mat_product(scaled, scaled)
    factor_square = (25.0 * identity - 10.0 * scaled + square) * 0.0625
    factor_scaled = (5.0 * scaled - square) * 0.25
    fourth = mat_product(factor_square, factor_square)
    tail = mat_product(fourth, factor_scaled)
    return (6.25 * identity - 1.25 * scaled - tail) * (0.25 * frobenius ** (-0.25))


def general_body(replica_grads, owners, left_stats, right_stats):
    width = left_stats.shape[1]
    owner_row = owners[0]
    block_count = owner_row.shape[0]
    replica = lax.axis_index("dp")
    replica_count = lax.axis_size("dp")
    entry_count = width * block_count * width * lax.axis_size("mp")
    share_rows = width // replica_count
    share = lax.psum_scatter(
        replica_grads[0].astype(jnp.float32), "dp", scatter_dimension=0, tiled=True
    )
    squares = lax.psum(jnp.sum(share * share), ("dp", "mp"))
    clip_factor = jnp.minimum(1.0, clip_level / jnp.sqrt(squares / entry_count))
    share_blocks = jnp.transpose(share.reshape(share_rows, block_count, width), (1, 0, 2))
    targets = jnp.arange(replica_count, dtype=jnp.int32)
    routing = (owner_row[None, :] == targets[:, None]).astype(jnp.float32)
    outgoing = jnp.einsum("db,brc->drc", routing, share_blocks, precision=lax.Precision.HIGHEST)
    arrived = lax.all_to_all(outgoing, "dp", split_axis=0, concat_axis=0, tiled=True)
    block = arrived.reshape(width, width) * clip_factor
    update = block_update(block, jnp.sum(block * block), 1.0, left_stats[0], right_stats[0])
    chosen = (owner_row == replica).astype(jnp.float32)
    whole = lax.psum(chosen[:, None, None] * update[None], "dp")
    return jnp.transpose(whole, (1, 0, 2)).reshape(width, block_count * width)


def block_update(block, block_norm, clip_factor, left_prev, right_prev):
    order_size = block.shape[-1]
    stat_scale = clip_factor * clip_factor / order_size
    transposed = block.T
    left = 0.5 * left_prev + mat_product(block, transposed) * stat_scale
    right = 0.5 * right_prev + mat_product(transposed, block) * stat_scale
    pre = mat_product(mat_product(inverse_root(left), block), inverse_root(right)) * clip_factor
    pre_norm = jnp.sum(pre * pre)
    return pre * (clip_factor * jnp.sqrt(block_norm / (pre_norm + graft_eps)))


SMALL = 2 << 20
CHUNK = 32
LARGE = 20 << 20
F32 = jnp.float32
HALVES = (0, 1)


def split(value):
    high = value.astype(jnp.bfloat16)
    return high, (value - high.astype(F32)).astype(jnp.bfloat16)


def left_operand(value):
    high, low = split(value)
    return jnp.concatenate([high, high, low], axis=1)


def right_operand(value):
    high, low = split(value)
    return jnp.concatenate([high, low, high], axis=0)


def triple_dot(left_side, right_side):
    return jnp.dot(left_side, right_side, preferred_element_type=F32)


def mirrored(upper, corner):
    half = corner.shape[0]
    lower = jnp.concatenate([upper[:, half:].T, corner], axis=1)
    return jnp.concatenate([upper, lower], axis=0)


def symmetric_dot(left_side, right_side):
    half = left_side.shape[0] // 2
    upper = triple_dot(left_side[:half], right_side)
    return mirrored(upper, triple_dot(left_side[half:], right_side[:, half:]))


def add_identity(value, amount):
    tile = 128
    rows = lax.broadcasted_iota(jnp.int32, (tile, tile), 0)
    columns = lax.broadcasted_iota(jnp.int32, (tile, tile), 1)
    diagonal = jnp.where(rows == columns, amount, 0.0)
    lines = []
    for i in range(value.shape[0] // tile):
        line = value[i * tile : (i + 1) * tile]
        parts = [line[:, j * tile : (j + 1) * tile] for j in range(value.shape[1] // tile)]
        parts[i] = parts[i] + diagonal
        lines.append(jnp.concatenate(parts, axis=1))
    return jnp.concatenate(lines, axis=0)


def piece_target(kind, device):
    along = 2 + 2 * (device & 1)
    flips = {"self": 0, "straight": along, "side": 6 - along, "corner": 6, "cross": along ^ 1, "diagonal": 7}
    return device ^ flips[kind]


def local_call(kernel, name, out_shape, operands, scalars=(), flops=0, vmem=None, **options):
    whole = pl.BlockSpec(memory_space=pltpu.VMEM)
    arrays = list(operands) + (list(out_shape) if isinstance(out_shape, (list, tuple)) else [out_shape])
    moved = sum(array.size * array.dtype.itemsize for array in arrays)
    return pl.pallas_call(
        kernel,
        in_specs=[pl.BlockSpec(memory_space=pltpu.SMEM)] * len(scalars) + [whole] * len(operands),
        out_specs=jax.tree.map(lambda _: whole, out_shape),
        out_shape=out_shape,
        compiler_params=pltpu.CompilerParams(vmem_limit_bytes=vmem or SMALL),
        cost_estimate=pl.CostEstimate(flops=flops, bytes_accessed=moved, transcendentals=0),
        name=name,
        **options,
    )(*scalars, *operands)


def owner_columns(places_ref, grad_ref, width, target):
    column = 0
    for index in range(1, grad_ref.shape[1] // width):
        column = column + jnp.where(places_ref[index] == target, index * width, 0)
    return pl.ds(pl.multiple_of(column, width), width)


def row_chunks(half, width):
    first = 0 if half is None else half * (width // 2)
    count = width if half is None else width // 2
    return [(pl.ds(first + row, CHUNK), pl.ds(row, CHUNK)) for row in range(0, count, CHUNK)]


def rows_of(half, width):
    return pl.ds(0, width) if half is None else pl.ds(half * (width // 2), width // 2)


def piece_shape(half, width):
    return jax.ShapeDtypeStruct((width if half is None else width // 2, width), F32)


def pack_call(places, grads, pieces, width, with_owned=False):
    block_count = grads.shape[1] // width

    def kernel(places_ref, grad_ref, *out_refs):
        me = places_ref[block_count]
        for (kind, flip, half), out_ref in zip(pieces, out_refs):
            columns = owner_columns(places_ref, grad_ref, width, piece_target(kind, me ^ flip))
            for block_rows, piece_rows in row_chunks(half, width):
                out_ref[piece_rows, :] = grad_ref[block_rows, columns].astype(F32)
        if with_owned:
            owned = 0
            for index in range(block_count):
                owned = owned + jnp.where(places_ref[index] == me, 1, 0)
            out_refs[-1][...] = jnp.full((8, 128), owned.astype(F32))

    shapes = [piece_shape(half, width) for _, _, half in pieces]
    if with_owned:
        shapes.append(jax.ShapeDtypeStruct((8, 128), F32))
    return local_call(kernel, "pack", shapes, (grads,), (places,))


def add_kernel(*refs):
    for row in range(0, refs[-1].shape[0], CHUNK):
        total = refs[0][row : row + CHUNK, :]
        for ref in refs[1:-1]:
            total = total + ref[row : row + CHUNK, :]
        refs[-1][row : row + CHUNK, :] = total


def add_call(*pieces):
    return local_call(add_kernel, "add", jax.ShapeDtypeStruct(pieces[0].shape, F32), pieces)


def join_call(total, arrival, owned, norm):
    rows, width = total.shape

    def kernel(total_ref, arrival_ref, owned_ref, *refs):
        block_ref, norm_ref = refs[-2:]
        squares = jnp.zeros((8, width), F32)
        for row in range(0, rows, CHUNK):
            block = total_ref[row : row + CHUNK, :] + arrival_ref[row : row + CHUNK, :]
            block_ref[row : row + CHUNK, :] = block
            squares = squares + jnp.sum((block * block).reshape(CHUNK // 8, 8, width), axis=0)
        squares = jnp.sum(squares, keepdims=True).reshape(1, 1)
        total_squares = squares * owned_ref[...]
        norm_ref[...] = total_squares if norm is None else total_squares + refs[0][...]

    shapes = [jax.ShapeDtypeStruct((rows, width), F32), jax.ShapeDtypeStruct((8, 128), F32)]
    operands = (total, arrival, owned) if norm is None else (total, arrival, owned, norm)
    return local_call(kernel, "join", shapes, operands)


def sum_kernel(*refs):
    total = refs[0][...]
    for ref in refs[1:-1]:
        total = total + ref[...]
    refs[-1][...] = total


def sum_call(*tiles):
    return local_call(sum_kernel, "sum", jax.ShapeDtypeStruct(tiles[0].shape, F32), tiles)


def whole_block(block_refs):
    return jnp.concatenate([ref[...] for ref in block_refs], axis=0)


def gram_kernel(upper_ref, lower_ref, left_ref, right_ref):
    high, low = split(whole_block((upper_ref, lower_ref)))
    for axis, out_ref in ((1, left_ref), (0, right_ref)):
        first = jnp.concatenate([high, high, low], axis=axis)
        second = jnp.concatenate([high, low, high], axis=axis)
        half = high.shape[0] // 2
        dims = (((axis,), (axis,)), ((), ()))
        first_upper = first[:half] if axis == 1 else first[:, :half]
        first_lower = first[half:] if axis == 1 else first[:, half:]
        second_lower = second[half:] if axis == 1 else second[:, half:]
        upper = lax.dot_general(first_upper, second, dims, preferred_element_type=F32)
        corner = lax.dot_general(first_lower, second_lower, dims, preferred_element_type=F32)
        out_ref[...] = mirrored(upper, corner)


def gram_call(block):
    width = block[0].shape[1]
    shape = jax.ShapeDtypeStruct((width, width), F32)
    return local_call(gram_kernel, "gram", [shape, shape], block, flops=12 * width**3, vmem=LARGE)


def square_kernel(*refs):
    for ref, out_ref in zip(refs[: len(refs) // 2], refs[len(refs) // 2 :]):
        value = ref[...]
        out_ref[...] = symmetric_dot(left_operand(value), right_operand(value))


def square_call(*statistics):
    shapes = [jax.ShapeDtypeStruct(value.shape, F32) for value in statistics]
    flops = 6 * len(statistics) * statistics[0].shape[0] ** 3
    return local_call(square_kernel, "square", shapes, statistics, flops=flops, vmem=LARGE)


def mix_kernel(previous_ref, gram_ref, mixed_ref, square_ref):
    gram = gram_ref[...]
    gram_right = right_operand(gram)
    product = triple_dot(left_operand(previous_ref[...]), gram_right)
    square_ref[...] = symmetric_dot(left_operand(gram), gram_right)
    mixed_ref[...] = product + product.T


def mix_call(previous, gram):
    shape = jax.ShapeDtypeStruct(gram.shape, F32)
    flops = 12 * gram.shape[0] ** 3
    return local_call(mix_kernel, "mix", [shape, shape], (previous, gram), flops=flops, vmem=LARGE)


def roots_of(sides, gram_scale):
    statistics = [0.5 * previous[...] + gram[...] * gram_scale for previous, gram, _, _, _ in sides]
    norms = [jnp.sum(value * value, keepdims=True).reshape(1, 1) for value in statistics]
    factor_square, factor_scaled, kept = [], [], []
    for statistic, norm, (_, _, previous_square, mixed, gram_square) in zip(statistics, norms, sides):
        inverse = 1.0 / norm
        scaled = statistic * jnp.sqrt(inverse)
        square = previous_square[...] * (0.25 * inverse) + mixed[...] * (0.5 * gram_scale * inverse)
        square = square + gram_square[...] * (gram_scale * gram_scale * inverse)
        factor_square.append(add_identity(0.0625 * square - 0.625 * scaled, 1.5625))
        factor_scaled.append(1.25 * scaled - 0.25 * square)
        kept.append(scaled)
    fourth = [symmetric_dot(left_operand(value), right_operand(value)) for value in factor_square]
    tail = [symmetric_dot(left_operand(f), right_operand(m)) for f, m in zip(fourth, factor_scaled)]
    roots = [add_identity(-1.25 * m - t, 6.25) for m, t in zip(kept, tail)]
    return roots, [0.25 * lax.rsqrt(jnp.sqrt(jnp.sqrt(norm))) for norm in norms]


def update_call(block, block_norm, left, right, norms, entry_count):
    width = block[0].shape[1]

    def kernel(upper_ref, lower_ref, block_norm_ref, *refs):
        left_refs, right_refs, norm_refs, out_refs = refs[:5], refs[5:10], refs[10:-3], refs[-3:]
        squares = sum(ref[:1, :1] for ref in norm_refs)
        clip_factor = jnp.minimum(1.0, clip_level / jnp.sqrt(squares / entry_count))
        gram_scale = clip_factor * clip_factor / width
        roots, scales = roots_of((left_refs, right_refs), gram_scale)
        halfway = triple_dot(left_operand(roots[0]), right_operand(whole_block((upper_ref, lower_ref))))
        pre = triple_dot(left_operand(halfway), right_operand(roots[1]))
        pre_scale = scales[0] * scales[1] * clip_factor
        pre_norm = jnp.sum(pre * pre, keepdims=True).reshape(1, 1) * (pre_scale * pre_scale)
        clipped_norm = block_norm_ref[:1, :1] * (clip_factor * clip_factor)
        update = pre * (pre_scale * jnp.sqrt(clipped_norm / (pre_norm + graft_eps)))
        out_refs[0][...] = update
        for half in HALVES:
            out_refs[1 + half][...] = update[half * (width // 2) : (half + 1) * (width // 2)]

    operands = (*block, block_norm, *left, *right, *norms)
    shapes = [piece_shape(half, width) for half in (None, *HALVES)]
    return local_call(kernel, "update", shapes, operands, flops=36 * width**3, vmem=LARGE)


def assemble_call(places, sources, slots, block_count, started):
    width = slots[0].shape[1]

    def kernel(places_ref, *refs):
        out_ref, sem = refs[-2:]
        copies = []
        for number, (kind, flip, half) in enumerate(sources):
            target = piece_target(kind, places_ref[block_count] ^ flip)
            owned, column = 0, 0
            for index in range(block_count):
                matches = places_ref[index] == target
                owned = owned + jnp.where(matches, 1, 0)
                column = column + jnp.where(matches, index * width, 0)
            columns = pl.ds(pl.multiple_of(column, width), width)
            spot = out_ref.at[rows_of(half, width), columns]
            copies.append((owned, pltpu.make_async_copy(refs[number], spot, sem.at[number])))
        for owned, copy in copies:
            pl.when(owned == 1)(copy.start)
        for owned, copy in copies:
            pl.when(owned == 1)(copy.wait)

    in_specs = [pl.BlockSpec(memory_space=pltpu.SMEM)]
    in_specs += [pl.BlockSpec(memory_space=pltpu.VMEM)] * len(slots)
    operands = [places, *slots]
    aliases = {}
    if started is not None:
        aliases = {len(operands): 0}
        in_specs.append(pl.BlockSpec(memory_space=pltpu.HBM))
        operands.append(started)
    return pl.pallas_call(
        kernel,
        in_specs=in_specs,
        out_specs=pl.BlockSpec(memory_space=pltpu.HBM),
        out_shape=jax.ShapeDtypeStruct((width, block_count * width), F32),
        scratch_shapes=[pltpu.SemaphoreType.DMA((len(slots),))],
        input_output_aliases=aliases,
        compiler_params=pltpu.CompilerParams(vmem_limit_bytes=SMALL),
        cost_estimate=pl.CostEstimate(
            flops=0, bytes_accessed=8 * slots[0].size * len(slots), transcendentals=0
        ),
        name="assemble",
    )(*operands)


def paired_body(replica_grads, owners, left_stats, right_stats):
    width = left_stats.shape[1]
    owner_row = owners[0]
    block_count = owner_row.shape[0]
    places = jnp.concatenate([owner_row, lax.axis_index("dp").astype(jnp.int32).reshape(1)])
    group_count = lax.axis_size("mp")
    entry_count = width * block_count * width * group_count
    grads = replica_grads[0]

    def flipped(mask):
        return [(i, i ^ mask) for i in range(8)]

    def over(pairs, value, label):
        with jax.named_scope(label):
            return lax.ppermute(value, "dp", pairs)

    def to_core(value, label):
        return over(flipped(1), value, "core_" + label)

    def to_link(value, label):
        return over([(i, i ^ (2 + 2 * (i % 2))) for i in range(8)], value, "link_" + label)

    def to_side(value, label):
        return over([(i, i ^ (4 - 2 * (i % 2))) for i in range(8)], value, "side_" + label)

    def assemble(result, *pieces):
        return assemble_call(places, *zip(*pieces), block_count, result)

    def after(value, *others):
        return lax.optimization_barrier((value, *others))[0]

    kinds = ("corner", "straight", "side", "self")
    keys = [(kind, half) for kind in kinds for half in HALVES]

    def cut(gate, for_other, for_own, **options):
        pieces = [(kind, 1, half) for kind, half in for_other] + [(kind, 0, half) for kind, half in for_own]
        return pack_call(gate, grads, pieces, width, **options)

    *pieces, own_first, own_second = cut(places, keys[:4], keys[:2])
    pieces += cut(places, keys[4:], [])
    from_core = {key: to_core(value, key[0]) for key, value in zip(keys, pieces)}
    sums = [add_call(own_first, from_core[keys[0]]), add_call(own_second, from_core[keys[1]])]
    *own, owned = cut(after(places, sums[1]), [], keys[2:], with_owned=True)
    own = dict(zip(keys[2:], own))
    sums += [add_call(own[key], from_core[key]) for key in keys[2:4]]
    from_link = {key: to_link(value, key[0]) for key, value in zip(keys[:4], sums)}
    arrived = [
        to_side(add_call(own["side", half], from_core["side", half], from_link["corner", half]), "side")
        for half in HALVES
    ]
    totals = [add_call(own["self", half], from_core["self", half], from_link["straight", half]) for half in HALVES]
    sides = [(left_stats[0],), (right_stats[0],)]
    squares = square_call(*[after(previous, totals[0]) for previous, in sides])
    totals[0] = after(totals[0], *squares)
    norm, block = None, []
    for half in HALVES:
        joined, norm = join_call(totals[half], arrived[half], owned, norm)
        block.append(joined)
    block_norm = norm
    norm = sum_call(norm, to_core(norm, "norm"))
    chip_norms = [over(flipped(mask), norm, "chip_norm") for mask in (6, 4, 2)]
    grams = gram_call([after(block[0], norm), block[1]])
    sides = [(previous, gram, square) for (previous,), gram, square in zip(sides, grams, squares)]
    sides[0] += tuple(mix_call(*sides[0][:2]))
    norm = sum_call(after(norm, sides[0][4]), *chip_norms)
    norms = [norm]
    for shift in reversed(range(1, group_count)):
        both_ways = group_count & (group_count - 1) == 0
        pairs = [(i, i ^ shift if both_ways else (i + shift) % group_count) for i in range(group_count)]
        with jax.named_scope("group_norm"):
            norms.append(lax.ppermute(norm, "mp", pairs))
    sides[1] += tuple(mix_call(*sides[1][:2]))
    whole, *own = update_call(block, block_norm, *sides, norms, entry_count)

    core_own = to_core(whole, "own")
    first = [to_link(value, "own") for value in own]
    core_first = [to_core(after(value, core_own), "first") for value in first]
    second = to_link(after(core_own, first[0]), "sibling")
    core_second = to_core(second, "second")
    relayed = [to_link(value, "relayed") for value in core_first]
    held = [(("self", 0, None), whole), (("self", 1, None), core_own)]
    held += [(("straight", 0, half), first[half]) for half in HALVES]
    held += [(("straight", 1, half), core_first[half]) for half in HALVES]
    crossed = [(("cross", 0, None), second), (("cross", 1, None), core_second)]
    result = assemble(None, *held, crossed[0])
    core_relayed = [to_core(after(relayed[0], result), "relayed"), to_core(relayed[1], "relayed")]
    result = assemble(result, crossed[1], *[(("diagonal", 0, half), relayed[half]) for half in HALVES])
    return assemble(result, *[(("diagonal", 1, half), core_relayed[half]) for half in HALVES])


def solution(mesh):
    return jax.shard_map(
        paired_body if mesh.shape["dp"] == 8 else general_body,
        mesh=mesh,
        in_specs=(P("dp", None, "mp"), P("mp", None), P("dp", None, "mp"), P("dp", None, "mp")),
        out_specs=P(None, "mp"),
        check_vma=False,
    )
```

```python
import functools

import jax
import jax.numpy as jnp
from jax import lax
from jax.experimental import pallas as pl
from jax.experimental.pallas import tpu as pltpu
from jax.sharding import PartitionSpec as P

clip_level = 1.0
graft_eps = 1e-06


def mat_product(left_side, right_side):
    return jnp.matmul(left_side, right_side, precision=lax.Precision.HIGH)


def inverse_root(statistic):
    order_size = statistic.shape[-1]
    identity = jnp.eye(order_size, dtype=jnp.float32)
    frobenius = jnp.sqrt(jnp.sum(statistic * statistic))
    scaled = statistic / frobenius
    square = mat_product(scaled, scaled)
    factor_square = (25.0 * identity - 10.0 * scaled + square) * 0.0625
    factor_scaled = (5.0 * scaled - square) * 0.25
    fourth = mat_product(factor_square, factor_square)
    tail = mat_product(fourth, factor_scaled)
    return (6.25 * identity - 1.25 * scaled - tail) * (0.25 * frobenius ** (-0.25))


def general_body(replica_grads, owners, left_stats, right_stats):
    width = left_stats.shape[1]
    owner_row = owners[0]
    block_count = owner_row.shape[0]
    replica = lax.axis_index("dp")
    replica_count = lax.axis_size("dp")
    entry_count = width * block_count * width * lax.axis_size("mp")
    share_rows = width // replica_count
    share = lax.psum_scatter(
        replica_grads[0].astype(jnp.float32), "dp", scatter_dimension=0, tiled=True
    )
    squares = lax.psum(jnp.sum(share * share), ("dp", "mp"))
    clip_factor = jnp.minimum(1.0, clip_level / jnp.sqrt(squares / entry_count))
    share_blocks = jnp.transpose(share.reshape(share_rows, block_count, width), (1, 0, 2))
    targets = jnp.arange(replica_count, dtype=jnp.int32)
    routing = (owner_row[None, :] == targets[:, None]).astype(jnp.float32)
    outgoing = jnp.einsum("db,brc->drc", routing, share_blocks, precision=lax.Precision.HIGHEST)
    arrived = lax.all_to_all(outgoing, "dp", split_axis=0, concat_axis=0, tiled=True)
    block = arrived.reshape(width, width) * clip_factor
    update = block_update(block, jnp.sum(block * block), 1.0, left_stats[0], right_stats[0])
    chosen = (owner_row == replica).astype(jnp.float32)
    whole = lax.psum(chosen[:, None, None] * update[None], "dp")
    return jnp.transpose(whole, (1, 0, 2)).reshape(width, block_count * width)


def block_update(block, block_norm, clip_factor, left_prev, right_prev):
    order_size = block.shape[-1]
    stat_scale = clip_factor * clip_factor / order_size
    transposed = block.T
    left = 0.5 * left_prev + mat_product(block, transposed) * stat_scale
    right = 0.5 * right_prev + mat_product(transposed, block) * stat_scale
    pre = mat_product(mat_product(inverse_root(left), block), inverse_root(right)) * clip_factor
    pre_norm = jnp.sum(pre * pre)
    return pre * (clip_factor * jnp.sqrt(block_norm / (pre_norm + graft_eps)))


SMALL = 2 << 20
CHUNK = 32
LARGE = 20 << 20
F32 = jnp.float32
HALVES = (0, 1)


def split(value):
    high = value.astype(jnp.bfloat16)
    return high, (value - high.astype(F32)).astype(jnp.bfloat16)


def left_operand(value):
    high, low = split(value)
    return jnp.concatenate([high, high, low], axis=1)


def right_operand(value):
    high, low = split(value)
    return jnp.concatenate([high, low, high], axis=0)


def triple_dot(left_side, right_side):
    return jnp.dot(left_side, right_side, preferred_element_type=F32)


def mirrored(upper, corner):
    half = corner.shape[0]
    lower = jnp.concatenate([upper[:, half:].T, corner], axis=1)
    return jnp.concatenate([upper, lower], axis=0)


def symmetric_dot(left_side, right_side):
    half = left_side.shape[0] // 2
    upper = triple_dot(left_side[:half], right_side)
    return mirrored(upper, triple_dot(left_side[half:], right_side[:, half:]))


def add_identity(value, amount):
    tile = 128
    rows = lax.broadcasted_iota(jnp.int32, (tile, tile), 0)
    columns = lax.broadcasted_iota(jnp.int32, (tile, tile), 1)
    diagonal = jnp.where(rows == columns, amount, 0.0)
    lines = []
    for i in range(value.shape[0] // tile):
        line = value[i * tile : (i + 1) * tile]
        parts = [line[:, j * tile : (j + 1) * tile] for j in range(value.shape[1] // tile)]
        parts[i] = parts[i] + diagonal
        lines.append(jnp.concatenate(parts, axis=1))
    return jnp.concatenate(lines, axis=0)


def piece_target(kind, device):
    along = 2 + 2 * (device & 1)
    flips = {"self": 0, "straight": along, "side": 6 - along, "corner": 6, "cross": along ^ 1, "diagonal": 7}
    return device ^ flips[kind]


def local_call(kernel, name, out_shape, operands, scalars=(), flops=0, vmem=None, **options):
    whole = pl.BlockSpec(memory_space=pltpu.VMEM)
    arrays = list(operands) + (list(out_shape) if isinstance(out_shape, (list, tuple)) else [out_shape])
    moved = sum(array.size * array.dtype.itemsize for array in arrays)
    return pl.pallas_call(
        kernel,
        in_specs=[pl.BlockSpec(memory_space=pltpu.SMEM)] * len(scalars) + [whole] * len(operands),
        out_specs=jax.tree.map(lambda _: whole, out_shape),
        out_shape=out_shape,
        compiler_params=pltpu.CompilerParams(vmem_limit_bytes=vmem or SMALL),
        cost_estimate=pl.CostEstimate(flops=flops, bytes_accessed=moved, transcendentals=0),
        name=name,
        **options,
    )(*scalars, *operands)


def owner_columns(places_ref, grad_ref, width, target):
    column = 0
    for index in range(1, grad_ref.shape[1] // width):
        column = column + jnp.where(places_ref[index] == target, index * width, 0)
    return pl.ds(pl.multiple_of(column, width), width)


def row_chunks(half, width):
    first = 0 if half is None else half * (width // 2)
    count = width if half is None else width // 2
    return [(pl.ds(first + row, CHUNK), pl.ds(row, CHUNK)) for row in range(0, count, CHUNK)]


def rows_of(half, width):
    return pl.ds(0, width) if half is None else pl.ds(half * (width // 2), width // 2)


def piece_shape(half, width):
    return jax.ShapeDtypeStruct((width if half is None else width // 2, width), F32)


def pack_call(places, grads, pieces, width, with_owned=False):
    block_count = grads.shape[1] // width

    def kernel(places_ref, grad_ref, *out_refs):
        me = places_ref[block_count]
        for (kind, flip, half), out_ref in zip(pieces, out_refs):
            columns = owner_columns(places_ref, grad_ref, width, piece_target(kind, me ^ flip))
            for block_rows, piece_rows in row_chunks(half, width):
                out_ref[piece_rows, :] = grad_ref[block_rows, columns].astype(F32)
        if with_owned:
            owned = 0
            for index in range(block_count):
                owned = owned + jnp.where(places_ref[index] == me, 1, 0)
            out_refs[-1][...] = jnp.full((8, 128), owned.astype(F32))

    shapes = [piece_shape(half, width) for _, _, half in pieces]
    if with_owned:
        shapes.append(jax.ShapeDtypeStruct((8, 128), F32))
    return local_call(kernel, "pack", shapes, (grads,), (places,))


def add_kernel(*refs):
    for row in range(0, refs[-1].shape[0], CHUNK):
        total = refs[0][row : row + CHUNK, :]
        for ref in refs[1:-1]:
            total = total + ref[row : row + CHUNK, :]
        refs[-1][row : row + CHUNK, :] = total


def add_call(*pieces):
    return local_call(add_kernel, "add", jax.ShapeDtypeStruct(pieces[0].shape, F32), pieces)


def join_call(total, arrival, owned, norm):
    rows, width = total.shape

    def kernel(total_ref, arrival_ref, owned_ref, *refs):
        block_ref, norm_ref = refs[-2:]
        squares = jnp.zeros((8, width), F32)
        for row in range(0, rows, CHUNK):
            block = total_ref[row : row + CHUNK, :] + arrival_ref[row : row + CHUNK, :]
            block_ref[row : row + CHUNK, :] = block
            squares = squares + jnp.sum((block * block).reshape(CHUNK // 8, 8, width), axis=0)
        squares = jnp.sum(squares, keepdims=True).reshape(1, 1)
        total_squares = squares * owned_ref[...]
        norm_ref[...] = total_squares if norm is None else total_squares + refs[0][...]

    shapes = [jax.ShapeDtypeStruct((rows, width), F32), jax.ShapeDtypeStruct((8, 128), F32)]
    operands = (total, arrival, owned) if norm is None else (total, arrival, owned, norm)
    return local_call(kernel, "join", shapes, operands)


def sum_kernel(*refs):
    total = refs[0][...]
    for ref in refs[1:-1]:
        total = total + ref[...]
    refs[-1][...] = total


def sum_call(*tiles):
    return local_call(sum_kernel, "sum", jax.ShapeDtypeStruct(tiles[0].shape, F32), tiles)


def whole_block(block_refs):
    return jnp.concatenate([ref[...] for ref in block_refs], axis=0)


def gram_kernel(upper_ref, lower_ref, left_ref, right_ref):
    high, low = split(whole_block((upper_ref, lower_ref)))
    for axis, out_ref in ((1, left_ref), (0, right_ref)):
        first = jnp.concatenate([high, high, low], axis=axis)
        second = jnp.concatenate([high, low, high], axis=axis)
        half = high.shape[0] // 2
        dims = (((axis,), (axis,)), ((), ()))
        first_upper = first[:half] if axis == 1 else first[:, :half]
        first_lower = first[half:] if axis == 1 else first[:, half:]
        second_lower = second[half:] if axis == 1 else second[:, half:]
        upper = lax.dot_general(first_upper, second, dims, preferred_element_type=F32)
        corner = lax.dot_general(first_lower, second_lower, dims, preferred_element_type=F32)
        out_ref[...] = mirrored(upper, corner)


def gram_call(block):
    width = block[0].shape[1]
    shape = jax.ShapeDtypeStruct((width, width), F32)
    return local_call(gram_kernel, "gram", [shape, shape], block, flops=12 * width**3, vmem=LARGE)


def square_kernel(*refs):
    for ref, out_ref in zip(refs[: len(refs) // 2], refs[len(refs) // 2 :]):
        value = ref[...]
        out_ref[...] = symmetric_dot(left_operand(value), right_operand(value))


def square_call(*statistics):
    shapes = [jax.ShapeDtypeStruct(value.shape, F32) for value in statistics]
    flops = 6 * len(statistics) * statistics[0].shape[0] ** 3
    return local_call(square_kernel, "square", shapes, statistics, flops=flops, vmem=LARGE)


def mix_kernel(previous_ref, gram_ref, mixed_ref, square_ref):
    gram = gram_ref[...]
    gram_right = right_operand(gram)
    product = triple_dot(left_operand(previous_ref[...]), gram_right)
    square_ref[...] = symmetric_dot(left_operand(gram), gram_right)
    mixed_ref[...] = product + product.T


def mix_call(previous, gram):
    shape = jax.ShapeDtypeStruct(gram.shape, F32)
    flops = 12 * gram.shape[0] ** 3
    return local_call(mix_kernel, "mix", [shape, shape], (previous, gram), flops=flops, vmem=LARGE)


def roots_of(sides, gram_scale):
    statistics = [0.5 * previous[...] + gram[...] * gram_scale for previous, gram, _, _, _ in sides]
    norms = [jnp.sum(value * value, keepdims=True).reshape(1, 1) for value in statistics]
    factor_square, factor_scaled, kept = [], [], []
    for statistic, norm, (_, _, previous_square, mixed, gram_square) in zip(statistics, norms, sides):
        inverse = 1.0 / norm
        scaled = statistic * jnp.sqrt(inverse)
        square = previous_square[...] * (0.25 * inverse) + mixed[...] * (0.5 * gram_scale * inverse)
        square = square + gram_square[...] * (gram_scale * gram_scale * inverse)
        factor_square.append(add_identity(0.0625 * square - 0.625 * scaled, 1.5625))
        factor_scaled.append(1.25 * scaled - 0.25 * square)
        kept.append(scaled)
    fourth = [symmetric_dot(left_operand(value), right_operand(value)) for value in factor_square]
    tail = [symmetric_dot(left_operand(f), right_operand(m)) for f, m in zip(fourth, factor_scaled)]
    roots = [add_identity(-1.25 * m - t, 6.25) for m, t in zip(kept, tail)]
    return roots, [0.25 * lax.rsqrt(jnp.sqrt(jnp.sqrt(norm))) for norm in norms]


def update_call(block, block_norm, left, right, norms, entry_count):
    width = block[0].shape[1]

    def kernel(upper_ref, lower_ref, block_norm_ref, *refs):
        left_refs, right_refs, norm_refs, out_refs = refs[:5], refs[5:10], refs[10:-3], refs[-3:]
        squares = sum(ref[:1, :1] for ref in norm_refs)
        clip_factor = jnp.minimum(1.0, clip_level / jnp.sqrt(squares / entry_count))
        gram_scale = clip_factor * clip_factor / width
        roots, scales = roots_of((left_refs, right_refs), gram_scale)
        halfway = triple_dot(left_operand(roots[0]), right_operand(whole_block((upper_ref, lower_ref))))
        pre = triple_dot(left_operand(halfway), right_operand(roots[1]))
        pre_scale = scales[0] * scales[1] * clip_factor
        pre_norm = jnp.sum(pre * pre, keepdims=True).reshape(1, 1) * (pre_scale * pre_scale)
        clipped_norm = block_norm_ref[:1, :1] * (clip_factor * clip_factor)
        update = pre * (pre_scale * jnp.sqrt(clipped_norm / (pre_norm + graft_eps)))
        out_refs[0][...] = update
        for half in HALVES:
            out_refs[1 + half][...] = update[half * (width // 2) : (half + 1) * (width // 2)]

    operands = (*block, block_norm, *left, *right, *norms)
    shapes = [piece_shape(half, width) for half in (None, *HALVES)]
    return local_call(kernel, "update", shapes, operands, flops=36 * width**3, vmem=LARGE)


def assemble_call(places, sources, slots, block_count, started):
    width = slots[0].shape[1]

    def kernel(places_ref, *refs):
        out_ref, sem = refs[-2:]
        copies = []
        for number, (kind, flip, half) in enumerate(sources):
            target = piece_target(kind, places_ref[block_count] ^ flip)
            owned, column = 0, 0
            for index in range(block_count):
                matches = places_ref[index] == target
                owned = owned + jnp.where(matches, 1, 0)
                column = column + jnp.where(matches, index * width, 0)
            columns = pl.ds(pl.multiple_of(column, width), width)
            spot = out_ref.at[rows_of(half, width), columns]
            copies.append((owned, pltpu.make_async_copy(refs[number], spot, sem.at[number])))
        for owned, copy in copies:
            pl.when(owned == 1)(copy.start)
        for owned, copy in copies:
            pl.when(owned == 1)(copy.wait)

    in_specs = [pl.BlockSpec(memory_space=pltpu.SMEM)]
    in_specs += [pl.BlockSpec(memory_space=pltpu.VMEM)] * len(slots)
    operands = [places, *slots]
    aliases = {}
    if started is not None:
        aliases = {len(operands): 0}
        in_specs.append(pl.BlockSpec(memory_space=pltpu.HBM))
        operands.append(started)
    return pl.pallas_call(
        kernel,
        in_specs=in_specs,
        out_specs=pl.BlockSpec(memory_space=pltpu.HBM),
        out_shape=jax.ShapeDtypeStruct((width, block_count * width), F32),
        scratch_shapes=[pltpu.SemaphoreType.DMA((len(slots),))],
        input_output_aliases=aliases,
        compiler_params=pltpu.CompilerParams(vmem_limit_bytes=SMALL),
        cost_estimate=pl.CostEstimate(
            flops=0, bytes_accessed=8 * slots[0].size * len(slots), transcendentals=0
        ),
        name="assemble",
    )(*operands)


def paired_body(replica_grads, owners, left_stats, right_stats):
    width = left_stats.shape[1]
    owner_row = owners[0]
    block_count = owner_row.shape[0]
    places = jnp.concatenate([owner_row, lax.axis_index("dp").astype(jnp.int32).reshape(1)])
    group_count = lax.axis_size("mp")
    entry_count = width * block_count * width * group_count
    grads = replica_grads[0]

    def flipped(mask):
        return [(i, i ^ mask) for i in range(8)]

    def over(pairs, value, label):
        with jax.named_scope(label):
            return lax.ppermute(value, "dp", pairs)

    def to_core(value, label):
        return over(flipped(1), value, "core_" + label)

    def to_link(value, label):
        return over([(i, i ^ (2 + 2 * (i % 2))) for i in range(8)], value, "link_" + label)

    def to_side(value, label):
        return over([(i, i ^ (4 - 2 * (i % 2))) for i in range(8)], value, "side_" + label)

    def assemble(result, *pieces):
        return assemble_call(places, *zip(*pieces), block_count, result)

    def after(value, *others):
        return lax.optimization_barrier((value, *others))[0]

    kinds = ("corner", "straight", "side", "self")
    keys = [(kind, half) for kind in kinds for half in HALVES]

    def cut(gate, for_other, for_own, **options):
        pieces = [(kind, 1, half) for kind, half in for_other] + [(kind, 0, half) for kind, half in for_own]
        return pack_call(gate, grads, pieces, width, **options)

    *pieces, own_first, own_second = cut(places, keys[:4], keys[:2])
    pieces += cut(places, keys[4:], [])
    from_core = {key: to_core(value, key[0]) for key, value in zip(keys, pieces)}
    sums = [add_call(own_first, from_core[keys[0]]), add_call(own_second, from_core[keys[1]])]
    *own, owned = cut(after(places, sums[1]), [], keys[2:], with_owned=True)
    own = dict(zip(keys[2:], own))
    sums += [add_call(own[key], from_core[key]) for key in keys[2:4]]
    from_link = {key: to_link(value, key[0]) for key, value in zip(keys[:4], sums)}
    arrived = [
        to_side(add_call(own["side", half], from_core["side", half], from_link["corner", half]), "side")
        for half in HALVES
    ]
    totals = [add_call(own["self", half], from_core["self", half], from_link["straight", half]) for half in HALVES]
    sides = [(left_stats[0],), (right_stats[0],)]
    squares = square_call(*[after(previous, totals[0]) for previous, in sides])
    totals[0] = after(totals[0], *squares)
    norm, block = None, []
    for half in HALVES:
        joined, norm = join_call(totals[half], arrived[half], owned, norm)
        block.append(joined)
    block_norm = norm
    norm = sum_call(norm, to_core(norm, "norm"))
    chip_norms = [over(flipped(mask), norm, "chip_norm") for mask in (6, 4, 2)]
    grams = gram_call([after(block[0], norm), block[1]])
    sides = [(previous, gram, square) for (previous,), gram, square in zip(sides, grams, squares)]
    sides[0] += tuple(mix_call(*sides[0][:2]))
    norm = sum_call(after(norm, sides[0][4]), *chip_norms)
    norms = [norm]
    far_first = sorted(range(1, group_count), key=lambda shift: (2 * shift != group_count, -shift))
    for shift in far_first:
        both_ways = group_count & (group_count - 1) == 0
        pairs = [(i, i ^ shift if both_ways else (i + shift) % group_count) for i in range(group_count)]
        with jax.named_scope("group_norm"):
            norms.append(lax.ppermute(norm, "mp", pairs))
    sides[1] += tuple(mix_call(*sides[1][:2]))
    whole, *own = update_call(block, block_norm, *sides, norms, entry_count)

    core_own = to_core(whole, "own")
    first = [to_link(value, "own") for value in own]
    core_first = [to_core(after(value, core_own), "first") for value in first]
    second = to_link(after(core_own, first[0]), "sibling")
    core_second = to_core(second, "second")
    relayed = [to_link(value, "relayed") for value in core_first]
    held = [(("self", 0, None), whole), (("self", 1, None), core_own)]
    held += [(("straight", 0, half), first[half]) for half in HALVES]
    held += [(("straight", 1, half), core_first[half]) for half in HALVES]
    crossed = [(("cross", 0, None), second), (("cross", 1, None), core_second)]
    result = assemble(None, *held, crossed[0])
    core_relayed = [to_core(after(relayed[0], result), "relayed"), to_core(relayed[1], "relayed")]
    result = assemble(
        result, crossed[1], *[(("diagonal", 0, half), relayed[half]) for half in HALVES], (("diagonal", 1, 0), core_relayed[0])
    )
    return assemble(result, (("diagonal", 1, 1), core_relayed[1]))


def solution(mesh):
    return jax.shard_map(
        paired_body if mesh.shape["dp"] == 8 else general_body,
        mesh=mesh,
        in_specs=(P("dp", None, "mp"), P("mp", None), P("dp", None, "mp"), P("dp", None, "mp")),
        out_specs=P(None, "mp"),
        check_vma=False,
    )
```

```python
import functools

import jax
import jax.numpy as jnp
from jax import lax
from jax.experimental import pallas as pl
from jax.experimental.pallas import tpu as pltpu
from jax.sharding import PartitionSpec as P

clip_level = 1.0
graft_eps = 1e-06


def mat_product(left_side, right_side):
    return jnp.matmul(left_side, right_side, precision=lax.Precision.HIGH)


def inverse_root(statistic):
    order_size = statistic.shape[-1]
    identity = jnp.eye(order_size, dtype=jnp.float32)
    frobenius = jnp.sqrt(jnp.sum(statistic * statistic))
    scaled = statistic / frobenius
    square = mat_product(scaled, scaled)
    factor_square = (25.0 * identity - 10.0 * scaled + square) * 0.0625
    factor_scaled = (5.0 * scaled - square) * 0.25
    fourth = mat_product(factor_square, factor_square)
    tail = mat_product(fourth, factor_scaled)
    return (6.25 * identity - 1.25 * scaled - tail) * (0.25 * frobenius ** (-0.25))


def general_body(replica_grads, owners, left_stats, right_stats):
    width = left_stats.shape[1]
    owner_row = owners[0]
    block_count = owner_row.shape[0]
    replica = lax.axis_index("dp")
    replica_count = lax.axis_size("dp")
    entry_count = width * block_count * width * lax.axis_size("mp")
    share_rows = width // replica_count
    share = lax.psum_scatter(
        replica_grads[0].astype(jnp.float32), "dp", scatter_dimension=0, tiled=True
    )
    squares = lax.psum(jnp.sum(share * share), ("dp", "mp"))
    clip_factor = jnp.minimum(1.0, clip_level / jnp.sqrt(squares / entry_count))
    share_blocks = jnp.transpose(share.reshape(share_rows, block_count, width), (1, 0, 2))
    targets = jnp.arange(replica_count, dtype=jnp.int32)
    routing = (owner_row[None, :] == targets[:, None]).astype(jnp.float32)
    outgoing = jnp.einsum("db,brc->drc", routing, share_blocks, precision=lax.Precision.HIGHEST)
    arrived = lax.all_to_all(outgoing, "dp", split_axis=0, concat_axis=0, tiled=True)
    block = arrived.reshape(width, width) * clip_factor
    update = block_update(block, jnp.sum(block * block), 1.0, left_stats[0], right_stats[0])
    chosen = (owner_row == replica).astype(jnp.float32)
    whole = lax.psum(chosen[:, None, None] * update[None], "dp")
    return jnp.transpose(whole, (1, 0, 2)).reshape(width, block_count * width)


def block_update(block, block_norm, clip_factor, left_prev, right_prev):
    order_size = block.shape[-1]
    stat_scale = clip_factor * clip_factor / order_size
    transposed = block.T
    left = 0.5 * left_prev + mat_product(block, transposed) * stat_scale
    right = 0.5 * right_prev + mat_product(transposed, block) * stat_scale
    pre = mat_product(mat_product(inverse_root(left), block), inverse_root(right)) * clip_factor
    pre_norm = jnp.sum(pre * pre)
    return pre * (clip_factor * jnp.sqrt(block_norm / (pre_norm + graft_eps)))


SMALL = 2 << 20
CHUNK = 32
LARGE = 20 << 20
F32 = jnp.float32
HALVES = (0, 1)


def split(value):
    high = value.astype(jnp.bfloat16)
    return high, (value - high.astype(F32)).astype(jnp.bfloat16)


def left_operand(value):
    high, low = split(value)
    return jnp.concatenate([high, high, low], axis=1)


def right_operand(value):
    high, low = split(value)
    return jnp.concatenate([high, low, high], axis=0)


def triple_dot(left_side, right_side):
    return jnp.dot(left_side, right_side, preferred_element_type=F32)


def mirrored(upper, corner):
    half = corner.shape[0]
    lower = jnp.concatenate([upper[:, half:].T, corner], axis=1)
    return jnp.concatenate([upper, lower], axis=0)


def symmetric_dot(left_side, right_side):
    half = left_side.shape[0] // 2
    upper = triple_dot(left_side[:half], right_side)
    return mirrored(upper, triple_dot(left_side[half:], right_side[:, half:]))


def add_identity(value, amount):
    tile = 128
    rows = lax.broadcasted_iota(jnp.int32, (tile, tile), 0)
    columns = lax.broadcasted_iota(jnp.int32, (tile, tile), 1)
    diagonal = jnp.where(rows == columns, amount, 0.0)
    lines = []
    for i in range(value.shape[0] // tile):
        line = value[i * tile : (i + 1) * tile]
        parts = [line[:, j * tile : (j + 1) * tile] for j in range(value.shape[1] // tile)]
        parts[i] = parts[i] + diagonal
        lines.append(jnp.concatenate(parts, axis=1))
    return jnp.concatenate(lines, axis=0)


def piece_target(kind, device):
    along = 2 + 2 * (device & 1)
    flips = {"self": 0, "straight": along, "side": 6 - along, "corner": 6, "cross": along ^ 1, "diagonal": 7}
    return device ^ flips[kind]


def local_call(kernel, name, out_shape, operands, scalars=(), flops=0, vmem=None, **options):
    whole = pl.BlockSpec(memory_space=pltpu.VMEM)
    arrays = list(operands) + (list(out_shape) if isinstance(out_shape, (list, tuple)) else [out_shape])
    moved = sum(array.size * array.dtype.itemsize for array in arrays)
    return pl.pallas_call(
        kernel,
        in_specs=[pl.BlockSpec(memory_space=pltpu.SMEM)] * len(scalars) + [whole] * len(operands),
        out_specs=jax.tree.map(lambda _: whole, out_shape),
        out_shape=out_shape,
        compiler_params=pltpu.CompilerParams(vmem_limit_bytes=vmem or SMALL),
        cost_estimate=pl.CostEstimate(flops=flops, bytes_accessed=moved, transcendentals=0),
        name=name,
        **options,
    )(*scalars, *operands)


def owner_columns(places_ref, grad_ref, width, target):
    column = 0
    for index in range(1, grad_ref.shape[1] // width):
        column = column + jnp.where(places_ref[index] == target, index * width, 0)
    return pl.ds(pl.multiple_of(column, width), width)


def row_chunks(half, width):
    first = 0 if half is None else half * (width // 2)
    count = width if half is None else width // 2
    return [(pl.ds(first + row, CHUNK), pl.ds(row, CHUNK)) for row in range(0, count, CHUNK)]


def rows_of(half, width):
    return pl.ds(0, width) if half is None else pl.ds(half * (width // 2), width // 2)


def piece_shape(half, width):
    return jax.ShapeDtypeStruct((width if half is None else width // 2, width), F32)


def pack_call(places, grads, pieces, width, with_flags=False):
    block_count = grads.shape[1] // width

    def kernel(places_ref, grad_ref, *out_refs):
        me = places_ref[block_count]
        for (kind, flip, half), out_ref in zip(pieces, out_refs):
            columns = owner_columns(places_ref, grad_ref, width, piece_target(kind, me ^ flip))
            for block_rows, piece_rows in row_chunks(half, width):
                out_ref[piece_rows, :] = grad_ref[block_rows, columns].astype(F32)
        if with_flags:
            owned = 0
            for index in range(block_count):
                owned = owned + jnp.where(places_ref[index] == me, 1, 0)
            out_refs[-2][...] = jnp.full((8, 128), owned.astype(F32))
            out_refs[-1][...] = jnp.full((8, 128), (me & 1).astype(F32))

    shapes = [piece_shape(half, width) for _, _, half in pieces]
    if with_flags:
        shapes += [jax.ShapeDtypeStruct((8, 128), F32)] * 2
    return local_call(kernel, "pack", shapes, (grads,), (places,))


def add_kernel(*refs):
    for row in range(0, refs[-1].shape[0], CHUNK):
        total = refs[0][row : row + CHUNK, :]
        for ref in refs[1:-1]:
            total = total + ref[row : row + CHUNK, :]
        refs[-1][row : row + CHUNK, :] = total


def add_call(*pieces):
    return local_call(add_kernel, "add", jax.ShapeDtypeStruct(pieces[0].shape, F32), pieces)


def join_call(total, arrival, owned, norm):
    rows, width = total.shape

    def kernel(total_ref, arrival_ref, owned_ref, *refs):
        block_ref, norm_ref = refs[-2:]
        squares = jnp.zeros((8, width), F32)
        for row in range(0, rows, CHUNK):
            block = total_ref[row : row + CHUNK, :] + arrival_ref[row : row + CHUNK, :]
            block_ref[row : row + CHUNK, :] = block
            squares = squares + jnp.sum((block * block).reshape(CHUNK // 8, 8, width), axis=0)
        squares = jnp.sum(squares, keepdims=True).reshape(1, 1)
        total_squares = squares * owned_ref[...]
        norm_ref[...] = total_squares if norm is None else total_squares + refs[0][...]

    shapes = [jax.ShapeDtypeStruct((rows, width), F32), jax.ShapeDtypeStruct((8, 128), F32)]
    operands = (total, arrival, owned) if norm is None else (total, arrival, owned, norm)
    return local_call(kernel, "join", shapes, operands)


def sum_kernel(*refs):
    total = refs[0][...]
    for ref in refs[1:-1]:
        total = total + ref[...]
    refs[-1][...] = total


def sum_call(*tiles):
    return local_call(sum_kernel, "sum", jax.ShapeDtypeStruct(tiles[0].shape, F32), tiles)


def whole_block(block_refs):
    return jnp.concatenate([ref[...] for ref in block_refs], axis=0)


def gram_kernel(upper_ref, lower_ref, left_ref, right_ref):
    high, low = split(whole_block((upper_ref, lower_ref)))
    for axis, out_ref in ((1, left_ref), (0, right_ref)):
        first = jnp.concatenate([high, high, low], axis=axis)
        second = jnp.concatenate([high, low, high], axis=axis)
        half = high.shape[0] // 2
        dims = (((axis,), (axis,)), ((), ()))
        first_upper = first[:half] if axis == 1 else first[:, :half]
        first_lower = first[half:] if axis == 1 else first[:, half:]
        second_lower = second[half:] if axis == 1 else second[:, half:]
        upper = lax.dot_general(first_upper, second, dims, preferred_element_type=F32)
        corner = lax.dot_general(first_lower, second_lower, dims, preferred_element_type=F32)
        out_ref[...] = mirrored(upper, corner)


def gram_call(block):
    width = block[0].shape[1]
    shape = jax.ShapeDtypeStruct((width, width), F32)
    return local_call(gram_kernel, "gram", [shape, shape], block, flops=12 * width**3, vmem=LARGE)


def square_kernel(*refs):
    for ref, out_ref in zip(refs[: len(refs) // 2], refs[len(refs) // 2 :]):
        value = ref[...]
        out_ref[...] = symmetric_dot(left_operand(value), right_operand(value))


def square_call(*statistics):
    shapes = [jax.ShapeDtypeStruct(value.shape, F32) for value in statistics]
    flops = 6 * len(statistics) * statistics[0].shape[0] ** 3
    return local_call(square_kernel, "square", shapes, statistics, flops=flops, vmem=LARGE)


def mix_kernel(previous_ref, gram_ref, mixed_ref, square_ref):
    gram = gram_ref[...]
    gram_right = right_operand(gram)
    product = triple_dot(left_operand(previous_ref[...]), gram_right)
    square_ref[...] = symmetric_dot(left_operand(gram), gram_right)
    mixed_ref[...] = product + product.T


def mix_call(previous, gram):
    shape = jax.ShapeDtypeStruct(gram.shape, F32)
    flops = 12 * gram.shape[0] ** 3
    return local_call(mix_kernel, "mix", [shape, shape], (previous, gram), flops=flops, vmem=LARGE)


def roots_of(sides, gram_scale):
    statistics = [0.5 * previous[...] + gram[...] * gram_scale for previous, gram, _, _, _ in sides]
    norms = [jnp.sum(value * value, keepdims=True).reshape(1, 1) for value in statistics]
    factor_square, factor_scaled, kept = [], [], []
    for statistic, norm, (_, _, previous_square, mixed, gram_square) in zip(statistics, norms, sides):
        inverse = 1.0 / norm
        scaled = statistic * jnp.sqrt(inverse)
        square = previous_square[...] * (0.25 * inverse) + mixed[...] * (0.5 * gram_scale * inverse)
        square = square + gram_square[...] * (gram_scale * gram_scale * inverse)
        factor_square.append(add_identity(0.0625 * square - 0.625 * scaled, 1.5625))
        factor_scaled.append(1.25 * scaled - 0.25 * square)
        kept.append(scaled)
    fourth = [symmetric_dot(left_operand(value), right_operand(value)) for value in factor_square]
    tail = [symmetric_dot(left_operand(f), right_operand(m)) for f, m in zip(fourth, factor_scaled)]
    roots = [add_identity(-1.25 * m - t, 6.25) for m, t in zip(kept, tail)]
    return roots, [0.25 * lax.rsqrt(jnp.sqrt(jnp.sqrt(norm))) for norm in norms]


def update_call(block, block_norm, left, right, norms, entry_count):
    width = block[0].shape[1]

    def kernel(upper_ref, lower_ref, block_norm_ref, *refs):
        left_refs, right_refs, norm_refs, out_refs = refs[:5], refs[5:10], refs[10:-3], refs[-3:]
        group_ref, handed_ref, second_core_ref = norm_refs
        squares = group_ref[:1, :1] * second_core_ref[:1, :1] + handed_ref[:1, :1]
        clip_factor = jnp.minimum(1.0, clip_level / jnp.sqrt(squares / entry_count))
        gram_scale = clip_factor * clip_factor / width
        roots, scales = roots_of((left_refs, right_refs), gram_scale)
        halfway = triple_dot(left_operand(roots[0]), right_operand(whole_block((upper_ref, lower_ref))))
        pre = triple_dot(left_operand(halfway), right_operand(roots[1]))
        pre_scale = scales[0] * scales[1] * clip_factor
        pre_norm = jnp.sum(pre * pre, keepdims=True).reshape(1, 1) * (pre_scale * pre_scale)
        clipped_norm = block_norm_ref[:1, :1] * (clip_factor * clip_factor)
        update = pre * (pre_scale * jnp.sqrt(clipped_norm / (pre_norm + graft_eps)))
        out_refs[0][...] = update
        for half in HALVES:
            out_refs[1 + half][...] = update[half * (width // 2) : (half + 1) * (width // 2)]

    operands = (*block, block_norm, *left, *right, *norms)
    shapes = [piece_shape(half, width) for half in (None, *HALVES)]
    return local_call(kernel, "update", shapes, operands, flops=36 * width**3, vmem=LARGE)


def assemble_call(places, sources, slots, block_count, started):
    width = slots[0].shape[1]

    def kernel(places_ref, *refs):
        out_ref, sem = refs[-2:]
        copies = []
        for number, (kind, flip, half) in enumerate(sources):
            target = piece_target(kind, places_ref[block_count] ^ flip)
            owned, column = 0, 0
            for index in range(block_count):
                matches = places_ref[index] == target
                owned = owned + jnp.where(matches, 1, 0)
                column = column + jnp.where(matches, index * width, 0)
            columns = pl.ds(pl.multiple_of(column, width), width)
            spot = out_ref.at[rows_of(half, width), columns]
            copies.append((owned, pltpu.make_async_copy(refs[number], spot, sem.at[number])))
        for owned, copy in copies:
            pl.when(owned == 1)(copy.start)
        for owned, copy in copies:
            pl.when(owned == 1)(copy.wait)

    in_specs = [pl.BlockSpec(memory_space=pltpu.SMEM)]
    in_specs += [pl.BlockSpec(memory_space=pltpu.VMEM)] * len(slots)
    operands = [places, *slots]
    aliases = {}
    if started is not None:
        aliases = {len(operands): 0}
        in_specs.append(pl.BlockSpec(memory_space=pltpu.HBM))
        operands.append(started)
    return pl.pallas_call(
        kernel,
        in_specs=in_specs,
        out_specs=pl.BlockSpec(memory_space=pltpu.HBM),
        out_shape=jax.ShapeDtypeStruct((width, block_count * width), F32),
        scratch_shapes=[pltpu.SemaphoreType.DMA((len(slots),))],
        input_output_aliases=aliases,
        compiler_params=pltpu.CompilerParams(vmem_limit_bytes=SMALL),
        cost_estimate=pl.CostEstimate(
            flops=0, bytes_accessed=8 * slots[0].size * len(slots), transcendentals=0
        ),
        name="assemble",
    )(*operands)


def paired_body(replica_grads, owners, left_stats, right_stats):
    width = left_stats.shape[1]
    owner_row = owners[0]
    block_count = owner_row.shape[0]
    places = jnp.concatenate([owner_row, lax.axis_index("dp").astype(jnp.int32).reshape(1)])
    group_count = lax.axis_size("mp")
    entry_count = width * block_count * width * group_count
    grads = replica_grads[0]

    def flipped(mask):
        return [(i, i ^ mask) for i in range(8)]

    def over(pairs, value, label):
        with jax.named_scope(label):
            return lax.ppermute(value, "dp", pairs)

    def to_core(value, label):
        return over(flipped(1), value, "core_" + label)

    def to_link(value, label):
        return over([(i, i ^ (2 + 2 * (i % 2))) for i in range(8)], value, "link_" + label)

    def to_side(value, label):
        return over([(i, i ^ (4 - 2 * (i % 2))) for i in range(8)], value, "side_" + label)

    def assemble(result, *pieces):
        return assemble_call(places, *zip(*pieces), block_count, result)

    def after(value, *others):
        return lax.optimization_barrier((value, *others))[0]

    kinds = ("corner", "straight", "side", "self")
    keys = [(kind, half) for kind in kinds for half in HALVES]

    def cut(gate, for_other, for_own, **options):
        pieces = [(kind, 1, half) for kind, half in for_other] + [(kind, 0, half) for kind, half in for_own]
        return pack_call(gate, grads, pieces, width, **options)

    *pieces, own_first, own_second = cut(places, keys[:4], keys[:2])
    pieces += cut(places, keys[4:], [])
    from_core = {key: to_core(value, key[0]) for key, value in zip(keys, pieces)}
    sums = [add_call(own_first, from_core[keys[0]]), add_call(own_second, from_core[keys[1]])]
    *own, owned, second_core = cut(after(places, sums[1]), [], keys[2:], with_flags=True)
    own = dict(zip(keys[2:], own))
    sums += [add_call(own[key], from_core[key]) for key in keys[2:4]]
    from_link = {key: to_link(value, key[0]) for key, value in zip(keys[:4], sums)}
    arrived = [
        to_side(add_call(own["side", half], from_core["side", half], from_link["corner", half]), "side")
        for half in HALVES
    ]
    totals = [add_call(own["self", half], from_core["self", half], from_link["straight", half]) for half in HALVES]
    sides = [(left_stats[0],), (right_stats[0],)]
    squares = square_call(*[after(previous, totals[0]) for previous, in sides])
    totals[0] = after(totals[0], *squares)
    norm, block = None, []
    for half in HALVES:
        joined, norm = join_call(totals[half], arrived[half], owned, norm)
        block.append(joined)
    block_norm = norm
    norm = sum_call(norm, to_core(norm, "norm"))
    chip_norms = [over(flipped(mask), norm, "chip_norm") for mask in (6, 4, 2)]
    grams = gram_call([after(block[0], norm), block[1]])
    sides = [(previous, gram, square) for (previous,), gram, square in zip(sides, grams, squares)]
    sides[0] += tuple(mix_call(*sides[0][:2]))
    norm = sum_call(after(norm, sides[0][4]), *chip_norms)
    tiles = [norm]
    both_ways = group_count & (group_count - 1) == 0
    far_first = sorted(range(1, group_count), key=lambda shift: (2 * shift != group_count, -shift))
    for shift in far_first:
        pairs = []
        for device in range(1, 8, 2):
            for group in range(group_count):
                other = group ^ shift if both_ways else (group + shift) % group_count
                pairs.append((device * group_count + group, device * group_count + other))
        with jax.named_scope("group_norm"):
            tiles.append(lax.ppermute(norm, ("dp", "mp"), pairs))
    sides[1] += tuple(mix_call(*sides[1][:2]))
    group_norm = sum_call(after(tiles[0], sides[1][3]), *tiles[1:])
    handed = over([(device, device ^ 1) for device in range(1, 8, 2)], group_norm, "core_norm")
    norms = [group_norm, handed, second_core]
    whole, *own = update_call(block, block_norm, *sides, norms, entry_count)

    core_own = to_core(whole, "own")
    first = [to_link(value, "own") for value in own]
    core_first = [to_core(after(value, core_own), "first") for value in first]
    second = to_link(after(core_own, first[0]), "sibling")
    core_second = to_core(second, "second")
    relayed = [to_link(value, "relayed") for value in core_first]
    held = [(("self", 0, None), whole), (("self", 1, None), core_own)]
    held += [(("straight", 0, half), first[half]) for half in HALVES]
    held += [(("straight", 1, half), core_first[half]) for half in HALVES]
    crossed = [(("cross", 0, None), second), (("cross", 1, None), core_second)]
    result = assemble(None, *held, crossed[0])
    core_relayed = [to_core(after(relayed[0], result), "relayed"), to_core(relayed[1], "relayed")]
    result = assemble(
        result, crossed[1], *[(("diagonal", 0, half), relayed[half]) for half in HALVES], (("diagonal", 1, 0), core_relayed[0])
    )
    return assemble(result, (("diagonal", 1, 1), core_relayed[1]))


def solution(mesh):
    return jax.shard_map(
        paired_body if mesh.shape["dp"] == 8 else general_body,
        mesh=mesh,
        in_specs=(P("dp", None, "mp"), P("mp", None), P("dp", None, "mp"), P("dp", None, "mp")),
        out_specs=P(None, "mp"),
        check_vma=False,
    )
```

```python
import functools

import jax
import jax.numpy as jnp
from jax import lax
from jax.experimental import pallas as pl
from jax.experimental.pallas import tpu as pltpu
from jax.sharding import PartitionSpec as P

clip_level = 1.0
graft_eps = 1e-06


def mat_product(left_side, right_side):
    return jnp.matmul(left_side, right_side, precision=lax.Precision.HIGH)


def inverse_root(statistic):
    order_size = statistic.shape[-1]
    identity = jnp.eye(order_size, dtype=jnp.float32)
    frobenius = jnp.sqrt(jnp.sum(statistic * statistic))
    scaled = statistic / frobenius
    square = mat_product(scaled, scaled)
    factor_square = (25.0 * identity - 10.0 * scaled + square) * 0.0625
    factor_scaled = (5.0 * scaled - square) * 0.25
    fourth = mat_product(factor_square, factor_square)
    tail = mat_product(fourth, factor_scaled)
    return (6.25 * identity - 1.25 * scaled - tail) * (0.25 * frobenius ** (-0.25))


def general_body(replica_grads, owners, left_stats, right_stats):
    width = left_stats.shape[1]
    owner_row = owners[0]
    block_count = owner_row.shape[0]
    replica = lax.axis_index("dp")
    replica_count = lax.axis_size("dp")
    entry_count = width * block_count * width * lax.axis_size("mp")
    share_rows = width // replica_count
    share = lax.psum_scatter(
        replica_grads[0].astype(jnp.float32), "dp", scatter_dimension=0, tiled=True
    )
    squares = lax.psum(jnp.sum(share * share), ("dp", "mp"))
    clip_factor = jnp.minimum(1.0, clip_level / jnp.sqrt(squares / entry_count))
    share_blocks = jnp.transpose(share.reshape(share_rows, block_count, width), (1, 0, 2))
    targets = jnp.arange(replica_count, dtype=jnp.int32)
    routing = (owner_row[None, :] == targets[:, None]).astype(jnp.float32)
    outgoing = jnp.einsum("db,brc->drc", routing, share_blocks, precision=lax.Precision.HIGHEST)
    arrived = lax.all_to_all(outgoing, "dp", split_axis=0, concat_axis=0, tiled=True)
    block = arrived.reshape(width, width) * clip_factor
    update = block_update(block, jnp.sum(block * block), 1.0, left_stats[0], right_stats[0])
    chosen = (owner_row == replica).astype(jnp.float32)
    whole = lax.psum(chosen[:, None, None] * update[None], "dp")
    return jnp.transpose(whole, (1, 0, 2)).reshape(width, block_count * width)


def block_update(block, block_norm, clip_factor, left_prev, right_prev):
    order_size = block.shape[-1]
    stat_scale = clip_factor * clip_factor / order_size
    transposed = block.T
    left = 0.5 * left_prev + mat_product(block, transposed) * stat_scale
    right = 0.5 * right_prev + mat_product(transposed, block) * stat_scale
    pre = mat_product(mat_product(inverse_root(left), block), inverse_root(right)) * clip_factor
    pre_norm = jnp.sum(pre * pre)
    return pre * (clip_factor * jnp.sqrt(block_norm / (pre_norm + graft_eps)))


SMALL = 2 << 20
CHUNK = 32
LARGE = 20 << 20
F32 = jnp.float32
HALVES = (0, 1)


def split(value):
    high = value.astype(jnp.bfloat16)
    return high, (value - high.astype(F32)).astype(jnp.bfloat16)


def left_operand(value):
    high, low = split(value)
    return jnp.concatenate([high, high, low], axis=1)


def right_operand(value):
    high, low = split(value)
    return jnp.concatenate([high, low, high], axis=0)


def triple_dot(left_side, right_side):
    return jnp.dot(left_side, right_side, preferred_element_type=F32)


def mirrored(upper, corner):
    half = corner.shape[0]
    lower = jnp.concatenate([upper[:, half:].T, corner], axis=1)
    return jnp.concatenate([upper, lower], axis=0)


def symmetric_dot(left_side, right_side):
    half = left_side.shape[0] // 2
    upper = triple_dot(left_side[:half], right_side)
    return mirrored(upper, triple_dot(left_side[half:], right_side[:, half:]))


def add_identity(value, amount):
    tile = 128
    rows = lax.broadcasted_iota(jnp.int32, (tile, tile), 0)
    columns = lax.broadcasted_iota(jnp.int32, (tile, tile), 1)
    diagonal = jnp.where(rows == columns, amount, 0.0)
    lines = []
    for i in range(value.shape[0] // tile):
        line = value[i * tile : (i + 1) * tile]
        parts = [line[:, j * tile : (j + 1) * tile] for j in range(value.shape[1] // tile)]
        parts[i] = parts[i] + diagonal
        lines.append(jnp.concatenate(parts, axis=1))
    return jnp.concatenate(lines, axis=0)


def piece_target(kind, device):
    along = 2 + 2 * (device & 1)
    flips = {"self": 0, "straight": along, "side": 6 - along, "corner": 6, "cross": along ^ 1, "diagonal": 7}
    return device ^ flips[kind]


def local_call(kernel, name, out_shape, operands, scalars=(), flops=0, vmem=None, **options):
    whole = pl.BlockSpec(memory_space=pltpu.VMEM)
    arrays = list(operands) + (list(out_shape) if isinstance(out_shape, (list, tuple)) else [out_shape])
    moved = sum(array.size * array.dtype.itemsize for array in arrays)
    return pl.pallas_call(
        kernel,
        in_specs=[pl.BlockSpec(memory_space=pltpu.SMEM)] * len(scalars) + [whole] * len(operands),
        out_specs=jax.tree.map(lambda _: whole, out_shape),
        out_shape=out_shape,
        compiler_params=pltpu.CompilerParams(vmem_limit_bytes=vmem or SMALL),
        cost_estimate=pl.CostEstimate(flops=flops, bytes_accessed=moved, transcendentals=0),
        name=name,
        **options,
    )(*scalars, *operands)


def owner_columns(places_ref, grad_ref, width, target):
    column = 0
    for index in range(1, grad_ref.shape[1] // width):
        column = column + jnp.where(places_ref[index] == target, index * width, 0)
    return pl.ds(pl.multiple_of(column, width), width)


def row_chunks(half, width):
    first = 0 if half is None else half * (width // 2)
    count = width if half is None else width // 2
    return [(pl.ds(first + row, CHUNK), pl.ds(row, CHUNK)) for row in range(0, count, CHUNK)]


def rows_of(half, width):
    return pl.ds(0, width) if half is None else pl.ds(half * (width // 2), width // 2)


def piece_shape(half, width):
    return jax.ShapeDtypeStruct((width if half is None else width // 2, width), F32)


def pack_call(places, grads, pieces, width, with_owned=False):
    block_count = grads.shape[1] // width

    def kernel(places_ref, grad_ref, *out_refs):
        me = places_ref[block_count]
        for (kind, flip, half), out_ref in zip(pieces, out_refs):
            columns = owner_columns(places_ref, grad_ref, width, piece_target(kind, me ^ flip))
            for block_rows, piece_rows in row_chunks(half, width):
                out_ref[piece_rows, :] = grad_ref[block_rows, columns].astype(F32)
        if with_owned:
            owned = 0
            for index in range(block_count):
                owned = owned + jnp.where(places_ref[index] == me, 1, 0)
            out_refs[-1][...] = jnp.full((8, 128), owned.astype(F32))

    shapes = [piece_shape(half, width) for _, _, half in pieces]
    if with_owned:
        shapes.append(jax.ShapeDtypeStruct((8, 128), F32))
    return local_call(kernel, "pack", shapes, (grads,), (places,))


def add_kernel(*refs):
    for row in range(0, refs[-1].shape[0], CHUNK):
        total = refs[0][row : row + CHUNK, :]
        for ref in refs[1:-1]:
            total = total + ref[row : row + CHUNK, :]
        refs[-1][row : row + CHUNK, :] = total


def add_call(*pieces):
    return local_call(add_kernel, "add", jax.ShapeDtypeStruct(pieces[0].shape, F32), pieces)


def join_call(total, arrival, owned, norm):
    rows, width = total.shape

    def kernel(total_ref, arrival_ref, owned_ref, *refs):
        block_ref, norm_ref = refs[-2:]
        squares = jnp.zeros((8, width), F32)
        for row in range(0, rows, CHUNK):
            block = total_ref[row : row + CHUNK, :] + arrival_ref[row : row + CHUNK, :]
            block_ref[row : row + CHUNK, :] = block
            squares = squares + jnp.sum((block * block).reshape(CHUNK // 8, 8, width), axis=0)
        squares = jnp.sum(squares, keepdims=True).reshape(1, 1)
        total_squares = squares * owned_ref[...]
        norm_ref[...] = total_squares if norm is None else total_squares + refs[0][...]

    shapes = [jax.ShapeDtypeStruct((rows, width), F32), jax.ShapeDtypeStruct((8, 128), F32)]
    operands = (total, arrival, owned) if norm is None else (total, arrival, owned, norm)
    return local_call(kernel, "join", shapes, operands)


def sum_kernel(*refs):
    total = refs[0][...]
    for ref in refs[1:-1]:
        total = total + ref[...]
    refs[-1][...] = total


def sum_call(*tiles):
    return local_call(sum_kernel, "sum", jax.ShapeDtypeStruct(tiles[0].shape, F32), tiles)


def whole_block(block_refs):
    return jnp.concatenate([ref[...] for ref in block_refs], axis=0)


def gram_kernel(upper_ref, lower_ref, left_ref, right_ref):
    high, low = split(whole_block((upper_ref, lower_ref)))
    for axis, out_ref in ((1, left_ref), (0, right_ref)):
        first = jnp.concatenate([high, high, low], axis=axis)
        second = jnp.concatenate([high, low, high], axis=axis)
        half = high.shape[0] // 2
        dims = (((axis,), (axis,)), ((), ()))
        first_upper = first[:half] if axis == 1 else first[:, :half]
        first_lower = first[half:] if axis == 1 else first[:, half:]
        second_lower = second[half:] if axis == 1 else second[:, half:]
        upper = lax.dot_general(first_upper, second, dims, preferred_element_type=F32)
        corner = lax.dot_general(first_lower, second_lower, dims, preferred_element_type=F32)
        out_ref[...] = mirrored(upper, corner)


def gram_call(block):
    width = block[0].shape[1]
    shape = jax.ShapeDtypeStruct((width, width), F32)
    return local_call(gram_kernel, "gram", [shape, shape], block, flops=12 * width**3, vmem=LARGE)


def square_kernel(*refs):
    for ref, out_ref in zip(refs[: len(refs) // 2], refs[len(refs) // 2 :]):
        value = ref[...]
        out_ref[...] = symmetric_dot(left_operand(value), right_operand(value))


def square_call(*statistics):
    shapes = [jax.ShapeDtypeStruct(value.shape, F32) for value in statistics]
    flops = 6 * len(statistics) * statistics[0].shape[0] ** 3
    return local_call(square_kernel, "square", shapes, statistics, flops=flops, vmem=LARGE)


def mix_kernel(previous_ref, gram_ref, mixed_ref, square_ref):
    gram = gram_ref[...]
    gram_right = right_operand(gram)
    product = triple_dot(left_operand(previous_ref[...]), gram_right)
    square_ref[...] = symmetric_dot(left_operand(gram), gram_right)
    mixed_ref[...] = product + product.T


def mix_call(previous, gram):
    shape = jax.ShapeDtypeStruct(gram.shape, F32)
    flops = 12 * gram.shape[0] ** 3
    return local_call(mix_kernel, "mix", [shape, shape], (previous, gram), flops=flops, vmem=LARGE)


def roots_of(sides, gram_scale):
    statistics = [0.5 * previous[...] + gram[...] * gram_scale for previous, gram, _, _, _ in sides]
    norms = [jnp.sum(value * value, keepdims=True).reshape(1, 1) for value in statistics]
    factor_square, factor_scaled, kept = [], [], []
    for statistic, norm, (_, _, previous_square, mixed, gram_square) in zip(statistics, norms, sides):
        inverse = 1.0 / norm
        scaled = statistic * jnp.sqrt(inverse)
        square = previous_square[...] * (0.25 * inverse) + mixed[...] * (0.5 * gram_scale * inverse)
        square = square + gram_square[...] * (gram_scale * gram_scale * inverse)
        factor_square.append(add_identity(0.0625 * square - 0.625 * scaled, 1.5625))
        factor_scaled.append(1.25 * scaled - 0.25 * square)
        kept.append(scaled)
    fourth = [symmetric_dot(left_operand(value), right_operand(value)) for value in factor_square]
    tail = [symmetric_dot(left_operand(f), right_operand(m)) for f, m in zip(fourth, factor_scaled)]
    roots = [add_identity(-1.25 * m - t, 6.25) for m, t in zip(kept, tail)]
    return roots, [0.25 * lax.rsqrt(jnp.sqrt(jnp.sqrt(norm))) for norm in norms]


def update_call(block, block_norm, left, right, norms, entry_count):
    width = block[0].shape[1]

    def kernel(upper_ref, lower_ref, block_norm_ref, *refs):
        left_refs, right_refs, norm_refs, out_refs = refs[:5], refs[5:10], refs[10:-3], refs[-3:]
        squares = sum(ref[:1, :1] for ref in norm_refs)
        clip_factor = jnp.minimum(1.0, clip_level / jnp.sqrt(squares / entry_count))
        gram_scale = clip_factor * clip_factor / width
        roots, scales = roots_of((left_refs, right_refs), gram_scale)
        halfway = triple_dot(left_operand(roots[0]), right_operand(whole_block((upper_ref, lower_ref))))
        pre = triple_dot(left_operand(halfway), right_operand(roots[1]))
        pre_scale = scales[0] * scales[1] * clip_factor
        pre_norm = jnp.sum(pre * pre, keepdims=True).reshape(1, 1) * (pre_scale * pre_scale)
        clipped_norm = block_norm_ref[:1, :1] * (clip_factor * clip_factor)
        update = pre * (pre_scale * jnp.sqrt(clipped_norm / (pre_norm + graft_eps)))
        out_refs[0][...] = update
        for half in HALVES:
            out_refs[1 + half][...] = update[half * (width // 2) : (half + 1) * (width // 2)]

    operands = (*block, block_norm, *left, *right, *norms)
    shapes = [piece_shape(half, width) for half in (None, *HALVES)]
    return local_call(kernel, "update", shapes, operands, flops=36 * width**3, vmem=LARGE)


def assemble_call(places, sources, slots, block_count, started):
    width = slots[0].shape[1]

    def kernel(places_ref, *refs):
        out_ref, sem = refs[-2:]
        copies = []
        for number, (kind, flip, half) in enumerate(sources):
            target = piece_target(kind, places_ref[block_count] ^ flip)
            owned, column = 0, 0
            for index in range(block_count):
                matches = places_ref[index] == target
                owned = owned + jnp.where(matches, 1, 0)
                column = column + jnp.where(matches, index * width, 0)
            columns = pl.ds(pl.multiple_of(column, width), width)
            spot = out_ref.at[rows_of(half, width), columns]
            copies.append((owned, pltpu.make_async_copy(refs[number], spot, sem.at[number])))
        for owned, copy in copies:
            pl.when(owned == 1)(copy.start)
        for owned, copy in copies:
            pl.when(owned == 1)(copy.wait)

    in_specs = [pl.BlockSpec(memory_space=pltpu.SMEM)]
    in_specs += [pl.BlockSpec(memory_space=pltpu.VMEM)] * len(slots)
    operands = [places, *slots]
    aliases = {}
    if started is not None:
        aliases = {len(operands): 0}
        in_specs.append(pl.BlockSpec(memory_space=pltpu.HBM))
        operands.append(started)
    return pl.pallas_call(
        kernel,
        in_specs=in_specs,
        out_specs=pl.BlockSpec(memory_space=pltpu.HBM),
        out_shape=jax.ShapeDtypeStruct((width, block_count * width), F32),
        scratch_shapes=[pltpu.SemaphoreType.DMA((len(slots),))],
        input_output_aliases=aliases,
        compiler_params=pltpu.CompilerParams(vmem_limit_bytes=SMALL),
        cost_estimate=pl.CostEstimate(
            flops=0, bytes_accessed=8 * slots[0].size * len(slots), transcendentals=0
        ),
        name="assemble",
    )(*operands)


def paired_body(replica_grads, owners, left_stats, right_stats):
    width = left_stats.shape[1]
    owner_row = owners[0]
    block_count = owner_row.shape[0]
    places = jnp.concatenate([owner_row, lax.axis_index("dp").astype(jnp.int32).reshape(1)])
    group_count = lax.axis_size("mp")
    entry_count = width * block_count * width * group_count
    grads = replica_grads[0]

    def flipped(mask):
        return [(i, i ^ mask) for i in range(8)]

    def over(pairs, value, label):
        with jax.named_scope(label):
            return lax.ppermute(value, "dp", pairs)

    def to_core(value, label):
        return over(flipped(1), value, "core_" + label)

    def to_link(value, label):
        return over([(i, i ^ (2 + 2 * (i % 2))) for i in range(8)], value, "link_" + label)

    def to_side(value, label):
        return over([(i, i ^ (4 - 2 * (i % 2))) for i in range(8)], value, "side_" + label)

    def assemble(result, *pieces):
        return assemble_call(places, *zip(*pieces), block_count, result)

    def after(value, *others):
        return lax.optimization_barrier((value, *others))[0]

    kinds = ("corner", "straight", "side", "self")
    keys = [(kind, half) for kind in kinds for half in HALVES]

    def cut(gate, for_other, for_own, **options):
        pieces = [(kind, 1, half) for kind, half in for_other] + [(kind, 0, half) for kind, half in for_own]
        return pack_call(gate, grads, pieces, width, **options)

    *pieces, own_first, own_second = cut(places, keys[:4], keys[:2])
    pieces += cut(places, keys[4:], [])
    from_core = {key: to_core(value, key[0]) for key, value in zip(keys, pieces)}
    sums = [add_call(own_first, from_core[keys[0]]), add_call(own_second, from_core[keys[1]])]
    *own, owned = cut(after(places, sums[1]), [], keys[2:], with_owned=True)
    own = dict(zip(keys[2:], own))
    sums += [add_call(own[key], from_core[key]) for key in keys[2:4]]
    from_link = {key: to_link(value, key[0]) for key, value in zip(keys[:4], sums)}
    arrived = [
        to_side(add_call(own["side", half], from_core["side", half], from_link["corner", half]), "side")
        for half in HALVES
    ]
    totals = [add_call(own["self", half], from_core["self", half], from_link["straight", half]) for half in HALVES]
    sides = [(left_stats[0],), (right_stats[0],)]
    squares = square_call(*[after(previous, totals[0]) for previous, in sides])
    totals[0] = after(totals[0], *squares)
    norm, block = None, []
    for half in HALVES:
        joined, norm = join_call(totals[half], arrived[half], owned, norm)
        block.append(joined)
    block_norm = norm
    norm = sum_call(norm, to_core(norm, "norm"))
    chip_norms = [over(flipped(mask), norm, "chip_norm") for mask in (6, 4, 2)]
    grams = gram_call([after(block[0], norm), block[1]])
    sides = [(previous, gram, square) for (previous,), gram, square in zip(sides, grams, squares)]
    sides[0] += tuple(mix_call(*sides[0][:2]))
    norm = sum_call(after(norm, sides[0][4]), *chip_norms)
    norms = [norm]
    far_first = sorted(range(1, group_count), key=lambda shift: (2 * shift != group_count, -shift))
    for shift in far_first:
        both_ways = group_count & (group_count - 1) == 0
        pairs = [(i, i ^ shift if both_ways else (i + shift) % group_count) for i in range(group_count)]
        with jax.named_scope("group_norm"):
            norms.append(lax.ppermute(norm, "mp", pairs))
    sides[1] += tuple(mix_call(*sides[1][:2]))
    whole, *own = update_call(block, block_norm, *sides, norms, entry_count)

    first = [to_link(value, "own") for value in own]
    core_own = [to_core(value, "own") for value in own]
    core_first = [to_core(value, "first") for value in first]
    second = [to_link(core_own[0], "sibling"), to_link(core_own[1], "sibling")]
    core_second = [to_core(value, "second") for value in second]
    relayed = [to_link(value, "relayed") for value in core_first]
    held = [(("self", 0, None), whole)]
    held += [(("self", 1, half), core_own[half]) for half in HALVES]
    held += [(("straight", 0, half), first[half]) for half in HALVES]
    held += [(("straight", 1, half), core_first[half]) for half in HALVES]
    held += [(("cross", 0, half), second[half]) for half in HALVES]
    result = assemble(None, *held)
    core_relayed = [to_core(after(relayed[0], result), "relayed"), to_core(relayed[1], "relayed")]
    result = assemble(
        result,
        *[(("cross", 1, half), core_second[half]) for half in HALVES],
        *[(("diagonal", 0, half), relayed[half]) for half in HALVES],
        (("diagonal", 1, 0), core_relayed[0]),
    )
    return assemble(result, (("diagonal", 1, 1), core_relayed[1]))


def solution(mesh):
    return jax.shard_map(
        paired_body if mesh.shape["dp"] == 8 else general_body,
        mesh=mesh,
        in_specs=(P("dp", None, "mp"), P("mp", None), P("dp", None, "mp"), P("dp", None, "mp")),
        out_specs=P(None, "mp"),
        check_vma=False,
    )
```

```python
import functools

import jax
import jax.numpy as jnp
from jax import lax
from jax.experimental import pallas as pl
from jax.experimental.pallas import tpu as pltpu
from jax.sharding import PartitionSpec as P

clip_level = 1.0
graft_eps = 1e-06


def mat_product(left_side, right_side):
    return jnp.matmul(left_side, right_side, precision=lax.Precision.HIGH)


def inverse_root(statistic):
    order_size = statistic.shape[-1]
    identity = jnp.eye(order_size, dtype=jnp.float32)
    frobenius = jnp.sqrt(jnp.sum(statistic * statistic))
    scaled = statistic / frobenius
    square = mat_product(scaled, scaled)
    factor_square = (25.0 * identity - 10.0 * scaled + square) * 0.0625
    factor_scaled = (5.0 * scaled - square) * 0.25
    fourth = mat_product(factor_square, factor_square)
    tail = mat_product(fourth, factor_scaled)
    return (6.25 * identity - 1.25 * scaled - tail) * (0.25 * frobenius ** (-0.25))


def general_body(replica_grads, owners, left_stats, right_stats):
    width = left_stats.shape[1]
    owner_row = owners[0]
    block_count = owner_row.shape[0]
    replica = lax.axis_index("dp")
    replica_count = lax.axis_size("dp")
    entry_count = width * block_count * width * lax.axis_size("mp")
    share_rows = width // replica_count
    share = lax.psum_scatter(
        replica_grads[0].astype(jnp.float32), "dp", scatter_dimension=0, tiled=True
    )
    squares = lax.psum(jnp.sum(share * share), ("dp", "mp"))
    clip_factor = jnp.minimum(1.0, clip_level / jnp.sqrt(squares / entry_count))
    share_blocks = jnp.transpose(share.reshape(share_rows, block_count, width), (1, 0, 2))
    targets = jnp.arange(replica_count, dtype=jnp.int32)
    routing = (owner_row[None, :] == targets[:, None]).astype(jnp.float32)
    outgoing = jnp.einsum("db,brc->drc", routing, share_blocks, precision=lax.Precision.HIGHEST)
    arrived = lax.all_to_all(outgoing, "dp", split_axis=0, concat_axis=0, tiled=True)
    block = arrived.reshape(width, width) * clip_factor
    update = block_update(block, jnp.sum(block * block), 1.0, left_stats[0], right_stats[0])
    chosen = (owner_row == replica).astype(jnp.float32)
    whole = lax.psum(chosen[:, None, None] * update[None], "dp")
    return jnp.transpose(whole, (1, 0, 2)).reshape(width, block_count * width)


def block_update(block, block_norm, clip_factor, left_prev, right_prev):
    order_size = block.shape[-1]
    stat_scale = clip_factor * clip_factor / order_size
    transposed = block.T
    left = 0.5 * left_prev + mat_product(block, transposed) * stat_scale
    right = 0.5 * right_prev + mat_product(transposed, block) * stat_scale
    pre = mat_product(mat_product(inverse_root(left), block), inverse_root(right)) * clip_factor
    pre_norm = jnp.sum(pre * pre)
    return pre * (clip_factor * jnp.sqrt(block_norm / (pre_norm + graft_eps)))


SMALL = 2 << 20
CHUNK = 32
LARGE = 20 << 20
F32 = jnp.float32
HALVES = (0, 1)


def split(value):
    high = value.astype(jnp.bfloat16)
    return high, (value - high.astype(F32)).astype(jnp.bfloat16)


def left_operand(value):
    high, low = split(value)
    return jnp.concatenate([high, high, low], axis=1)


def right_operand(value):
    high, low = split(value)
    return jnp.concatenate([high, low, high], axis=0)


def triple_dot(left_side, right_side):
    return jnp.dot(left_side, right_side, preferred_element_type=F32)


def mirrored(upper, corner):
    half = corner.shape[0]
    lower = jnp.concatenate([upper[:, half:].T, corner], axis=1)
    return jnp.concatenate([upper, lower], axis=0)


def symmetric_dot(left_side, right_side):
    half = left_side.shape[0] // 2
    upper = triple_dot(left_side[:half], right_side)
    return mirrored(upper, triple_dot(left_side[half:], right_side[:, half:]))


def add_identity(value, amount):
    tile = 128
    rows = lax.broadcasted_iota(jnp.int32, (tile, tile), 0)
    columns = lax.broadcasted_iota(jnp.int32, (tile, tile), 1)
    diagonal = jnp.where(rows == columns, amount, 0.0)
    lines = []
    for i in range(value.shape[0] // tile):
        line = value[i * tile : (i + 1) * tile]
        parts = [line[:, j * tile : (j + 1) * tile] for j in range(value.shape[1] // tile)]
        parts[i] = parts[i] + diagonal
        lines.append(jnp.concatenate(parts, axis=1))
    return jnp.concatenate(lines, axis=0)


def piece_target(kind, device):
    along = 2 + 2 * (device & 1)
    flips = {"self": 0, "straight": along, "side": 6 - along, "corner": 6, "cross": along ^ 1, "diagonal": 7}
    return device ^ flips[kind]


def local_call(kernel, name, out_shape, operands, scalars=(), flops=0, vmem=None, **options):
    whole = pl.BlockSpec(memory_space=pltpu.VMEM)
    arrays = list(operands) + (list(out_shape) if isinstance(out_shape, (list, tuple)) else [out_shape])
    moved = sum(array.size * array.dtype.itemsize for array in arrays)
    return pl.pallas_call(
        kernel,
        in_specs=[pl.BlockSpec(memory_space=pltpu.SMEM)] * len(scalars) + [whole] * len(operands),
        out_specs=jax.tree.map(lambda _: whole, out_shape),
        out_shape=out_shape,
        compiler_params=pltpu.CompilerParams(vmem_limit_bytes=vmem or SMALL),
        cost_estimate=pl.CostEstimate(flops=flops, bytes_accessed=moved, transcendentals=0),
        name=name,
        **options,
    )(*scalars, *operands)


def owner_columns(places_ref, grad_ref, width, target):
    column = 0
    for index in range(1, grad_ref.shape[1] // width):
        column = column + jnp.where(places_ref[index] == target, index * width, 0)
    return pl.ds(pl.multiple_of(column, width), width)


def row_chunks(half, width):
    first = 0 if half is None else half * (width // 2)
    count = width if half is None else width // 2
    return [(pl.ds(first + row, CHUNK), pl.ds(row, CHUNK)) for row in range(0, count, CHUNK)]


def rows_of(half, width):
    return pl.ds(0, width) if half is None else pl.ds(half * (width // 2), width // 2)


def piece_shape(half, width):
    return jax.ShapeDtypeStruct((width if half is None else width // 2, width), F32)


def pack_call(places, grads, pieces, width, with_owned=False):
    block_count = grads.shape[1] // width

    def kernel(places_ref, grad_ref, *out_refs):
        me = places_ref[block_count]
        for (kind, flip, half), out_ref in zip(pieces, out_refs):
            columns = owner_columns(places_ref, grad_ref, width, piece_target(kind, me ^ flip))
            for block_rows, piece_rows in row_chunks(half, width):
                out_ref[piece_rows, :] = grad_ref[block_rows, columns].astype(F32)
        if with_owned:
            owned = 0
            for index in range(block_count):
                owned = owned + jnp.where(places_ref[index] == me, 1, 0)
            out_refs[-1][...] = jnp.full((8, 128), owned.astype(F32))

    shapes = [piece_shape(half, width) for _, _, half in pieces]
    if with_owned:
        shapes.append(jax.ShapeDtypeStruct((8, 128), F32))
    return local_call(kernel, "pack", shapes, (grads,), (places,))


def add_kernel(*refs):
    for row in range(0, refs[-1].shape[0], CHUNK):
        total = refs[0][row : row + CHUNK, :]
        for ref in refs[1:-1]:
            total = total + ref[row : row + CHUNK, :]
        refs[-1][row : row + CHUNK, :] = total


def add_call(*pieces):
    return local_call(add_kernel, "add", jax.ShapeDtypeStruct(pieces[0].shape, F32), pieces)


def join_call(total, arrival, owned, norm):
    rows, width = total.shape

    def kernel(total_ref, arrival_ref, owned_ref, *refs):
        block_ref, norm_ref = refs[-2:]
        squares = jnp.zeros((8, width), F32)
        for row in range(0, rows, CHUNK):
            block = total_ref[row : row + CHUNK, :] + arrival_ref[row : row + CHUNK, :]
            block_ref[row : row + CHUNK, :] = block
            squares = squares + jnp.sum((block * block).reshape(CHUNK // 8, 8, width), axis=0)
        squares = jnp.sum(squares, keepdims=True).reshape(1, 1)
        total_squares = squares * owned_ref[...]
        norm_ref[...] = total_squares if norm is None else total_squares + refs[0][...]

    shapes = [jax.ShapeDtypeStruct((rows, width), F32), jax.ShapeDtypeStruct((8, 128), F32)]
    operands = (total, arrival, owned) if norm is None else (total, arrival, owned, norm)
    return local_call(kernel, "join", shapes, operands)


def sum_kernel(*refs):
    total = refs[0][...]
    for ref in refs[1:-1]:
        total = total + ref[...]
    refs[-1][...] = total


def sum_call(*tiles):
    return local_call(sum_kernel, "sum", jax.ShapeDtypeStruct(tiles[0].shape, F32), tiles)


def whole_block(block_refs):
    return jnp.concatenate([ref[...] for ref in block_refs], axis=0)


def gram_kernel(upper_ref, lower_ref, left_ref, right_ref):
    high, low = split(whole_block((upper_ref, lower_ref)))
    for axis, out_ref in ((1, left_ref), (0, right_ref)):
        first = jnp.concatenate([high, high, low], axis=axis)
        second = jnp.concatenate([high, low, high], axis=axis)
        half = high.shape[0] // 2
        dims = (((axis,), (axis,)), ((), ()))
        first_upper = first[:half] if axis == 1 else first[:, :half]
        first_lower = first[half:] if axis == 1 else first[:, half:]
        second_lower = second[half:] if axis == 1 else second[:, half:]
        upper = lax.dot_general(first_upper, second, dims, preferred_element_type=F32)
        corner = lax.dot_general(first_lower, second_lower, dims, preferred_element_type=F32)
        out_ref[...] = mirrored(upper, corner)


def gram_call(block):
    width = block[0].shape[1]
    shape = jax.ShapeDtypeStruct((width, width), F32)
    return local_call(gram_kernel, "gram", [shape, shape], block, flops=12 * width**3, vmem=LARGE)


def square_kernel(*refs):
    for ref, out_ref in zip(refs[: len(refs) // 2], refs[len(refs) // 2 :]):
        value = ref[...]
        out_ref[...] = symmetric_dot(left_operand(value), right_operand(value))


def square_call(*statistics):
    shapes = [jax.ShapeDtypeStruct(value.shape, F32) for value in statistics]
    flops = 6 * len(statistics) * statistics[0].shape[0] ** 3
    return local_call(square_kernel, "square", shapes, statistics, flops=flops, vmem=LARGE)


def mix_kernel(previous_ref, gram_ref, mixed_ref, square_ref):
    gram = gram_ref[...]
    gram_right = right_operand(gram)
    product = triple_dot(left_operand(previous_ref[...]), gram_right)
    square_ref[...] = symmetric_dot(left_operand(gram), gram_right)
    mixed_ref[...] = product + product.T


def mix_call(previous, gram):
    shape = jax.ShapeDtypeStruct(gram.shape, F32)
    flops = 12 * gram.shape[0] ** 3
    return local_call(mix_kernel, "mix", [shape, shape], (previous, gram), flops=flops, vmem=LARGE)


def roots_of(sides, gram_scale):
    statistics = [0.5 * previous[...] + gram[...] * gram_scale for previous, gram, _, _, _ in sides]
    norms = [jnp.sum(value * value, keepdims=True).reshape(1, 1) for value in statistics]
    factor_square, factor_scaled, kept = [], [], []
    for statistic, norm, (_, _, previous_square, mixed, gram_square) in zip(statistics, norms, sides):
        inverse = 1.0 / norm
        scaled = statistic * jnp.sqrt(inverse)
        square = previous_square[...] * (0.25 * inverse) + mixed[...] * (0.5 * gram_scale * inverse)
        square = square + gram_square[...] * (gram_scale * gram_scale * inverse)
        factor_square.append(add_identity(0.0625 * square - 0.625 * scaled, 1.5625))
        factor_scaled.append(1.25 * scaled - 0.25 * square)
        kept.append(scaled)
    fourth = [symmetric_dot(left_operand(value), right_operand(value)) for value in factor_square]
    tail = [symmetric_dot(left_operand(f), right_operand(m)) for f, m in zip(fourth, factor_scaled)]
    roots = [add_identity(-1.25 * m - t, 6.25) for m, t in zip(kept, tail)]
    return roots, [0.25 * lax.rsqrt(jnp.sqrt(jnp.sqrt(norm))) for norm in norms]


def update_call(block, block_norm, left, right, norms, entry_count):
    width = block[0].shape[1]

    def kernel(upper_ref, lower_ref, block_norm_ref, *refs):
        left_refs, right_refs, norm_refs, out_refs = refs[:5], refs[5:10], refs[10:-3], refs[-3:]
        squares = sum(ref[:1, :1] for ref in norm_refs)
        clip_factor = jnp.minimum(1.0, clip_level / jnp.sqrt(squares / entry_count))
        gram_scale = clip_factor * clip_factor / width
        roots, scales = roots_of((left_refs, right_refs), gram_scale)
        rows = width // 2
        block_side = right_operand(whole_block((upper_ref, lower_ref)))
        halfway = [triple_dot(left_operand(roots[0][h * rows : (h + 1) * rows]), block_side) for h in HALVES]
        root_side = right_operand(roots[1])
        pre = [triple_dot(left_operand(value), root_side) for value in halfway]
        pre_scale = scales[0] * scales[1] * clip_factor
        pre_norm = sum(jnp.sum(value * value, keepdims=True).reshape(1, 1) for value in pre)
        pre_norm = pre_norm * (pre_scale * pre_scale)
        clipped_norm = block_norm_ref[:1, :1] * (clip_factor * clip_factor)
        scale = pre_scale * jnp.sqrt(clipped_norm / (pre_norm + graft_eps))
        for half in HALVES:
            update = pre[half] * scale
            out_refs[0][half * rows : (half + 1) * rows, :] = update
            out_refs[1 + half][...] = update

    operands = (*block, block_norm, *left, *right, *norms)
    shapes = [piece_shape(half, width) for half in (None, *HALVES)]
    return local_call(kernel, "update", shapes, operands, flops=36 * width**3, vmem=LARGE)


def assemble_call(places, sources, slots, block_count, started):
    width = slots[0].shape[1]

    def kernel(places_ref, *refs):
        out_ref, sem = refs[-2:]
        copies = []
        for number, (kind, flip, half) in enumerate(sources):
            target = piece_target(kind, places_ref[block_count] ^ flip)
            owned, column = 0, 0
            for index in range(block_count):
                matches = places_ref[index] == target
                owned = owned + jnp.where(matches, 1, 0)
                column = column + jnp.where(matches, index * width, 0)
            columns = pl.ds(pl.multiple_of(column, width), width)
            spot = out_ref.at[rows_of(half, width), columns]
            copies.append((owned, pltpu.make_async_copy(refs[number], spot, sem.at[number])))
        for owned, copy in copies:
            pl.when(owned == 1)(copy.start)
        for owned, copy in copies:
            pl.when(owned == 1)(copy.wait)

    in_specs = [pl.BlockSpec(memory_space=pltpu.SMEM)]
    in_specs += [pl.BlockSpec(memory_space=pltpu.VMEM)] * len(slots)
    operands = [places, *slots]
    aliases = {}
    if started is not None:
        aliases = {len(operands): 0}
        in_specs.append(pl.BlockSpec(memory_space=pltpu.HBM))
        operands.append(started)
    return pl.pallas_call(
        kernel,
        in_specs=in_specs,
        out_specs=pl.BlockSpec(memory_space=pltpu.HBM),
        out_shape=jax.ShapeDtypeStruct((width, block_count * width), F32),
        scratch_shapes=[pltpu.SemaphoreType.DMA((len(slots),))],
        input_output_aliases=aliases,
        compiler_params=pltpu.CompilerParams(vmem_limit_bytes=SMALL),
        cost_estimate=pl.CostEstimate(
            flops=0, bytes_accessed=8 * slots[0].size * len(slots), transcendentals=0
        ),
        name="assemble",
    )(*operands)


def paired_body(replica_grads, owners, left_stats, right_stats):
    width = left_stats.shape[1]
    owner_row = owners[0]
    block_count = owner_row.shape[0]
    places = jnp.concatenate([owner_row, lax.axis_index("dp").astype(jnp.int32).reshape(1)])
    group_count = lax.axis_size("mp")
    entry_count = width * block_count * width * group_count
    grads = replica_grads[0]

    def flipped(mask):
        return [(i, i ^ mask) for i in range(8)]

    def over(pairs, value, label):
        with jax.named_scope(label):
            return lax.ppermute(value, "dp", pairs)

    def to_core(value, label):
        return over(flipped(1), value, "core_" + label)

    def to_link(value, label):
        return over([(i, i ^ (2 + 2 * (i % 2))) for i in range(8)], value, "link_" + label)

    def to_side(value, label):
        return over([(i, i ^ (4 - 2 * (i % 2))) for i in range(8)], value, "side_" + label)

    def assemble(result, *pieces):
        return assemble_call(places, *zip(*pieces), block_count, result)

    def after(value, *others):
        return lax.optimization_barrier((value, *others))[0]

    kinds = ("corner", "straight", "side", "self")
    keys = [(kind, half) for kind in kinds for half in HALVES]

    def cut(gate, for_other, for_own, **options):
        pieces = [(kind, 1, half) for kind, half in for_other] + [(kind, 0, half) for kind, half in for_own]
        return pack_call(gate, grads, pieces, width, **options)

    *pieces, own_first, own_second = cut(places, keys[:4], keys[:2])
    pieces += cut(places, keys[4:], [])
    from_core = {key: to_core(value, key[0]) for key, value in zip(keys, pieces)}
    sums = [add_call(own_first, from_core[keys[0]]), add_call(own_second, from_core[keys[1]])]
    *own, owned = cut(after(places, sums[1]), [], keys[2:], with_owned=True)
    own = dict(zip(keys[2:], own))
    sums += [add_call(own[key], from_core[key]) for key in keys[2:4]]
    from_link = {key: to_link(value, key[0]) for key, value in zip(keys[:4], sums)}
    arrived = [
        to_side(add_call(own["side", half], from_core["side", half], from_link["corner", half]), "side")
        for half in HALVES
    ]
    totals = [add_call(own["self", half], from_core["self", half], from_link["straight", half]) for half in HALVES]
    sides = [(left_stats[0],), (right_stats[0],)]
    squares = square_call(*[after(previous, totals[0]) for previous, in sides])
    totals[0] = after(totals[0], *squares)
    norm, block = None, []
    for half in HALVES:
        joined, norm = join_call(totals[half], arrived[half], owned, norm)
        block.append(joined)
    block_norm = norm
    norm = sum_call(norm, to_core(norm, "norm"))
    chip_norms = [over(flipped(mask), norm, "chip_norm") for mask in (6, 4, 2)]
    grams = gram_call([after(block[0], norm), block[1]])
    sides = [(previous, gram, square) for (previous,), gram, square in zip(sides, grams, squares)]
    sides[0] += tuple(mix_call(*sides[0][:2]))
    norm = sum_call(after(norm, sides[0][4]), *chip_norms)
    norms = [norm]
    far_first = sorted(range(1, group_count), key=lambda shift: (2 * shift != group_count, -shift))
    for shift in far_first:
        both_ways = group_count & (group_count - 1) == 0
        pairs = [(i, i ^ shift if both_ways else (i + shift) % group_count) for i in range(group_count)]
        with jax.named_scope("group_norm"):
            norms.append(lax.ppermute(norm, "mp", pairs))
    sides[1] += tuple(mix_call(*sides[1][:2]))
    whole, *own = update_call(block, block_norm, *sides, norms, entry_count)

    core_own = to_core(whole, "own")
    first = [to_link(value, "own") for value in own]
    core_first = [to_core(after(value, core_own), "first") for value in first]
    second = to_link(after(core_own, first[0]), "sibling")
    core_second = to_core(second, "second")
    relayed = [to_link(value, "relayed") for value in core_first]
    held = [(("self", 0, None), whole), (("self", 1, None), core_own)]
    held += [(("straight", 0, half), first[half]) for half in HALVES]
    held += [(("straight", 1, half), core_first[half]) for half in HALVES]
    crossed = [(("cross", 0, None), second), (("cross", 1, None), core_second)]
    result = assemble(None, *held, crossed[0])
    core_relayed = [to_core(after(relayed[0], result), "relayed"), to_core(relayed[1], "relayed")]
    result = assemble(
        result, crossed[1], *[(("diagonal", 0, half), relayed[half]) for half in HALVES], (("diagonal", 1, 0), core_relayed[0])
    )
    return assemble(result, (("diagonal", 1, 1), core_relayed[1]))


def solution(mesh):
    return jax.shard_map(
        paired_body if mesh.shape["dp"] == 8 else general_body,
        mesh=mesh,
        in_specs=(P("dp", None, "mp"), P("mp", None), P("dp", None, "mp"), P("dp", None, "mp")),
        out_specs=P(None, "mp"),
        check_vma=False,
    )
```

```python
import functools

import jax
import jax.numpy as jnp
from jax import lax
from jax.experimental import pallas as pl
from jax.experimental.pallas import tpu as pltpu
from jax.sharding import PartitionSpec as P

clip_level = 1.0
graft_eps = 1e-06


def mat_product(left_side, right_side):
    return jnp.matmul(left_side, right_side, precision=lax.Precision.HIGH)


def inverse_root(statistic):
    order_size = statistic.shape[-1]
    identity = jnp.eye(order_size, dtype=jnp.float32)
    frobenius = jnp.sqrt(jnp.sum(statistic * statistic))
    scaled = statistic / frobenius
    square = mat_product(scaled, scaled)
    factor_square = (25.0 * identity - 10.0 * scaled + square) * 0.0625
    factor_scaled = (5.0 * scaled - square) * 0.25
    fourth = mat_product(factor_square, factor_square)
    tail = mat_product(fourth, factor_scaled)
    return (6.25 * identity - 1.25 * scaled - tail) * (0.25 * frobenius ** (-0.25))


def general_body(replica_grads, owners, left_stats, right_stats):
    width = left_stats.shape[1]
    owner_row = owners[0]
    block_count = owner_row.shape[0]
    replica = lax.axis_index("dp")
    replica_count = lax.axis_size("dp")
    entry_count = width * block_count * width * lax.axis_size("mp")
    share_rows = width // replica_count
    share = lax.psum_scatter(
        replica_grads[0].astype(jnp.float32), "dp", scatter_dimension=0, tiled=True
    )
    squares = lax.psum(jnp.sum(share * share), ("dp", "mp"))
    clip_factor = jnp.minimum(1.0, clip_level / jnp.sqrt(squares / entry_count))
    share_blocks = jnp.transpose(share.reshape(share_rows, block_count, width), (1, 0, 2))
    targets = jnp.arange(replica_count, dtype=jnp.int32)
    routing = (owner_row[None, :] == targets[:, None]).astype(jnp.float32)
    outgoing = jnp.einsum("db,brc->drc", routing, share_blocks, precision=lax.Precision.HIGHEST)
    arrived = lax.all_to_all(outgoing, "dp", split_axis=0, concat_axis=0, tiled=True)
    block = arrived.reshape(width, width) * clip_factor
    update = block_update(block, jnp.sum(block * block), 1.0, left_stats[0], right_stats[0])
    chosen = (owner_row == replica).astype(jnp.float32)
    whole = lax.psum(chosen[:, None, None] * update[None], "dp")
    return jnp.transpose(whole, (1, 0, 2)).reshape(width, block_count * width)


def block_update(block, block_norm, clip_factor, left_prev, right_prev):
    order_size = block.shape[-1]
    stat_scale = clip_factor * clip_factor / order_size
    transposed = block.T
    left = 0.5 * left_prev + mat_product(block, transposed) * stat_scale
    right = 0.5 * right_prev + mat_product(transposed, block) * stat_scale
    pre = mat_product(mat_product(inverse_root(left), block), inverse_root(right)) * clip_factor
    pre_norm = jnp.sum(pre * pre)
    return pre * (clip_factor * jnp.sqrt(block_norm / (pre_norm + graft_eps)))


SMALL = 2 << 20
CHUNK = 32
LARGE = 20 << 20
F32 = jnp.float32
HALVES = (0, 1)


def split(value):
    high = value.astype(jnp.bfloat16)
    return high, (value - high.astype(F32)).astype(jnp.bfloat16)


def left_operand(value):
    high, low = split(value)
    return jnp.concatenate([high, high, low], axis=1)


def right_operand(value):
    high, low = split(value)
    return jnp.concatenate([high, low, high], axis=0)


def triple_dot(left_side, right_side):
    return jnp.dot(left_side, right_side, preferred_element_type=F32)


def mirrored(upper, corner):
    half = corner.shape[0]
    lower = jnp.concatenate([upper[:, half:].T, corner], axis=1)
    return jnp.concatenate([upper, lower], axis=0)


def symmetric_dot(left_side, right_side):
    half = left_side.shape[0] // 2
    upper = triple_dot(left_side[:half], right_side)
    return mirrored(upper, triple_dot(left_side[half:], right_side[:, half:]))


def add_identity(value, amount):
    tile = 128
    rows = lax.broadcasted_iota(jnp.int32, (tile, tile), 0)
    columns = lax.broadcasted_iota(jnp.int32, (tile, tile), 1)
    diagonal = jnp.where(rows == columns, amount, 0.0)
    lines = []
    for i in range(value.shape[0] // tile):
        line = value[i * tile : (i + 1) * tile]
        parts = [line[:, j * tile : (j + 1) * tile] for j in range(value.shape[1] // tile)]
        parts[i] = parts[i] + diagonal
        lines.append(jnp.concatenate(parts, axis=1))
    return jnp.concatenate(lines, axis=0)


def piece_target(kind, device):
    along = 2 + 2 * (device & 1)
    flips = {"self": 0, "straight": along, "side": 6 - along, "corner": 6, "cross": along ^ 1, "diagonal": 7}
    return device ^ flips[kind]


def local_call(kernel, name, out_shape, operands, scalars=(), flops=0, vmem=None, **options):
    whole = pl.BlockSpec(memory_space=pltpu.VMEM)
    arrays = list(operands) + (list(out_shape) if isinstance(out_shape, (list, tuple)) else [out_shape])
    moved = sum(array.size * array.dtype.itemsize for array in arrays)
    return pl.pallas_call(
        kernel,
        in_specs=[pl.BlockSpec(memory_space=pltpu.SMEM)] * len(scalars) + [whole] * len(operands),
        out_specs=jax.tree.map(lambda _: whole, out_shape),
        out_shape=out_shape,
        compiler_params=pltpu.CompilerParams(vmem_limit_bytes=vmem or SMALL),
        cost_estimate=pl.CostEstimate(flops=flops, bytes_accessed=moved, transcendentals=0),
        name=name,
        **options,
    )(*scalars, *operands)


def owner_columns(places_ref, grad_ref, width, target):
    column = 0
    for index in range(1, grad_ref.shape[1] // width):
        column = column + jnp.where(places_ref[index] == target, index * width, 0)
    return pl.ds(pl.multiple_of(column, width), width)


def row_chunks(half, width):
    first = 0 if half is None else half * (width // 2)
    count = width if half is None else width // 2
    return [(pl.ds(first + row, CHUNK), pl.ds(row, CHUNK)) for row in range(0, count, CHUNK)]


def rows_of(half, width):
    return pl.ds(0, width) if half is None else pl.ds(half * (width // 2), width // 2)


def piece_shape(half, width):
    return jax.ShapeDtypeStruct((width if half is None else width // 2, width), F32)


def pack_call(places, grads, pieces, width, with_owned=False):
    block_count = grads.shape[1] // width

    def kernel(places_ref, grad_ref, *out_refs):
        me = places_ref[block_count]
        for (kind, flip, half), out_ref in zip(pieces, out_refs):
            columns = owner_columns(places_ref, grad_ref, width, piece_target(kind, me ^ flip))
            for block_rows, piece_rows in row_chunks(half, width):
                out_ref[piece_rows, :] = grad_ref[block_rows, columns].astype(F32)
        if with_owned:
            owned = 0
            for index in range(block_count):
                owned = owned + jnp.where(places_ref[index] == me, 1, 0)
            out_refs[-1][...] = jnp.full((8, 128), owned.astype(F32))

    shapes = [piece_shape(half, width) for _, _, half in pieces]
    if with_owned:
        shapes.append(jax.ShapeDtypeStruct((8, 128), F32))
    return local_call(kernel, "pack", shapes, (grads,), (places,))


def add_kernel(*refs):
    for row in range(0, refs[-1].shape[0], CHUNK):
        total = refs[0][row : row + CHUNK, :]
        for ref in refs[1:-1]:
            total = total + ref[row : row + CHUNK, :]
        refs[-1][row : row + CHUNK, :] = total


def add_call(*pieces):
    return local_call(add_kernel, "add", jax.ShapeDtypeStruct(pieces[0].shape, F32), pieces)


def join_call(total, arrival, owned, norm):
    rows, width = total.shape

    def kernel(total_ref, arrival_ref, owned_ref, *refs):
        block_ref, norm_ref = refs[-2:]
        squares = jnp.zeros((8, width), F32)
        for row in range(0, rows, CHUNK):
            block = total_ref[row : row + CHUNK, :] + arrival_ref[row : row + CHUNK, :]
            block_ref[row : row + CHUNK, :] = block
            squares = squares + jnp.sum((block * block).reshape(CHUNK // 8, 8, width), axis=0)
        squares = jnp.sum(squares, keepdims=True).reshape(1, 1)
        total_squares = squares * owned_ref[...]
        norm_ref[...] = total_squares if norm is None else total_squares + refs[0][...]

    shapes = [jax.ShapeDtypeStruct((rows, width), F32), jax.ShapeDtypeStruct((8, 128), F32)]
    operands = (total, arrival, owned) if norm is None else (total, arrival, owned, norm)
    return local_call(kernel, "join", shapes, operands)


def sum_kernel(*refs):
    total = refs[0][...]
    for ref in refs[1:-1]:
        total = total + ref[...]
    refs[-1][...] = total


def sum_call(*tiles):
    return local_call(sum_kernel, "sum", jax.ShapeDtypeStruct(tiles[0].shape, F32), tiles)


def whole_block(block_refs):
    return jnp.concatenate([ref[...] for ref in block_refs], axis=0)


def gram_kernel(upper_ref, lower_ref, left_ref, right_ref):
    high, low = split(whole_block((upper_ref, lower_ref)))
    for axis, out_ref in ((1, left_ref), (0, right_ref)):
        first = jnp.concatenate([high, high, low], axis=axis)
        second = jnp.concatenate([high, low, high], axis=axis)
        half = high.shape[0] // 2
        dims = (((axis,), (axis,)), ((), ()))
        first_upper = first[:half] if axis == 1 else first[:, :half]
        first_lower = first[half:] if axis == 1 else first[:, half:]
        second_lower = second[half:] if axis == 1 else second[:, half:]
        upper = lax.dot_general(first_upper, second, dims, preferred_element_type=F32)
        corner = lax.dot_general(first_lower, second_lower, dims, preferred_element_type=F32)
        out_ref[...] = mirrored(upper, corner)


def gram_call(block):
    width = block[0].shape[1]
    shape = jax.ShapeDtypeStruct((width, width), F32)
    return local_call(gram_kernel, "gram", [shape, shape], block, flops=12 * width**3, vmem=LARGE)


def square_kernel(*refs):
    for ref, out_ref in zip(refs[: len(refs) // 2], refs[len(refs) // 2 :]):
        value = ref[...]
        out_ref[...] = symmetric_dot(left_operand(value), right_operand(value))


def square_call(*statistics):
    shapes = [jax.ShapeDtypeStruct(value.shape, F32) for value in statistics]
    flops = 6 * len(statistics) * statistics[0].shape[0] ** 3
    return local_call(square_kernel, "square", shapes, statistics, flops=flops, vmem=LARGE)


def mix_kernel(previous_ref, gram_ref, mixed_ref, square_ref):
    gram = gram_ref[...]
    gram_right = right_operand(gram)
    product = triple_dot(left_operand(previous_ref[...]), gram_right)
    square_ref[...] = symmetric_dot(left_operand(gram), gram_right)
    mixed_ref[...] = product + product.T


def mix_call(previous, gram):
    shape = jax.ShapeDtypeStruct(gram.shape, F32)
    flops = 12 * gram.shape[0] ** 3
    return local_call(mix_kernel, "mix", [shape, shape], (previous, gram), flops=flops, vmem=LARGE)


def roots_of(sides, gram_scale):
    statistics = [0.5 * previous[...] + gram[...] * gram_scale for previous, gram, _, _, _ in sides]
    norms = [jnp.sum(value * value, keepdims=True).reshape(1, 1) for value in statistics]
    factor_square, factor_scaled, kept = [], [], []
    for statistic, norm, (_, _, previous_square, mixed, gram_square) in zip(statistics, norms, sides):
        inverse = 1.0 / norm
        scaled = statistic * jnp.sqrt(inverse)
        square = previous_square[...] * (0.25 * inverse) + mixed[...] * (0.5 * gram_scale * inverse)
        square = square + gram_square[...] * (gram_scale * gram_scale * inverse)
        factor_square.append(add_identity(0.0625 * square - 0.625 * scaled, 1.5625))
        factor_scaled.append(1.25 * scaled - 0.25 * square)
        kept.append(scaled)
    fourth = [symmetric_dot(left_operand(value), right_operand(value)) for value in factor_square]
    tail = [symmetric_dot(left_operand(f), right_operand(m)) for f, m in zip(fourth, factor_scaled)]
    roots = [add_identity(-1.25 * m - t, 6.25) for m, t in zip(kept, tail)]
    return roots, [0.25 * lax.rsqrt(jnp.sqrt(jnp.sqrt(norm))) for norm in norms]


def update_call(block, block_norm, left, right, norms, entry_count):
    width = block[0].shape[1]

    def kernel(upper_ref, lower_ref, block_norm_ref, *refs):
        left_refs, right_refs, norm_refs, out_refs = refs[:5], refs[5:10], refs[10:-3], refs[-3:]
        squares = sum(ref[:1, :1] for ref in norm_refs)
        clip_factor = jnp.minimum(1.0, clip_level / jnp.sqrt(squares / entry_count))
        gram_scale = clip_factor * clip_factor / width
        roots, scales = roots_of((left_refs, right_refs), gram_scale)
        halfway = triple_dot(left_operand(roots[0]), right_operand(whole_block((upper_ref, lower_ref))))
        pre = triple_dot(left_operand(halfway), right_operand(roots[1]))
        pre_scale = scales[0] * scales[1] * clip_factor
        pre_norm = jnp.sum(pre * pre, keepdims=True).reshape(1, 1) * (pre_scale * pre_scale)
        clipped_norm = block_norm_ref[:1, :1] * (clip_factor * clip_factor)
        update = pre * (pre_scale * jnp.sqrt(clipped_norm / (pre_norm + graft_eps)))
        out_refs[0][...] = update
        for half in HALVES:
            out_refs[1 + half][...] = update[half * (width // 2) : (half + 1) * (width // 2)]

    operands = (*block, block_norm, *left, *right, *norms)
    shapes = [piece_shape(half, width) for half in (None, *HALVES)]
    return local_call(kernel, "update", shapes, operands, flops=36 * width**3, vmem=LARGE)


def assemble_call(places, sources, slots, block_count, started):
    width = slots[0].shape[1]

    def kernel(places_ref, *refs):
        out_ref, sem = refs[-2:]
        copies = []
        for number, (kind, flip, half) in enumerate(sources):
            target = piece_target(kind, places_ref[block_count] ^ flip)
            owned, column = 0, 0
            for index in range(block_count):
                matches = places_ref[index] == target
                owned = owned + jnp.where(matches, 1, 0)
                column = column + jnp.where(matches, index * width, 0)
            columns = pl.ds(pl.multiple_of(column, width), width)
            spot = out_ref.at[rows_of(half, width), columns]
            copies.append((owned, pltpu.make_async_copy(refs[number], spot, sem.at[number])))
        for owned, copy in copies:
            pl.when(owned == 1)(copy.start)
        for owned, copy in copies:
            pl.when(owned == 1)(copy.wait)

    in_specs = [pl.BlockSpec(memory_space=pltpu.SMEM)]
    in_specs += [pl.BlockSpec(memory_space=pltpu.VMEM)] * len(slots)
    operands = [places, *slots]
    aliases = {}
    if started is not None:
        aliases = {len(operands): 0}
        in_specs.append(pl.BlockSpec(memory_space=pltpu.HBM))
        operands.append(started)
    return pl.pallas_call(
        kernel,
        in_specs=in_specs,
        out_specs=pl.BlockSpec(memory_space=pltpu.HBM),
        out_shape=jax.ShapeDtypeStruct((width, block_count * width), F32),
        scratch_shapes=[pltpu.SemaphoreType.DMA((len(slots),))],
        input_output_aliases=aliases,
        compiler_params=pltpu.CompilerParams(vmem_limit_bytes=SMALL),
        cost_estimate=pl.CostEstimate(
            flops=0, bytes_accessed=8 * slots[0].size * len(slots), transcendentals=0
        ),
        name="assemble",
    )(*operands)


def paired_body(replica_grads, owners, left_stats, right_stats):
    width = left_stats.shape[1]
    owner_row = owners[0]
    block_count = owner_row.shape[0]
    places = jnp.concatenate([owner_row, lax.axis_index("dp").astype(jnp.int32).reshape(1)])
    group_count = lax.axis_size("mp")
    entry_count = width * block_count * width * group_count
    grads = replica_grads[0]

    def flipped(mask):
        return [(i, i ^ mask) for i in range(8)]

    def over(pairs, value, label):
        with jax.named_scope(label):
            return lax.ppermute(value, "dp", pairs)

    def to_core(value, label):
        return over(flipped(1), value, "core_" + label)

    def to_link(value, label):
        return over([(i, i ^ (2 + 2 * (i % 2))) for i in range(8)], value, "link_" + label)

    def to_side(value, label):
        return over([(i, i ^ (4 - 2 * (i % 2))) for i in range(8)], value, "side_" + label)

    def assemble(result, *pieces):
        return assemble_call(places, *zip(*pieces), block_count, result)

    def after(value, *others):
        return lax.optimization_barrier((value, *others))[0]

    kinds = ("corner", "straight", "side", "self")
    keys = [(kind, half) for kind in kinds for half in HALVES]

    def cut(gate, for_other, for_own, **options):
        pieces = [(kind, 1, half) for kind, half in for_other] + [(kind, 0, half) for kind, half in for_own]
        return pack_call(gate, grads, pieces, width, **options)

    *pieces, own_first, own_second = cut(places, keys[:4], keys[:2])
    pieces += cut(places, keys[4:], [])
    from_core = {key: to_core(value, key[0]) for key, value in zip(keys, pieces)}
    sums = [add_call(own_first, from_core[keys[0]]), add_call(own_second, from_core[keys[1]])]
    *own, owned = cut(after(places, sums[1]), [], keys[2:], with_owned=True)
    own = dict(zip(keys[2:], own))
    sums += [add_call(own[key], from_core[key]) for key in keys[2:4]]
    from_link = {key: to_link(value, key[0]) for key, value in zip(keys[:4], sums)}
    arrived = [
        to_side(add_call(own["side", half], from_core["side", half], from_link["corner", half]), "side")
        for half in HALVES
    ]
    totals = [add_call(own["self", half], from_core["self", half], from_link["straight", half]) for half in HALVES]
    sides = [(left_stats[0],), (right_stats[0],)]
    squares = square_call(*[after(previous, totals[0]) for previous, in sides])
    totals[0] = after(totals[0], *squares)
    norm, block = None, []
    for half in HALVES:
        joined, norm = join_call(totals[half], arrived[half], owned, norm)
        block.append(joined)
    block_norm = norm
    norm = sum_call(norm, to_core(norm, "norm"))
    chip_norms = [over(flipped(mask), norm, "chip_norm") for mask in (4, 6, 2)]
    grams = gram_call([after(block[0], norm), block[1]])
    sides = [(previous, gram, square) for (previous,), gram, square in zip(sides, grams, squares)]
    sides[0] += tuple(mix_call(*sides[0][:2]))
    norm = sum_call(after(norm, sides[0][4]), *chip_norms)
    norms = [norm]
    far_first = sorted(range(1, group_count), key=lambda shift: (2 * shift != group_count, -shift))
    for shift in far_first:
        both_ways = group_count & (group_count - 1) == 0
        pairs = [(i, i ^ shift if both_ways else (i + shift) % group_count) for i in range(group_count)]
        with jax.named_scope("group_norm"):
            norms.append(lax.ppermute(norm, "mp", pairs))
    sides[1] += tuple(mix_call(*sides[1][:2]))
    whole, *own = update_call(block, block_norm, *sides, norms, entry_count)

    core_own = to_core(whole, "own")
    first = [to_link(value, "own") for value in own]
    core_first = [to_core(after(value, core_own), "first") for value in first]
    second = to_link(after(core_own, first[0]), "sibling")
    core_second = to_core(second, "second")
    relayed = [to_link(value, "relayed") for value in core_first]
    held = [(("self", 0, None), whole), (("self", 1, None), core_own)]
    held += [(("straight", 0, half), first[half]) for half in HALVES]
    held += [(("straight", 1, half), core_first[half]) for half in HALVES]
    crossed = [(("cross", 0, None), second), (("cross", 1, None), core_second)]
    result = assemble(None, *held, crossed[0])
    core_relayed = [to_core(after(relayed[0], result), "relayed"), to_core(relayed[1], "relayed")]
    result = assemble(
        result, crossed[1], *[(("diagonal", 0, half), relayed[half]) for half in HALVES], (("diagonal", 1, 0), core_relayed[0])
    )
    return assemble(result, (("diagonal", 1, 1), core_relayed[1]))


def solution(mesh):
    return jax.shard_map(
        paired_body if mesh.shape["dp"] == 8 else general_body,
        mesh=mesh,
        in_specs=(P("dp", None, "mp"), P("mp", None), P("dp", None, "mp"), P("dp", None, "mp")),
        out_specs=P(None, "mp"),
        check_vma=False,
    )
```
